32 devices in a mesh: groups: 2 (over y), tm: 4 (over z), space: 4 (over x, core).
Axes of the slice: x: 2, y: 2, z: 4, core: 2. Of those that a mesh axis runs over, the one named last changes fastest.
Arguments:
- guess: float32 [8, 320, 2048], P('tm', None, ('groups', 'space')), parts along dimension 2, may hold values from -6 to 6
- source_cos: bfloat16 [320, 2048], P(None, ('groups', 'space')), parts along dimension 1, may hold values from -6 to 6
- source_sin: bfloat16 [320, 2048], P(None, ('groups', 'space')), parts along dimension 1, may hold values from -6 to 6
- damping: float32 [320, 2048], P(None, ('groups', 'space')), parts along dimension 1, may hold values from 0.5 to 4
- volume: bfloat16 [320, 320], replicated, may hold values from -0.3125 to 0.3125
- lifts: bfloat16 [6, 320, 80], replicated, may hold values from -0.25 to 0.25
- neighbor: int32 [6, 2048], P(None, ('groups', 'space')), parts along dimension 1, may hold values from 0 to 1023, as said below
- tags: int32 [6, 2048], P(None, ('groups', 'space')), parts along dimension 1, may hold values from 0 to 3, as said below
- codes: int32 [6, 2048], P(None, ('groups', 'space')), parts along dimension 1, may hold values from 0 to 7
Outputs:
- solution: float32 [8, 320, 2048], P('tm', None, ('groups', 'space')), parts along dimension 2
- after_residual: bfloat16 [8, 320, 2048], P('tm', None, ('groups', 'space')), parts along dimension 2
The draws below stay inside these ranges and needn't reach their ends.
There are 2 independent parts, one for each index of `groups`. The reference program is written for one: setup_inputs(seed, part) draws one part's arguments, and reference() takes and returns one part's arrays. A program takes and returns all parts, laid end to end along the dimension named above; an argument that names none is the same for every part. Nothing has to cross between parts.
Inputs may be any that keep to these rules, and one draw needn't show every extreme that they name: `neighbor`: elements are numbered layer by layer along the trench, 64 to a layer, 16 layers. Where tags is 0, faces 0 and 1 join an element to one of the previous and of the next layer, faces 2 to 5 to one of its own layer; where tags is not 0, the entry is the element itself. `tags`: face 0 of every element of the first layer is 2 and face 1 of every element of the last layer is 3.
All inputs are finite; a program needn't handle non-finite values.
Results may differ from the reference program's by a relative error of at most 0.001.
Values sent between devices are 32-bit elements; how exact they have to be, the bound alone decides.
No kernel may reach another device: no remote copies, remote signals or barrier semaphores. Data moves between devices by JAX's collectives and lax.ppermute only.
A program may use at most 192 MiB of HBM per device.

```python
import math
import jax
import jax.numpy as jnp
from jax import lax

NF = 5
NP = 4
GY = 8
GZ = 8
ROWS = 320
FROWS = 80
XSEC = 64
LAYERS = 16
ELEMS = 1024
TSL = 8


def mesh_tables(key):
    mesh_key = jax.random.fold_in(key, 11)
    layer_keys = jax.random.split(mesh_key, LAYERS)
    slot_of = jax.vmap(lambda item: jax.random.permutation(item, XSEC))(layer_keys).astype(jnp.int32)
    place_of = jnp.argsort(slot_of, axis=1).astype(jnp.int32)
    element = jnp.arange(ELEMS, dtype=jnp.int32)
    layer = element // XSEC
    slot = element % XSEC
    place = place_of[layer, slot]
    across = place // GZ
    upward = place % GZ
    moves = [(-1, 0, 0), (1, 0, 0), (0, -1, 0), (0, 1, 0), (0, 0, -1), (0, 0, 1)]
    outside = [2, 3, 1, 1, 1, 3]
    targets = []
    kinds = []
    for face in range(6):
        move_layer, move_across, move_up = moves[face]
        new_layer = layer + move_layer
        new_across = across + move_across
        new_up = upward + move_up
        inside = (new_layer >= 0) & (new_layer < LAYERS) & (new_across >= 0) & (new_across < GY) & (new_up >= 0) & (new_up < GZ)
        safe_layer = jnp.clip(new_layer, 0, LAYERS - 1)
        safe_across = jnp.clip(new_across, 0, GY - 1)
        safe_up = jnp.clip(new_up, 0, GZ - 1)
        other = safe_layer * XSEC + slot_of[safe_layer, safe_across * GZ + safe_up]
        targets.append(jnp.where(inside, other, element).astype(jnp.int32))
        kinds.append(jnp.where(inside, 0, outside[face]).astype(jnp.int32))
    return (jnp.stack(targets, axis=0), jnp.stack(kinds, axis=0))


def draw_neighbor(key, part):
    return mesh_tables(key)[0]


def draw_tags(key, part):
    return mesh_tables(key)[1]


def place_ends(array, stream_key, low, top_value):
    longest = array.shape.index(max(array.shape))
    spots = []
    for shift in (0, 1):
        where = [jax.random.randint(jax.random.fold_in(stream_key, axis), (), 0, length) for axis, length in enumerate(array.shape)]
        where[longest] = (where[longest] + shift) % array.shape[longest]
        spots.append(tuple(where))
    return array.at[spots[0]].set(low).at[spots[1]].set(top_value)


def steps_of(stream_key, shape, cuts, least, high):
    def one(dim, parts):
        steps = jax.random.uniform(jax.random.fold_in(jax.random.fold_in(stream_key, 6), dim), (parts,), jnp.float32, least / len(cuts), high / len(cuts))
        return jnp.repeat(jnp.exp(steps), shape[dim] // parts).reshape((-1,) + (1,) * (len(shape) - dim - 1))

    gain = one(*cuts[0])
    for cut in cuts[1:]:
        gain = gain * one(*cut)
    return gain


def noise(rng, dims, width, bound, cuts=(), kind=jnp.bfloat16):
    array = width * jax.random.normal(rng, dims, jnp.float32)
    if cuts:
        array = array * steps_of(rng, dims, cuts, -0.22, 0.18)
    return jnp.clip(array, -bound, bound).astype(kind)


def setup_inputs(seed: int = 0, part: int = 0) -> dict:
    arg_keys = jax.random.split(jax.random.key(seed), 10)
    own_keys = jax.random.split(jax.random.fold_in(arg_keys[9], part), 10)
    guess = noise(own_keys[0], (TSL, ROWS, ELEMS), 1.0, 6.0, ((0, 4), (2, 4)), jnp.float32)
    source_cos = noise(own_keys[1], (ROWS, ELEMS), 1.0, 6.0, ((1, 4),))
    source_sin = noise(own_keys[2], (ROWS, ELEMS), 1.0, 6.0, ((1, 4),))
    damping = jnp.clip(jnp.exp(math.log(4.0) - 2.0794415 * jax.random.uniform(own_keys[3], (ROWS, ELEMS), jnp.float32) ** steps_of(own_keys[3], (ROWS, ELEMS), ((1, 4),), -0.2, 0.2)), 0.5, 4.0)
    volume = noise(arg_keys[4], (ROWS, ROWS), ROWS ** -0.5, 0.3125)
    lifts = noise(arg_keys[5], (6, ROWS, FROWS), (6 * FROWS) ** -0.5, 0.25)
    neighbor = draw_neighbor(jax.random.fold_in(jax.random.fold_in(arg_keys[9], part), 71), part)
    tags = draw_tags(jax.random.fold_in(jax.random.fold_in(arg_keys[9], part), 71), part)
    codes = place_ends(jax.random.randint(own_keys[8], (6, ELEMS), 0, 8), jax.random.fold_in(own_keys[8], 1), 0, 7).astype(jnp.int32)
    return {"guess": guess, "source_cos": source_cos, "source_sin": source_sin, "damping": damping, "volume": volume, "lifts": lifts, "neighbor": neighbor, "tags": tags, "codes": codes}


HIGHEST = lax.Precision.HIGHEST


def face_traces(field_state):
    slices = field_state.shape[0]
    columns = field_state.shape[2]
    cube_view = field_state.reshape(slices, NF, NP, NP, NP, columns)
    edge = NP - 1
    return jnp.stack([cube_view[:, :, 0], cube_view[:, :, edge], cube_view[:, :, :, 0], cube_view[:, :, :, edge], cube_view[:, :, :, :, 0], cube_view[:, :, :, :, edge]], axis=0)


def orient(trace_block, codes_row):
    turned = jnp.swapaxes(trace_block, 2, 3)
    trace_block = jnp.where(codes_row % 2 == 1, turned, trace_block)
    trace_block = jnp.where((codes_row // 2) % 2 == 1, jnp.flip(trace_block, 2), trace_block)
    trace_block = jnp.where((codes_row // 4) % 2 == 1, jnp.flip(trace_block, 3), trace_block)
    return trace_block


def seen_traces(own_traces, lookup, targets, tags, codes):
    pieces = []
    for face in range(6):
        across = jnp.take(lookup[face ^ 1], targets[face], axis=-1)
        across = orient(across, codes[face])
        mine = own_traces[face]
        normal_sign = jnp.where(jnp.arange(NF) == 1 + face // 2, -1.0, 1.0).astype(jnp.float32)
        wall = mine * normal_sign[None, :, None, None, None]
        kind = tags[face]
        chosen = jnp.where(kind == 0, across, jnp.where(kind == 1, wall, jnp.where(kind == 2, jnp.zeros_like(mine), mine)))
        pieces.append(chosen)
    return jnp.stack(pieces, axis=0)


def apply_operator(field_state, own_traces, lookup, targets, tags, codes, volume, lifts):
    slices = field_state.shape[0]
    columns = field_state.shape[2]
    seen = seen_traces(own_traces, lookup, targets, tags, codes).reshape(6, slices, NF * NP * NP, columns)
    inner = jnp.einsum("mk,ske->sme", volume.astype(jnp.float32), field_state, precision=HIGHEST)
    return inner + jnp.einsum("fmk,fske->sme", lifts.astype(jnp.float32), seen, precision=HIGHEST)


def frequency_solve(residual_block, damping_block):
    total_slices = residual_block.shape[0]
    flat = residual_block.reshape(total_slices, -1)
    index = jnp.arange(total_slices, dtype=jnp.int32)
    angle = 2.0 * math.pi * ((index[:, None] * index[None, :]) % total_slices).astype(jnp.float32) / total_slices
    cos_table = jnp.cos(angle)
    sin_table = jnp.sin(angle)
    real_part = jnp.dot(cos_table, flat, precision=HIGHEST).reshape(residual_block.shape)
    imag_part = (-jnp.dot(sin_table, flat, precision=HIGHEST)).reshape(residual_block.shape)
    phase = 2.0 * math.pi * index.astype(jnp.float32) / total_slices
    shape_out = (total_slices,) + (1,) * (residual_block.ndim - 1)
    near = (1.0 - jnp.cos(phase)).reshape(shape_out) + damping_block[None]
    far = jnp.sin(phase).reshape(shape_out)
    modulus = near * near + far * far
    fix_real = (real_part * near + imag_part * far) / modulus
    fix_imag = (imag_part * near - real_part * far) / modulus
    back = jnp.dot(cos_table, fix_real.reshape(total_slices, -1), precision=HIGHEST) - jnp.dot(sin_table, fix_imag.reshape(total_slices, -1), precision=HIGHEST)
    return (back / total_slices).reshape(residual_block.shape)


def reference(guess, source_cos, source_sin, damping, volume, lifts, neighbor, tags, codes):
    total_slices = guess.shape[0]
    columns = guess.shape[2]
    phases = 2.0 * math.pi * jnp.arange(total_slices, dtype=jnp.int32).astype(jnp.float32) / total_slices
    wide_cos = source_cos.astype(jnp.float32)
    wide_sin = source_sin.astype(jnp.float32)

    def residual_all(field_state):
        def one_slice(items):
            current, previous, phase = items
            block = current[None]
            own = face_traces(block)
            image = apply_operator(block, own, own, neighbor, tags, codes, volume, lifts)[0]
            forcing = jnp.cos(phase) * wide_cos + jnp.sin(phase) * wide_sin
            return forcing - current + previous + image
        return lax.map(one_slice, (field_state, jnp.roll(field_state, 1, axis=0), phases))

    first = residual_all(guess)
    moved = jnp.moveaxis(first.reshape(total_slices, NF, NP ** 3, columns), 1, 0)
    damp_moved = damping.reshape(NF, NP ** 3, columns)
    fixed = lax.map(lambda pair: frequency_solve(pair[0], pair[1]), (moved, damp_moved))
    correction = jnp.moveaxis(fixed, 0, 1).reshape(total_slices, NF * NP ** 3, columns)
    solution = guess + correction
    after_residual = residual_all(solution).astype(jnp.bfloat16)
    return (solution, after_residual)
```

```python
import functools
import math

import jax
import jax.numpy as jnp
import numpy as np
from jax import lax
from jax.experimental import pallas as pl
from jax.experimental.pallas import tpu as pltpu
from jax.sharding import PartitionSpec as P

NF = 5
NP = 4
FACE = NF * NP * NP
LANES = 128
HALF = 64


def split(value):
    high = value.astype(jnp.bfloat16)
    low = (value - high.astype(jnp.float32)).astype(jnp.bfloat16)
    return high, low


def end_trace(cube, face):
    rows = cube[:, 0:16] if face == 0 else cube[:, 48:64]
    return rows.reshape(FACE, LANES)


def side_trace(cube, face):
    tiles = cube.reshape(NF, 2, 2, 16, LANES)
    part = tiles[:, :, :, 0:8] if face == 2 else tiles[:, :, :, 8:16]
    even = part[:, :, 0].reshape(FACE // 8, 8, LANES)
    odd = part[:, :, 1].reshape(FACE // 8, 8, LANES)
    lower = lax.broadcasted_iota(jnp.int32, (FACE // 8, 8, LANES), 1) < 4
    if face == 2:
        odd = pltpu.roll(odd, 4, axis=1)
    else:
        even = pltpu.roll(even, 4, axis=1)
    return jnp.where(lower, even, odd).reshape(FACE, LANES)


def lane_index(row):
    return jnp.broadcast_to(row, (FACE, LANES))


def orientation(code):
    swap = (code & 1) == 1
    turn_i = (code & 2) == 2
    turn_j = (code & 4) == 4
    result = []
    for tile in range(2):
        row = lax.broadcasted_iota(jnp.int32, (8, LANES), 0) + 8 * tile
        i, j = row >> 2, row & 3
        i = jnp.where(turn_i, 3 - i, i)
        j = jnp.where(turn_j, 3 - j, j)
        source = jnp.where(swap, j * 4 + i, i * 4 + j)
        result.append((source >= 8, source & 7))
    return result


def oriented(value, plan):
    pieces = []
    for field in range(NF):
        first = value[field * 16 : field * 16 + 8]
        second = value[field * 16 + 8 : field * 16 + 16]
        for upper, sub in plan:
            pick = functools.partial(jnp.take_along_axis, axis=0, mode="promise_in_bounds")
            pieces.append(jnp.where(upper, pick(second, sub), pick(first, sub)))
    return jnp.concatenate(pieces, axis=0)


def gather_lanes(value, row):
    return jnp.take_along_axis(value, lane_index(row), axis=1, mode="promise_in_bounds")


def operator(state, blocks, stack, weights, volume_ref, lifts_ref, neighbor_ref, tags_ref, codes_ref):
    slices, rows, columns = state.shape
    count = columns // LANES
    wide = slices * columns
    weights[:, 0:rows] = volume_ref[...]
    for face in range(6):
        weights[:, rows + FACE * face : rows + FACE * (face + 1)] = lifts_ref[face]
    lane = lax.broadcasted_iota(jnp.int32, (FACE, LANES), 1)
    for item in range(slices):
        for block in range(count):
            n = item * count + block
            value = state[item, :, block * LANES : (block + 1) * LANES]
            blocks[n] = value
            high, low = split(value)
            stack[0:rows, n * LANES : (n + 1) * LANES] = high
            stack[0:rows, wide + n * LANES : wide + (n + 1) * LANES] = low
    for item in range(slices):
        cubes = []
        turned = []
        for block in range(count):
            cube = blocks[item * count + block].reshape(NF, NP**3, LANES)
            cubes.append(cube)
            turned.append(
                [pltpu.roll(end_trace(cube, face), HALF, axis=1) for face in range(2)]
            )
        zero = jnp.zeros((FACE, LANES), jnp.float32)
        for block in range(count):
            n = item * count + block
            cube = cubes[block]
            before = turned[block - 1][1] if block > 0 else zero
            after = turned[block + 1][0] if block + 1 < count else zero
            ends = [end_trace(cube, 0), end_trace(cube, 1)]
            sides = [side_trace(cube, 2), side_trace(cube, 3)]
            tops = [
                blocks[n, pl.ds(0, FACE, stride=4), :],
                blocks[n, pl.ds(3, FACE, stride=4), :],
            ]
            mine = ends + sides + tops
            across = [
                jnp.where(lane < HALF, before, turned[block][1]),
                jnp.where(lane < HALF, turned[block][0], after),
                sides[1],
                sides[0],
                tops[1],
                tops[0],
            ]
            for face in range(6):
                span = slice(block * LANES, (block + 1) * LANES)
                target = neighbor_ref[face : face + 1, span]
                kind = tags_ref[face : face + 1, span]
                code = codes_ref[face : face + 1, span]
                if face < 2:
                    target = target + HALF
                plan = orientation(code)
                taken = oriented(gather_lanes(across[face], target & (LANES - 1)), plan)
                keep = jnp.where((kind == 1) | (kind == 3), 1.0, 0.0)
                flip = jnp.where(kind == 1, -1.0, keep)
                axis = 1 + face // 2
                inner = []
                for field in range(NF):
                    own = mine[face][field * 16 : (field + 1) * 16]
                    inner.append(own * (flip if field == axis else keep))
                seen = jnp.where(kind == 0, taken, jnp.concatenate(inner, axis=0))
                high, low = split(seen)
                place = rows + FACE * face
                stack[place : place + FACE, n * LANES : (n + 1) * LANES] = high
                stack[place : place + FACE, wide + n * LANES : wide + (n + 1) * LANES] = low
    image = jnp.dot(weights[...], stack[:, 0:wide], preferred_element_type=jnp.float32)
    return image + jnp.dot(weights[...], stack[:, wide:], preferred_element_type=jnp.float32)


def rim(left, right, lifts_ref, neighbor_ref, tags_ref, codes_ref, count):
    slices = left.shape[0]
    lane = lax.broadcasted_iota(jnp.int32, (1, LANES), 1)
    result = []
    for face, halo in ((0, left), (1, right)):
        block = 0 if face == 0 else count - 1
        span = slice(block * LANES, (block + 1) * LANES)
        target = (neighbor_ref[face : face + 1, span] + HALF) & (LANES - 1)
        inside = lane < HALF if face == 0 else lane >= HALF
        use = (tags_ref[face : face + 1, span] == 0) & inside
        plan = orientation(codes_ref[face : face + 1, span])
        pieces = []
        for item in range(slices):
            shifted = pltpu.roll(halo[item], HALF, axis=1)
            seen = jnp.where(use, oriented(gather_lanes(shifted, target), plan), 0.0)
            pieces.append(split(seen))
        both = jnp.concatenate([p[0] for p in pieces] + [p[1] for p in pieces], axis=1)
        product = jnp.dot(lifts_ref[face], both, preferred_element_type=jnp.float32)
        wide = slices * LANES
        result.append(product[:, :wide] + product[:, wide:])
    return result


def send_kernel(state_ref, left_ref, right_ref):
    slices, rows, columns = state_ref.shape
    for item in range(slices):
        for field in range(NF):
            at = field * 64
            to = slice(field * 16, field * 16 + 16)
            left_ref[item, to, :] = state_ref[item, at : at + 16, 0:LANES]
            right_ref[item, to, :] = state_ref[item, at + 48 : at + 64, columns - LANES :]


def forcing_of(waves_ref, item, slices, cos_ref, sin_ref):
    at = lax.axis_index("tm") * slices + item
    return waves_ref[0, at] * cos_ref[...].astype(jnp.float32) + waves_ref[1, at] * sin_ref[
        ...
    ].astype(jnp.float32)


def first_kernel(
    waves_ref, state_ref, cos_ref, sin_ref, damping_ref, volume_ref, lifts_ref, neighbor_ref,
    tags_ref, codes_ref, out_ref, blocks, stack, weights,
):
    slices, _, columns = state_ref.shape
    image = operator(
        state_ref, blocks, stack, weights, volume_ref, lifts_ref, neighbor_ref, tags_ref, codes_ref
    )
    for item in range(slices):
        forcing = forcing_of(waves_ref, item, slices, cos_ref, sin_ref)
        out_ref[item] = (
            image[:, item * columns : (item + 1) * columns]
            + forcing
            + damping_ref[...] * state_ref[item]
        )


def carry_kernel(
    part_ref, left_ref, right_ref, damping_ref, lifts_ref, neighbor_ref, tags_ref, codes_ref,
    out_ref, carry_ref,
):
    slices, _, columns = part_ref.shape
    count = columns // LANES
    low, high = rim(left_ref, right_ref, lifts_ref, neighbor_ref, tags_ref, codes_ref, count)
    for block in range(count):
        span = slice(block * LANES, (block + 1) * LANES)
        rate = 1.0 / (1.0 + damping_ref[:, span])
        carry = None
        for item in range(slices):
            value = part_ref[item, :, span]
            piece = slice(item * LANES, (item + 1) * LANES)
            if block == 0:
                value = value + low[:, piece]
            if block == count - 1:
                value = value + high[:, piece]
            out_ref[item, :, span] = value
            carry = rate * value if carry is None else rate * (carry + value)
        carry_ref[:, span] = carry


def solve_kernel(pieces, *refs):
    piece_refs = refs[:pieces]
    right_ref, damping_ref, state_ref, before_ref, low_ref, high_ref = refs[pieces:]
    slices, rows, columns = right_ref.shape
    if pieces == 1:
        before_ref[...] = piece_refs[0][...]
    else:
        share = rows // pieces
        me = lax.axis_index("tm")
        for step in range(pieces):
            owner = lax.rem(me + pieces - step, pieces)
            before_ref[pl.ds(pl.multiple_of(owner * share, 8), share), :] = piece_refs[step][...]
    rate = 1.0 / (1.0 + damping_ref[...])
    value = before_ref[...]
    for item in range(slices):
        value = rate * (value + right_ref[item])
        state_ref[item] = value
    send_kernel(state_ref, low_ref, high_ref)


def second_kernel(
    waves_ref, state_ref, before_ref, cos_ref, sin_ref, volume_ref, lifts_ref, neighbor_ref,
    tags_ref, codes_ref, out_ref, blocks, stack, weights,
):
    slices, _, columns = state_ref.shape
    image = operator(
        state_ref, blocks, stack, weights, volume_ref, lifts_ref, neighbor_ref, tags_ref, codes_ref
    )
    for item in range(slices):
        forcing = forcing_of(waves_ref, item, slices, cos_ref, sin_ref)
        previous = before_ref[...] if item == 0 else state_ref[item - 1]
        out_ref[item] = (
            image[:, item * columns : (item + 1) * columns]
            + forcing
            + (previous - state_ref[item])
        )


def finish_kernel(
    part_ref, left_ref, right_ref, lifts_ref, neighbor_ref, tags_ref, codes_ref, out_ref
):
    slices, _, columns = part_ref.shape
    count = columns // LANES
    low, high = rim(left_ref, right_ref, lifts_ref, neighbor_ref, tags_ref, codes_ref, count)
    for block in range(count):
        span = slice(block * LANES, (block + 1) * LANES)
        for item in range(slices):
            value = part_ref[item, :, span]
            piece = slice(item * LANES, (item + 1) * LANES)
            if block == 0:
                value = value + low[:, piece]
            if block == count - 1:
                value = value + high[:, piece]
            out_ref[item, :, span] = value.astype(out_ref.dtype)


def call(kernel, name, outs, args, scratch=(), scalars=0, flops=0):
    vmem = pl.BlockSpec(memory_space=pltpu.VMEM)
    smem = pl.BlockSpec(memory_space=pltpu.SMEM)
    size = sum(math.prod(a.shape) * a.dtype.itemsize for a in list(args) + list(outs))
    return pl.pallas_call(
        kernel,
        name=name,
        out_shape=outs,
        in_specs=[smem] * scalars + [vmem] * (len(args) - scalars),
        out_specs=[vmem] * len(outs),
        scratch_shapes=list(scratch),
        compiler_params=pltpu.CompilerParams(vmem_limit_bytes=40 * 2**20),
        cost_estimate=pl.CostEstimate(flops=flops, bytes_accessed=size, transcendentals=0),
    )(*args)


def halos(low, high):
    count = lax.axis_size("space")
    left = lax.ppermute(high, "space", [(i, i + 1) for i in range(count - 1)])
    right = lax.ppermute(low, "space", [(i + 1, i) for i in range(count - 1)])
    return left, right


def turned(value, distance):
    count = lax.axis_size("tm")
    return lax.ppermute(value, "tm", [(i, (i + distance) % count) for i in range(count)])


def periodic(carries, factor):
    count = len(carries)
    total = carries[0]
    for k in range(1, count):
        total = carries[k] + factor * total
    power = factor
    for _ in range(count - 1):
        power = power * factor
    entering = [total / (1.0 - power)]
    for k in range(count - 1):
        entering.append(carries[k] + factor * entering[-1])
    return entering


def around(carry, damping, slices):
    count = lax.axis_size("tm")
    rows = carry.shape[0]
    share = rows // count
    me = lax.axis_index("tm")
    rate = 1.0 / (1.0 + lax.dynamic_slice_in_dim(damping, me * share, share, 0))
    factor = rate
    for _ in range(slices - 1):
        factor = factor * rate
    if count > 8 or share % 8:
        parts = lax.all_to_all(carry, "tm", split_axis=0, concat_axis=0, tiled=True)
        parts = parts.reshape(count, share, -1)
        back = jnp.concatenate(periodic([parts[k] for k in range(count)], factor), axis=0)
        return [lax.all_to_all(back, "tm", split_axis=0, concat_axis=0, tiled=True)]
    parts = carry.reshape(count, share, -1)
    sent = [
        lax.dynamic_index_in_dim(parts, lax.rem(me + d, count), 0, keepdims=False)
        for d in range(count)
    ]
    got = [sent[0]] + [turned(sent[d], d) for d in range(1, count)]
    entering = periodic([got[(count - k) % count] for k in range(count)], factor)
    return [entering[0]] + [turned(entering[d], d) for d in range(1, count)]


def local(guess, source_cos, source_sin, damping, volume, lifts, neighbor, tags, codes):
    slices, rows, columns = guess.shape
    total = slices * lax.axis_size("tm")
    angles = 2.0 * np.pi * np.arange(total) / total
    waves = jnp.asarray(np.stack([np.cos(angles), np.sin(angles)]).astype(np.float32))
    f32 = jnp.float32
    whole = jax.ShapeDtypeStruct((slices, rows, columns), f32)
    plane = jax.ShapeDtypeStruct((rows, columns), f32)
    rimmed = jax.ShapeDtypeStruct((slices, FACE, LANES), f32)
    tables = (lifts, neighbor, tags, codes)
    depth = rows + 6 * FACE
    scratch = (
        pltpu.VMEM((slices * columns // LANES, rows, LANES), f32),
        pltpu.VMEM((depth, 2 * slices * columns), jnp.bfloat16),
        pltpu.VMEM((rows, depth), jnp.bfloat16),
    )
    work = 4 * rows * depth * slices * columns

    low, high = call(send_kernel, "ends", [rimmed] * 2, [guess])
    left, right = halos(low, high)
    (part,) = call(
        first_kernel, "first", [whole],
        [waves, guess, source_cos, source_sin, damping, volume, *tables],
        scratch, scalars=1, flops=work,
    )
    known, carry = call(
        carry_kernel, "carry", [whole, plane], [part, left, right, damping, *tables]
    )
    pieces = around(carry, damping, slices)
    state, before, low, high = call(
        functools.partial(solve_kernel, len(pieces)), "solve",
        [whole, plane, rimmed, rimmed], [*pieces, known, damping],
    )
    left, right = halos(low, high)
    (part,) = call(
        second_kernel, "second", [whole],
        [waves, state, before, source_cos, source_sin, volume, *tables],
        scratch, scalars=1, flops=work,
    )
    (after,) = call(
        finish_kernel, "finish", [jax.ShapeDtypeStruct(whole.shape, jnp.bfloat16)],
        [part, left, right, *tables],
    )
    return state, after


def solution(mesh):
    column = P(None, ("groups", "space"))
    state = P("tm", None, ("groups", "space"))
    in_specs = (state, column, column, column, P(), P(), column, column, column)
    return jax.shard_map(
        local, mesh=mesh, in_specs=in_specs, out_specs=(state, state), check_vma=False
    )
```

```python
import functools
import math

import jax
import jax.numpy as jnp
import numpy as np
from jax import lax
from jax.experimental import pallas as pl
from jax.experimental.pallas import tpu as pltpu
from jax.sharding import PartitionSpec as P

NF = 5
NP = 4
FACE = NF * NP * NP
LANES = 128
HALF = 64


def split(value):
    high = value.astype(jnp.bfloat16)
    low = (value - high.astype(jnp.float32)).astype(jnp.bfloat16)
    return high, low


def end_trace(cube, face):
    rows = cube[:, 0:16] if face == 0 else cube[:, 48:64]
    return rows.reshape(FACE, LANES)


def side_trace(cube, face):
    tiles = cube.reshape(NF, 2, 2, 16, LANES)
    part = tiles[:, :, :, 0:8] if face == 2 else tiles[:, :, :, 8:16]
    even = part[:, :, 0].reshape(FACE // 8, 8, LANES)
    odd = part[:, :, 1].reshape(FACE // 8, 8, LANES)
    lower = lax.broadcasted_iota(jnp.int32, (FACE // 8, 8, LANES), 1) < 4
    if face == 2:
        odd = pltpu.roll(odd, 4, axis=1)
    else:
        even = pltpu.roll(even, 4, axis=1)
    return jnp.where(lower, even, odd).reshape(FACE, LANES)


def lane_index(row):
    return jnp.broadcast_to(row, (FACE, LANES))


def orientation(code):
    swap = (code & 1) == 1
    turn_i = (code & 2) == 2
    turn_j = (code & 4) == 4
    result = []
    for tile in range(2):
        row = lax.broadcasted_iota(jnp.int32, (8, LANES), 0) + 8 * tile
        i, j = row >> 2, row & 3
        i = jnp.where(turn_i, 3 - i, i)
        j = jnp.where(turn_j, 3 - j, j)
        source = jnp.where(swap, j * 4 + i, i * 4 + j)
        result.append((source >= 8, source & 7))
    return result


def oriented(value, plan):
    pieces = []
    for field in range(NF):
        first = value[field * 16 : field * 16 + 8]
        second = value[field * 16 + 8 : field * 16 + 16]
        for upper, sub in plan:
            pick = functools.partial(jnp.take_along_axis, axis=0, mode="promise_in_bounds")
            pieces.append(jnp.where(upper, pick(second, sub), pick(first, sub)))
    return jnp.concatenate(pieces, axis=0)


def gather_lanes(value, row):
    return jnp.take_along_axis(value, lane_index(row), axis=1, mode="promise_in_bounds")


def operator(state, blocks, stack, weights_ref, neighbor_ref, tags_ref, codes_ref):
    slices, rows, columns = state.shape
    count = columns // LANES
    wide = slices * columns
    base = 6 * FACE
    lane = lax.broadcasted_iota(jnp.int32, (FACE, LANES), 1)
    for item in range(slices):
        for block in range(count):
            n = item * count + block
            value = state[item, :, block * LANES : (block + 1) * LANES]
            blocks[n] = value
            high, low = split(value)
            stack[base:, n * LANES : (n + 1) * LANES] = high
            stack[base:, wide + n * LANES : wide + (n + 1) * LANES] = low
    for item in range(slices):
        cubes = []
        turned = []
        for block in range(count):
            cube = blocks[item * count + block].reshape(NF, NP**3, LANES)
            cubes.append(cube)
            turned.append(
                [pltpu.roll(end_trace(cube, face), HALF, axis=1) for face in range(2)]
            )
        zero = jnp.zeros((FACE, LANES), jnp.float32)
        for block in range(count):
            n = item * count + block
            cube = cubes[block]
            before = turned[block - 1][1] if block > 0 else zero
            after = turned[block + 1][0] if block + 1 < count else zero
            ends = [end_trace(cube, 0), end_trace(cube, 1)]
            sides = [side_trace(cube, 2), side_trace(cube, 3)]
            tops = [
                blocks[n, pl.ds(0, FACE, stride=4), :],
                blocks[n, pl.ds(3, FACE, stride=4), :],
            ]
            mine = ends + sides + tops
            across = [
                jnp.where(lane < HALF, before, turned[block][1]),
                jnp.where(lane < HALF, turned[block][0], after),
                sides[1],
                sides[0],
                tops[1],
                tops[0],
            ]
            for face in range(6):
                span = slice(block * LANES, (block + 1) * LANES)
                target = neighbor_ref[face : face + 1, span]
                kind = tags_ref[face : face + 1, span]
                code = codes_ref[face : face + 1, span]
                if face < 2:
                    target = target + HALF
                plan = orientation(code)
                taken = oriented(gather_lanes(across[face], target & (LANES - 1)), plan)
                keep = jnp.where((kind == 1) | (kind == 3), 1.0, 0.0)
                flip = jnp.where(kind == 1, -1.0, keep)
                axis = 1 + face // 2
                inner = []
                for field in range(NF):
                    own = mine[face][field * 16 : (field + 1) * 16]
                    inner.append(own * (flip if field == axis else keep))
                seen = jnp.where(kind == 0, taken, jnp.concatenate(inner, axis=0))
                high, low = split(seen)
                place = FACE * face
                stack[place : place + FACE, n * LANES : (n + 1) * LANES] = high
                stack[place : place + FACE, wide + n * LANES : wide + (n + 1) * LANES] = low
    image = jnp.dot(weights_ref[...], stack[:, 0:wide], preferred_element_type=jnp.float32)
    return image + jnp.dot(
        weights_ref[...], stack[:, wide:], preferred_element_type=jnp.float32
    )


def even_place():
    return (lax.axis_index("space") & 1) == 0


def rim(near, far, slices, rim_weights_ref, neighbor_ref, tags_ref, codes_ref, count):
    lane = lax.broadcasted_iota(jnp.int32, (1, LANES), 1)
    even = even_place()
    result = []
    for face in range(2):
        block = 0 if face == 0 else count - 1
        span = slice(block * LANES, (block + 1) * LANES)
        target = neighbor_ref[face : face + 1, span] & (HALF - 1)
        inside = lane < HALF if face == 0 else lane >= HALF
        use = (tags_ref[face : face + 1, span] == 0) & inside
        plan = orientation(codes_ref[face : face + 1, span])
        pieces = []
        for item in range(slices):
            a, b = (far, near) if face == 0 else (near, far)
            halo = jnp.where(even, a[item // 2], b[item // 2])
            taken = gather_lanes(halo, target + HALF * (item % 2))
            pieces.append(split(jnp.where(use, oriented(taken, plan), 0.0)))
        both = jnp.concatenate([p[0] for p in pieces] + [p[1] for p in pieces], axis=1)
        product = jnp.dot(rim_weights_ref[face], both, preferred_element_type=jnp.float32)
        wide = slices * LANES
        result.append(product[:, :wide] + product[:, wide:])
    return result


def send(low, high, near_ref, far_ref):
    slices = len(low)
    lane = lax.broadcasted_iota(jnp.int32, (FACE, LANES), 1)
    even = even_place()
    for item in range(0, slices, 2):
        other = min(item + 1, slices - 1)
        first = jnp.where(lane < HALF, low[item], pltpu.roll(low[other], HALF, axis=1))
        last = jnp.where(lane < HALF, pltpu.roll(high[item], HALF, axis=1), high[other])
        near_ref[item // 2] = jnp.where(even, last, first)
        far_ref[item // 2] = jnp.where(even, first, last)


def ends_kernel(state_ref, near_ref, far_ref, low, high, semaphore):
    slices, _, _, columns = state_ref.shape
    copies = [
        pltpu.make_async_copy(
            state_ref.at[:, :, pl.ds(0, 16), pl.ds(0, LANES)], low, semaphore.at[0]
        ),
        pltpu.make_async_copy(
            state_ref.at[:, :, pl.ds(48, 16), pl.ds(columns - LANES, LANES)], high, semaphore.at[1]
        ),
    ]
    for copy in copies:
        copy.start()
    for copy in copies:
        copy.wait()
    send(
        [low[item].reshape(FACE, LANES) for item in range(slices)],
        [high[item].reshape(FACE, LANES) for item in range(slices)],
        near_ref,
        far_ref,
    )


def forcing_of(waves_ref, item, slices, cos_ref, sin_ref):
    at = lax.axis_index("tm") * slices + item
    return waves_ref[0, at] * cos_ref[...].astype(jnp.float32) + waves_ref[1, at] * sin_ref[
        ...
    ].astype(jnp.float32)


def first_kernel(
    waves_ref, state_ref, cos_ref, sin_ref, damping_ref, volume_ref, lifts_ref, neighbor_ref,
    tags_ref, codes_ref, out_ref, weights_ref, rim_weights_ref, rate_ref, blocks, stack,
):
    slices, _, columns = state_ref.shape
    for face in range(6):
        lift = lifts_ref[face].T
        weights_ref[:, FACE * face : FACE * (face + 1)] = lift
        if face < 2:
            rim_weights_ref[face] = lift
    weights_ref[:, 6 * FACE :] = volume_ref[...]
    rate_ref[...] = 1.0 / (1.0 + damping_ref[...])
    image = operator(
        state_ref, blocks, stack, weights_ref, neighbor_ref, tags_ref, codes_ref
    )
    for item in range(slices):
        forcing = forcing_of(waves_ref, item, slices, cos_ref, sin_ref)
        out_ref[item] = (
            image[:, item * columns : (item + 1) * columns]
            + forcing
            + damping_ref[...] * state_ref[item]
        )


def carry_kernel(
    part_ref, near_ref, far_ref, rate_ref, rim_weights_ref, neighbor_ref, tags_ref, codes_ref,
    out_ref, carry_ref,
):
    slices, _, columns = part_ref.shape
    count = columns // LANES
    low, high = rim(
        near_ref, far_ref, slices, rim_weights_ref, neighbor_ref, tags_ref, codes_ref, count
    )
    for block in range(count):
        span = slice(block * LANES, (block + 1) * LANES)
        rate = rate_ref[:, span]
        carry = None
        for item in range(slices):
            value = part_ref[item, :, span]
            piece = slice(item * LANES, (item + 1) * LANES)
            if block == 0:
                value = value + low[:, piece]
            if block == count - 1:
                value = value + high[:, piece]
            out_ref[item, :, span] = value
            carry = rate * value if carry is None else rate * (carry + value)
        carry_ref[:, span] = carry


def solve_kernel(pieces, *refs):
    piece_refs = refs[:pieces]
    right_ref, rate_ref, state_ref, before_ref, near_ref, far_ref = refs[pieces:]
    slices, rows, columns = right_ref.shape
    if pieces == 1:
        before_ref[...] = piece_refs[0][...]
    else:
        share = rows // pieces
        me = lax.axis_index("tm")
        for step in range(pieces):
            owner = lax.rem(me + pieces - step, pieces)
            before_ref[pl.ds(pl.multiple_of(owner * share, 8), share), :] = piece_refs[step][...]
    rate = rate_ref[...]
    value = before_ref[...]
    low = []
    high = []
    for item in range(slices):
        value = rate * (value + right_ref[item])
        state_ref[item] = value
        cube = value.reshape(NF, NP**3, columns)
        low.append(cube[:, 0:16, 0:LANES].reshape(FACE, LANES))
        high.append(cube[:, 48:64, columns - LANES :].reshape(FACE, LANES))
    send(low, high, near_ref, far_ref)


def second_kernel(
    waves_ref, state_ref, before_ref, cos_ref, sin_ref, weights_ref, neighbor_ref, tags_ref,
    codes_ref, out_ref, result_ref, blocks, stack, semaphore,
):
    slices, _, columns = state_ref.shape
    copy = pltpu.make_async_copy(state_ref, result_ref, semaphore)
    copy.start()
    image = operator(
        state_ref, blocks, stack, weights_ref, neighbor_ref, tags_ref, codes_ref
    )
    for item in range(slices):
        forcing = forcing_of(waves_ref, item, slices, cos_ref, sin_ref)
        previous = before_ref[...] if item == 0 else state_ref[item - 1]
        out_ref[item] = (
            image[:, item * columns : (item + 1) * columns]
            + forcing
            + (previous - state_ref[item])
        )
    copy.wait()


def finish_kernel(
    part_ref, near_ref, far_ref, rim_weights_ref, neighbor_ref, tags_ref, codes_ref, out_ref
):
    slices, _, columns = part_ref.shape
    count = columns // LANES
    low, high = rim(
        near_ref, far_ref, slices, rim_weights_ref, neighbor_ref, tags_ref, codes_ref, count
    )
    for block in range(count):
        span = slice(block * LANES, (block + 1) * LANES)
        for item in range(slices):
            value = part_ref[item, :, span]
            piece = slice(item * LANES, (item + 1) * LANES)
            if block == 0:
                value = value + low[:, piece]
            if block == count - 1:
                value = value + high[:, piece]
            out_ref[item, :, span] = value.astype(out_ref.dtype)


VMEM = pl.BlockSpec(memory_space=pltpu.VMEM)
SMEM = pl.BlockSpec(memory_space=pltpu.SMEM)
HBM = pl.BlockSpec(memory_space=pltpu.HBM)


def call(kernel, name, outs, args, scratch=(), flops=0, in_specs=None, out_specs=None):
    size = sum(math.prod(a.shape) * a.dtype.itemsize for a in list(args) + list(outs))
    return pl.pallas_call(
        kernel,
        name=name,
        out_shape=outs,
        in_specs=in_specs or [VMEM] * len(args),
        out_specs=out_specs or [VMEM] * len(outs),
        scratch_shapes=list(scratch),
        compiler_params=pltpu.CompilerParams(vmem_limit_bytes=40 * 2**20),
        cost_estimate=pl.CostEstimate(flops=flops, bytes_accessed=size, transcendentals=0),
    )(*args)


def exchange(near, far):
    count = lax.axis_size("space")
    inner = [(i, i + 1) for i in range(0, count - 1, 2)]
    outer = [(i, i + 1) for i in range(1, count - 1, 2)]
    near = lax.ppermute(near, "space", inner + [(j, i) for i, j in inner])
    far = lax.ppermute(far, "space", outer + [(j, i) for i, j in outer])
    return near, far


def turned(value, distance):
    count = lax.axis_size("tm")
    return lax.ppermute(value, "tm", [(i, (i + distance) % count) for i in range(count)])


def periodic(carries, factor):
    count = len(carries)
    total = carries[0]
    for k in range(1, count):
        total = carries[k] + factor * total
    power = factor
    for _ in range(count - 1):
        power = power * factor
    entering = [total / (1.0 - power)]
    for k in range(count - 1):
        entering.append(carries[k] + factor * entering[-1])
    return entering


def around(carry, damping, slices):
    count = lax.axis_size("tm")
    rows = carry.shape[0]
    share = rows // count
    me = lax.axis_index("tm")
    rate = 1.0 / (1.0 + lax.dynamic_slice_in_dim(damping, me * share, share, 0))
    factor = rate
    for _ in range(slices - 1):
        factor = factor * rate
    if count > 8 or share % 8:
        parts = lax.all_to_all(carry, "tm", split_axis=0, concat_axis=0, tiled=True)
        parts = parts.reshape(count, share, -1)
        back = jnp.concatenate(periodic([parts[k] for k in range(count)], factor), axis=0)
        return [lax.all_to_all(back, "tm", split_axis=0, concat_axis=0, tiled=True)]
    parts = carry.reshape(count, share, -1)
    sent = [
        lax.dynamic_index_in_dim(parts, lax.rem(me + d, count), 0, keepdims=False)
        for d in range(count)
    ]
    got = [sent[0]] + [turned(sent[d], d) for d in range(1, count)]
    entering = periodic([got[(count - k) % count] for k in range(count)], factor)
    return [entering[0]] + [turned(entering[d], d) for d in range(1, count)]


def local(guess, source_cos, source_sin, damping, volume, lifts, neighbor, tags, codes):
    slices, rows, columns = guess.shape
    total = slices * lax.axis_size("tm")
    angles = 2.0 * np.pi * np.arange(total) / total
    waves = jnp.asarray(np.stack([np.cos(angles), np.sin(angles)]).astype(np.float32))
    f32, bf16 = jnp.float32, jnp.bfloat16
    shape = jax.ShapeDtypeStruct
    whole = shape((slices, rows, columns), f32)
    plane = shape((rows, columns), f32)
    packed = shape(((slices + 1) // 2, FACE, LANES), f32)
    tables = (neighbor, tags, codes)
    depth = rows + 6 * FACE
    scratch = [
        pltpu.VMEM((slices * columns // LANES, rows, LANES), f32),
        pltpu.VMEM((depth, 2 * slices * columns), bf16),
    ]
    work = 4 * rows * depth * slices * columns
    end = pltpu.VMEM((slices, NF, NP * NP, LANES), f32)

    near, far = call(
        ends_kernel, "ends", [packed] * 2,
        [guess.reshape(slices, NF, NP**3, columns)],
        [end, end, pltpu.SemaphoreType.DMA((2,))], in_specs=[HBM],
    )
    near, far = exchange(near, far)
    part, weights, rim_weights, rate = call(
        first_kernel, "first",
        [whole, shape((rows, depth), bf16), shape((2, rows, FACE), bf16), plane],
        [
            waves, guess, source_cos, source_sin, damping, volume, jnp.swapaxes(lifts, 1, 2),
            *tables,
        ],
        scratch, flops=work, in_specs=[SMEM] + [VMEM] * 9,
    )
    known, carry = call(
        carry_kernel, "carry", [whole, plane], [part, near, far, rate, rim_weights, *tables]
    )
    pieces = around(carry, damping, slices)
    state, before, near, far = call(
        functools.partial(solve_kernel, len(pieces)), "solve",
        [whole, plane, packed, packed], [*pieces, known, rate],
    )
    near, far = exchange(near, far)
    part, result = call(
        second_kernel, "second", [whole, whole],
        [waves, state, before, source_cos, source_sin, weights, *tables],
        [*scratch, pltpu.SemaphoreType.DMA], flops=work,
        in_specs=[SMEM] + [VMEM] * 8, out_specs=[VMEM, HBM],
    )
    (after,) = call(
        finish_kernel, "finish", [shape(whole.shape, bf16)],
        [part, near, far, rim_weights, *tables],
    )
    return result, after


def solution(mesh):
    column = P(None, ("groups", "space"))
    state = P("tm", None, ("groups", "space"))
    in_specs = (state, column, column, column, P(), P(), column, column, column)
    return jax.shard_map(
        local, mesh=mesh, in_specs=in_specs, out_specs=(state, state), check_vma=False
    )
```

```python
import functools
import math

import jax
import jax.numpy as jnp
from jax import lax
from jax.experimental import pallas as pl
from jax.experimental.pallas import tpu as pltpu
from jax.sharding import PartitionSpec as P

NF = 5
NP = 4
FACE = NF * NP * NP
LANES = 128
HALF = 64


def split(value):
    high = value.astype(jnp.bfloat16)
    low = (value - high.astype(jnp.float32)).astype(jnp.bfloat16)
    return high, low


def end_trace(cube, face):
    rows = cube[:, 0:16] if face == 0 else cube[:, 48:64]
    return rows.reshape(FACE, LANES)


def side_trace(cube, face):
    tiles = cube.reshape(NF, 2, 2, 16, LANES)
    part = tiles[:, :, :, 0:8] if face == 2 else tiles[:, :, :, 8:16]
    even = part[:, :, 0].reshape(FACE // 8, 8, LANES)
    odd = part[:, :, 1].reshape(FACE // 8, 8, LANES)
    lower = lax.broadcasted_iota(jnp.int32, (FACE // 8, 8, LANES), 1) < 4
    if face == 2:
        odd = pltpu.roll(odd, 4, axis=1)
    else:
        even = pltpu.roll(even, 4, axis=1)
    return jnp.where(lower, even, odd).reshape(FACE, LANES)


def lane_index(row):
    return jnp.broadcast_to(row, (FACE, LANES))


def orientation(code):
    swap = (code & 1) == 1
    turn_i = (code & 2) == 2
    turn_j = (code & 4) == 4
    result = []
    for tile in range(2):
        row = lax.broadcasted_iota(jnp.int32, (8, LANES), 0) + 8 * tile
        i, j = row >> 2, row & 3
        i = jnp.where(turn_i, 3 - i, i)
        j = jnp.where(turn_j, 3 - j, j)
        source = jnp.where(swap, j * 4 + i, i * 4 + j)
        result.append((source >= 8, source & 7))
    return result


def oriented(value, plan):
    pieces = []
    for field in range(NF):
        first = value[field * 16 : field * 16 + 8]
        second = value[field * 16 + 8 : field * 16 + 16]
        for upper, sub in plan:
            pick = functools.partial(jnp.take_along_axis, axis=0, mode="promise_in_bounds")
            pieces.append(jnp.where(upper, pick(second, sub), pick(first, sub)))
    return jnp.concatenate(pieces, axis=0)


def gather_lanes(value, row):
    return jnp.take_along_axis(value, lane_index(row), axis=1, mode="promise_in_bounds")


def operator(
    state, blocks, stack, weights_ref, neighbor_ref, tags_ref, codes_ref, ahead=lambda: None
):
    slices, rows, columns = state.shape
    count = columns // LANES
    wide = slices * columns
    base = 6 * FACE
    lane = lax.broadcasted_iota(jnp.int32, (FACE, LANES), 1)
    for item in range(slices):
        for block in range(count):
            n = item * count + block
            value = state[item, :, block * LANES : (block + 1) * LANES]
            blocks[n] = value
            high, low = split(value)
            stack[base:, n * LANES : (n + 1) * LANES] = high
            stack[base:, wide + n * LANES : wide + (n + 1) * LANES] = low
    for item in range(slices):
        cubes = []
        turned = []
        for block in range(count):
            cube = blocks[item * count + block].reshape(NF, NP**3, LANES)
            cubes.append(cube)
            turned.append(
                [pltpu.roll(end_trace(cube, face), HALF, axis=1) for face in range(2)]
            )
        zero = jnp.zeros((FACE, LANES), jnp.float32)
        for block in range(count):
            n = item * count + block
            cube = cubes[block]
            before = turned[block - 1][1] if block > 0 else zero
            after = turned[block + 1][0] if block + 1 < count else zero
            ends = [end_trace(cube, 0), end_trace(cube, 1)]
            sides = [side_trace(cube, 2), side_trace(cube, 3)]
            tops = [
                blocks[n, pl.ds(0, FACE, stride=4), :],
                blocks[n, pl.ds(3, FACE, stride=4), :],
            ]
            mine = ends + sides + tops
            across = [
                jnp.where(lane < HALF, before, turned[block][1]),
                jnp.where(lane < HALF, turned[block][0], after),
                sides[1],
                sides[0],
                tops[1],
                tops[0],
            ]
            for face in range(6):
                span = slice(block * LANES, (block + 1) * LANES)
                target = neighbor_ref[face : face + 1, span]
                kind = tags_ref[face : face + 1, span]
                code = codes_ref[face : face + 1, span]
                if face < 2:
                    target = target + HALF
                plan = orientation(code)
                taken = oriented(gather_lanes(across[face], target & (LANES - 1)), plan)
                keep = jnp.where((kind == 1) | (kind == 3), 1.0, 0.0)
                flip = jnp.where(kind == 1, -1.0, keep)
                axis = 1 + face // 2
                inner = []
                for field in range(NF):
                    own = mine[face][field * 16 : (field + 1) * 16]
                    inner.append(own * (flip if field == axis else keep))
                seen = jnp.where(kind == 0, taken, jnp.concatenate(inner, axis=0))
                high, low = split(seen)
                place = FACE * face
                stack[place : place + FACE, n * LANES : (n + 1) * LANES] = high
                stack[place : place + FACE, wide + n * LANES : wide + (n + 1) * LANES] = low
    ahead()
    image = jnp.dot(weights_ref[...], stack[:, 0:wide], preferred_element_type=jnp.float32)
    return image + jnp.dot(
        weights_ref[...], stack[:, wide:], preferred_element_type=jnp.float32
    )


def even_place():
    return (lax.axis_index("space") & 1) == 0


def rim(near, far, slices, rim_weights_ref, neighbor_ref, tags_ref, codes_ref, count):
    lane = lax.broadcasted_iota(jnp.int32, (1, LANES), 1)
    even = even_place()
    result = []
    for face in range(2):
        block = 0 if face == 0 else count - 1
        span = slice(block * LANES, (block + 1) * LANES)
        target = neighbor_ref[face : face + 1, span] & (HALF - 1)
        inside = lane < HALF if face == 0 else lane >= HALF
        use = (tags_ref[face : face + 1, span] == 0) & inside
        plan = orientation(codes_ref[face : face + 1, span])
        pieces = []
        for item in range(slices):
            a, b = (far, near) if face == 0 else (near, far)
            halo = jnp.where(even, a[item // 2], b[item // 2])
            taken = gather_lanes(halo, target + HALF * (item % 2))
            pieces.append(split(jnp.where(use, oriented(taken, plan), 0.0)))
        both = jnp.concatenate([p[0] for p in pieces] + [p[1] for p in pieces], axis=1)
        product = jnp.dot(rim_weights_ref[face], both, preferred_element_type=jnp.float32)
        wide = slices * LANES
        result.append(product[:, :wide] + product[:, wide:])
    return result


def send(low, high, near_ref, far_ref):
    slices = len(low)
    lane = lax.broadcasted_iota(jnp.int32, (FACE, LANES), 1)
    even = even_place()
    for item in range(0, slices, 2):
        other = min(item + 1, slices - 1)
        first = jnp.where(lane < HALF, low[item], pltpu.roll(low[other], HALF, axis=1))
        last = jnp.where(lane < HALF, pltpu.roll(high[item], HALF, axis=1), high[other])
        near_ref[item // 2] = jnp.where(even, last, first)
        far_ref[item // 2] = jnp.where(even, first, last)


def ends_kernel(state_ref, near_ref, far_ref, low, high, semaphore):
    slices, _, _, columns = state_ref.shape
    copies = [
        pltpu.make_async_copy(
            state_ref.at[:, :, pl.ds(0, 16), pl.ds(0, LANES)], low, semaphore.at[0]
        ),
        pltpu.make_async_copy(
            state_ref.at[:, :, pl.ds(48, 16), pl.ds(columns - LANES, LANES)], high, semaphore.at[1]
        ),
    ]
    for copy in copies:
        copy.start()
    for copy in copies:
        copy.wait()
    send(
        [low[item].reshape(FACE, LANES) for item in range(slices)],
        [high[item].reshape(FACE, LANES) for item in range(slices)],
        near_ref,
        far_ref,
    )


def wave(at, values):
    result = jnp.float32(values[0])
    for k in range(1, len(values)):
        result = jnp.where(at == k, jnp.float32(values[k]), result)
    return result


def first_kernel(total, *refs):
    sources = refs[:9]
    out_ref, weights_ref, rim_weights_ref, rate_ref, forcing_ref = refs[9:14]
    neighbor_ref, tags_ref, codes_ref = refs[14:17]
    state_ref, cos_ref, sin_ref, damping_ref, volume_ref, lifts_ref = refs[17:23]
    blocks, stack, semaphores = refs[23:]
    targets = (
        state_ref, neighbor_ref, tags_ref, codes_ref, lifts_ref, volume_ref, damping_ref,
        cos_ref, sin_ref,
    )
    copies = [
        pltpu.make_async_copy(source, target, semaphores.at[k])
        for k, (source, target) in enumerate(zip(sources, targets))
    ]
    for copy in copies:
        copy.start()
    for copy in copies[:4]:
        copy.wait()
    slices, _, columns = state_ref.shape

    def ahead():
        for copy in copies[4:]:
            copy.wait()
        for face in range(6):
            lift = lifts_ref[face].T
            weights_ref[:, FACE * face : FACE * (face + 1)] = lift
            if face < 2:
                rim_weights_ref[face] = lift
        weights_ref[:, 6 * FACE :] = volume_ref[...]

    image = operator(
        state_ref, blocks, stack, weights_ref, neighbor_ref, tags_ref, codes_ref, ahead
    )
    rate_ref[...] = 1.0 / (1.0 + damping_ref[...])
    angles = [2.0 * math.pi * k / total for k in range(total)]
    for item in range(slices):
        at = lax.axis_index("tm") * slices + item
        forcing = wave(at, [math.cos(x) for x in angles]) * cos_ref[...].astype(jnp.float32)
        forcing += wave(at, [math.sin(x) for x in angles]) * sin_ref[...].astype(jnp.float32)
        forcing_ref[item] = forcing
        out_ref[item] = (
            image[:, item * columns : (item + 1) * columns]
            + forcing
            + damping_ref[...] * state_ref[item]
        )


def carry_kernel(
    pieces, part_ref, near_ref, far_ref, rate_ref, rim_weights_ref, neighbor_ref, tags_ref,
    codes_ref, out_ref, *refs
):
    *piece_refs, carry_ref = refs
    slices, rows, columns = part_ref.shape
    count = columns // LANES
    low, high = rim(
        near_ref, far_ref, slices, rim_weights_ref, neighbor_ref, tags_ref, codes_ref, count
    )
    for block in range(count):
        span = slice(block * LANES, (block + 1) * LANES)
        rate = rate_ref[:, span]
        carry = None
        for item in range(slices):
            value = part_ref[item, :, span]
            piece = slice(item * LANES, (item + 1) * LANES)
            if block == 0:
                value = value + low[:, piece]
            if block == count - 1:
                value = value + high[:, piece]
            out_ref[item, :, span] = value
            carry = rate * value if carry is None else rate * (carry + value)
        carry_ref[:, span] = carry
    if pieces == 1:
        piece_refs[0][...] = carry_ref[...]
    else:
        for step in range(pieces):
            piece_refs[step][...] = carry_ref[row_part(step, pieces, rows), :]


def row_part(step, pieces, rows):
    share = rows // pieces
    return pl.ds(pl.multiple_of((lax.axis_index("tm") ^ step) * share, 8), share)


def periodic(carries, factor):
    count = len(carries)
    total = carries[0]
    for k in range(1, count):
        total = carries[k] + factor * total
    power = factor
    for _ in range(count - 1):
        power = power * factor
    entering = [total / (1.0 - power)]
    for k in range(count - 1):
        entering.append(carries[k] + factor * entering[-1])
    return entering


def around_kernel(slices, pieces, *refs):
    got, rate_ref = refs[:pieces], refs[pieces]
    sent, held = refs[pieces + 1 : 2 * pieces + 1], refs[2 * pieces + 1]
    me = lax.axis_index("tm")
    rate = rate_ref[row_part(0, pieces, rate_ref.shape[0]), :]
    factor = rate
    for _ in range(slices - 1):
        factor = factor * rate
    for step in range(pieces):
        held[me ^ step] = got[step][...]
    entering = periodic([held[k] for k in range(pieces)], factor)
    for k in range(pieces):
        held[k] = entering[k]
    for step in range(pieces):
        sent[step][...] = held[me ^ step]


def solve_kernel(pieces, *refs):
    piece_refs = refs[:pieces]
    right_ref, rate_ref, state_ref, before_ref, near_ref, far_ref = refs[pieces:]
    slices, rows, columns = right_ref.shape
    if pieces == 1:
        before_ref[...] = piece_refs[0][...]
    else:
        for step in range(pieces):
            before_ref[row_part(step, pieces, rows), :] = piece_refs[step][...]
    rate = rate_ref[...]
    value = before_ref[...]
    low = []
    high = []
    for item in range(slices):
        value = rate * (value + right_ref[item])
        state_ref[item] = value
        cube = value.reshape(NF, NP**3, columns)
        low.append(cube[:, 0:16, 0:LANES].reshape(FACE, LANES))
        high.append(cube[:, 48:64, columns - LANES :].reshape(FACE, LANES))
    send(low, high, near_ref, far_ref)


def second_kernel(
    state_ref, before_ref, forcing_ref, weights_ref, neighbor_ref, tags_ref, codes_ref, out_ref,
    result_ref, blocks, stack, semaphore,
):
    slices, _, columns = state_ref.shape
    copy = pltpu.make_async_copy(state_ref, result_ref, semaphore)
    copy.start()
    image = operator(
        state_ref, blocks, stack, weights_ref, neighbor_ref, tags_ref, codes_ref
    )
    for item in range(slices):
        previous = before_ref[...] if item == 0 else state_ref[item - 1]
        out_ref[item] = (
            image[:, item * columns : (item + 1) * columns]
            + forcing_ref[item]
            + (previous - state_ref[item])
        )
    copy.wait()


def finish_kernel(
    part_ref, near_ref, far_ref, rim_weights_ref, neighbor_ref, tags_ref, codes_ref, out_ref
):
    slices, _, columns = part_ref.shape
    count = columns // LANES
    low, high = rim(
        near_ref, far_ref, slices, rim_weights_ref, neighbor_ref, tags_ref, codes_ref, count
    )
    for block in range(count):
        span = slice(block * LANES, (block + 1) * LANES)
        for item in range(slices):
            value = part_ref[item, :, span]
            piece = slice(item * LANES, (item + 1) * LANES)
            if block == 0:
                value = value + low[:, piece]
            if block == count - 1:
                value = value + high[:, piece]
            out_ref[item, :, span] = value.astype(out_ref.dtype)


VMEM = pl.BlockSpec(memory_space=pltpu.VMEM)
HBM = pl.BlockSpec(memory_space=pltpu.HBM)


def call(kernel, name, outs, args, scratch=(), flops=0, in_specs=None, out_specs=None):
    size = sum(math.prod(a.shape) * a.dtype.itemsize for a in list(args) + list(outs))
    return pl.pallas_call(
        kernel,
        name=name,
        out_shape=outs,
        in_specs=in_specs or [VMEM] * len(args),
        out_specs=out_specs or [VMEM] * len(outs),
        scratch_shapes=list(scratch),
        compiler_params=pltpu.CompilerParams(vmem_limit_bytes=40 * 2**20),
        cost_estimate=pl.CostEstimate(flops=flops, bytes_accessed=size, transcendentals=0),
    )(*args)


def exchange(near, far):
    count = lax.axis_size("space")
    inner = [(i, i + 1) for i in range(0, count - 1, 2)]
    outer = [(i, i + 1) for i in range(1, count - 1, 2)]
    near = lax.ppermute(near, "space", inner + [(j, i) for i, j in inner])
    far = lax.ppermute(far, "space", outer + [(j, i) for i, j in outer])
    return near, far


def swapped(value, step):
    count = lax.axis_size("tm")
    return lax.ppermute(value, "tm", [(i, i ^ step) for i in range(count)])


def in_hbm(value):
    return pltpu.with_memory_space_constraint(value, pltpu.HBM)


def local(guess, source_cos, source_sin, damping, volume, lifts, neighbor, tags, codes):
    slices, rows, columns = guess.shape
    devices = lax.axis_size("tm")
    f32, bf16 = jnp.float32, jnp.bfloat16
    shape = jax.ShapeDtypeStruct
    whole = shape((slices, rows, columns), f32)
    plane = shape((rows, columns), f32)
    packed = shape(((slices + 1) // 2, FACE, LANES), f32)
    depth = rows + 6 * FACE
    scratch = [
        pltpu.VMEM((slices * columns // LANES, rows, LANES), f32),
        pltpu.VMEM((depth, 2 * slices * columns), bf16),
    ]
    work = 4 * rows * depth * slices * columns
    end = pltpu.VMEM((slices, NF, NP * NP, LANES), f32)
    share = rows // devices
    pairs = devices & (devices - 1) == 0 and devices <= 8 and share % 8 == 0
    pieces = devices if pairs else 1
    piece = shape((rows // pieces, columns), f32)

    near, far = call(
        ends_kernel, "ends", [packed] * 2,
        [in_hbm(guess.reshape(slices, NF, NP**3, columns))],
        [end, end, pltpu.SemaphoreType.DMA((2,))], in_specs=[HBM],
    )
    near, far = exchange(near, far)
    operands = (
        guess, neighbor, tags, codes, jnp.swapaxes(lifts, 1, 2), volume, damping, source_cos,
        source_sin,
    )
    part, weights, rim_weights, rate, forcing, *tables = call(
        functools.partial(first_kernel, slices * devices), "first",
        [whole, shape((rows, depth), bf16), shape((2, rows, FACE), bf16), plane, whole]
        + [shape(neighbor.shape, jnp.int32)] * 3,
        [in_hbm(operand) for operand in operands],
        [
            pltpu.VMEM(whole.shape, f32),
            pltpu.VMEM(plane.shape, bf16),
            pltpu.VMEM(plane.shape, bf16),
            pltpu.VMEM(plane.shape, f32),
            pltpu.VMEM(volume.shape, bf16),
            pltpu.VMEM((6, FACE, rows), bf16),
            *scratch,
            pltpu.SemaphoreType.DMA((len(operands),)),
        ],
        flops=work, in_specs=[HBM] * len(operands),
    )
    known, *parts = call(
        functools.partial(carry_kernel, pieces), "carry", [whole] + [piece] * pieces,
        [part, near, far, rate, rim_weights, *tables], [pltpu.VMEM(plane.shape, f32)],
    )
    if pairs:
        parts = parts[:1] + [swapped(parts[step], step) for step in range(1, pieces)]
        parts = call(
            functools.partial(around_kernel, slices, pieces), "around", [piece] * pieces,
            [*parts, rate], [pltpu.VMEM((pieces, *piece.shape), f32)],
        )
        parts = list(parts[:1]) + [swapped(parts[step], step) for step in range(1, pieces)]
    else:
        me = lax.axis_index("tm")
        factor = lax.dynamic_slice_in_dim(rate, me * share, share, 0) ** slices
        carries = lax.all_to_all(parts[0], "tm", split_axis=0, concat_axis=0, tiled=True)
        carries = carries.reshape(devices, share, columns)
        back = jnp.concatenate(periodic([carries[k] for k in range(devices)], factor), axis=0)
        parts = [lax.all_to_all(back, "tm", split_axis=0, concat_axis=0, tiled=True)]
    state, before, near, far = call(
        functools.partial(solve_kernel, pieces), "solve",
        [whole, plane, packed, packed], [*parts, known, rate],
    )
    near, far = exchange(near, far)
    part, result = call(
        second_kernel, "second", [whole, whole],
        [state, before, forcing, weights, *tables],
        [*scratch, pltpu.SemaphoreType.DMA], flops=work, out_specs=[VMEM, HBM],
    )
    (after,) = call(
        finish_kernel, "finish", [shape(whole.shape, bf16)],
        [part, near, far, rim_weights, *tables],
    )
    return result, after


def solution(mesh):
    column = P(None, ("groups", "space"))
    state = P("tm", None, ("groups", "space"))
    in_specs = (state, column, column, column, P(), P(), column, column, column)
    return jax.shard_map(
        local, mesh=mesh, in_specs=in_specs, out_specs=(state, state), check_vma=False
    )
```

```python
import functools
import math

import jax
import jax.numpy as jnp
from jax import lax
from jax.experimental import pallas as pl
from jax.experimental.pallas import tpu as pltpu
from jax.sharding import PartitionSpec as P

NF = 5
NP = 4
FACE = NF * NP * NP
LANES = 128
HALF = 64


def split(value):
    high = value.astype(jnp.bfloat16)
    low = (value - high.astype(jnp.float32)).astype(jnp.bfloat16)
    return high, low


def end_trace(cube, face):
    rows = cube[:, 0:16] if face == 0 else cube[:, 48:64]
    return rows.reshape(FACE, LANES)


def side_trace(cube, face):
    tiles = cube.reshape(NF, 2, 2, 16, LANES)
    part = tiles[:, :, :, 0:8] if face == 2 else tiles[:, :, :, 8:16]
    even = part[:, :, 0].reshape(FACE // 8, 8, LANES)
    odd = part[:, :, 1].reshape(FACE // 8, 8, LANES)
    lower = lax.broadcasted_iota(jnp.int32, (FACE // 8, 8, LANES), 1) < 4
    if face == 2:
        odd = pltpu.roll(odd, 4, axis=1)
    else:
        even = pltpu.roll(even, 4, axis=1)
    return jnp.where(lower, even, odd).reshape(FACE, LANES)


def lane_index(row):
    return jnp.broadcast_to(row, (FACE, LANES))


def orientation(code):
    swap = (code & 1) == 1
    turn_i = (code & 2) == 2
    turn_j = (code & 4) == 4
    result = []
    for tile in range(2):
        row = lax.broadcasted_iota(jnp.int32, (8, LANES), 0) + 8 * tile
        i, j = row >> 2, row & 3
        i = jnp.where(turn_i, 3 - i, i)
        j = jnp.where(turn_j, 3 - j, j)
        source = jnp.where(swap, j * 4 + i, i * 4 + j)
        result.append((source >= 8, source & 7))
    return result


def oriented(value, plan):
    pieces = []
    for field in range(NF):
        first = value[field * 16 : field * 16 + 8]
        second = value[field * 16 + 8 : field * 16 + 16]
        for upper, sub in plan:
            pick = functools.partial(jnp.take_along_axis, axis=0, mode="promise_in_bounds")
            pieces.append(jnp.where(upper, pick(second, sub), pick(first, sub)))
    return jnp.concatenate(pieces, axis=0)


def gather_lanes(value, row):
    return jnp.take_along_axis(value, lane_index(row), axis=1, mode="promise_in_bounds")


def operator(
    state, blocks, stack, weights_ref, neighbor_ref, tags_ref, codes_ref, ahead=lambda: None
):
    slices, rows, columns = state.shape
    count = columns // LANES
    wide = slices * columns
    base = 6 * FACE
    lane = lax.broadcasted_iota(jnp.int32, (FACE, LANES), 1)
    for item in range(slices):
        for block in range(count):
            n = item * count + block
            value = state[item, :, block * LANES : (block + 1) * LANES]
            blocks[n] = value
            high, low = split(value)
            stack[base:, n * LANES : (n + 1) * LANES] = high
            stack[base:, wide + n * LANES : wide + (n + 1) * LANES] = low
    for item in range(slices):
        cubes = []
        turned = []
        for block in range(count):
            cube = blocks[item * count + block].reshape(NF, NP**3, LANES)
            cubes.append(cube)
            turned.append(
                [pltpu.roll(end_trace(cube, face), HALF, axis=1) for face in range(2)]
            )
        zero = jnp.zeros((FACE, LANES), jnp.float32)
        for block in range(count):
            n = item * count + block
            cube = cubes[block]
            before = turned[block - 1][1] if block > 0 else zero
            after = turned[block + 1][0] if block + 1 < count else zero
            ends = [end_trace(cube, 0), end_trace(cube, 1)]
            sides = [side_trace(cube, 2), side_trace(cube, 3)]
            tops = [
                blocks[n, pl.ds(0, FACE, stride=4), :],
                blocks[n, pl.ds(3, FACE, stride=4), :],
            ]
            mine = ends + sides + tops
            across = [
                jnp.where(lane < HALF, before, turned[block][1]),
                jnp.where(lane < HALF, turned[block][0], after),
                sides[1],
                sides[0],
                tops[1],
                tops[0],
            ]
            for face in range(6):
                span = slice(block * LANES, (block + 1) * LANES)
                target = neighbor_ref[face : face + 1, span]
                kind = tags_ref[face : face + 1, span]
                code = codes_ref[face : face + 1, span]
                if face < 2:
                    target = target + HALF
                plan = orientation(code)
                taken = oriented(gather_lanes(across[face], target & (LANES - 1)), plan)
                keep = jnp.where((kind == 1) | (kind == 3), 1.0, 0.0)
                flip = jnp.where(kind == 1, -1.0, keep)
                axis = 1 + face // 2
                inner = []
                for field in range(NF):
                    own = mine[face][field * 16 : (field + 1) * 16]
                    inner.append(own * (flip if field == axis else keep))
                seen = jnp.where(kind == 0, taken, jnp.concatenate(inner, axis=0))
                high, low = split(seen)
                place = FACE * face
                stack[place : place + FACE, n * LANES : (n + 1) * LANES] = high
                stack[place : place + FACE, wide + n * LANES : wide + (n + 1) * LANES] = low
    ahead()
    image = jnp.dot(weights_ref[...], stack[:, 0:wide], preferred_element_type=jnp.float32)
    return image + jnp.dot(
        weights_ref[...], stack[:, wide:], preferred_element_type=jnp.float32
    )


def even_place():
    return (lax.axis_index("space") & 1) == 0


def rim(near, far, slices, rim_weights_ref, neighbor_ref, tags_ref, codes_ref, count):
    lane = lax.broadcasted_iota(jnp.int32, (1, LANES), 1)
    even = even_place()
    result = []
    for face in range(2):
        block = 0 if face == 0 else count - 1
        span = slice(block * LANES, (block + 1) * LANES)
        target = neighbor_ref[face : face + 1, span] & (HALF - 1)
        inside = lane < HALF if face == 0 else lane >= HALF
        use = (tags_ref[face : face + 1, span] == 0) & inside
        plan = orientation(codes_ref[face : face + 1, span])
        pieces = []
        for item in range(slices):
            a, b = (far, near) if face == 0 else (near, far)
            halo = jnp.where(even, a[item // 2], b[item // 2])
            taken = gather_lanes(halo, target + HALF * (item % 2))
            pieces.append(split(jnp.where(use, oriented(taken, plan), 0.0)))
        both = jnp.concatenate([p[0] for p in pieces] + [p[1] for p in pieces], axis=1)
        product = jnp.dot(rim_weights_ref[face], both, preferred_element_type=jnp.float32)
        wide = slices * LANES
        result.append(product[:, :wide] + product[:, wide:])
    return result


def send(low, high, near_ref, far_ref):
    slices = len(low)
    lane = lax.broadcasted_iota(jnp.int32, (FACE, LANES), 1)
    even = even_place()
    for item in range(0, slices, 2):
        other = min(item + 1, slices - 1)
        first = jnp.where(lane < HALF, low[item], pltpu.roll(low[other], HALF, axis=1))
        last = jnp.where(lane < HALF, pltpu.roll(high[item], HALF, axis=1), high[other])
        near_ref[item // 2] = jnp.where(even, last, first)
        far_ref[item // 2] = jnp.where(even, first, last)


def ends_kernel(state_ref, near_ref, far_ref, low, high, semaphore):
    slices, _, _, columns = state_ref.shape
    copies = [
        pltpu.make_async_copy(
            state_ref.at[:, :, pl.ds(0, 16), pl.ds(0, LANES)], low, semaphore.at[0]
        ),
        pltpu.make_async_copy(
            state_ref.at[:, :, pl.ds(48, 16), pl.ds(columns - LANES, LANES)], high, semaphore.at[1]
        ),
    ]
    for copy in copies:
        copy.start()
    for copy in copies:
        copy.wait()
    send(
        [low[item].reshape(FACE, LANES) for item in range(slices)],
        [high[item].reshape(FACE, LANES) for item in range(slices)],
        near_ref,
        far_ref,
    )


def wave(at, values):
    result = jnp.float32(values[0])
    for k in range(1, len(values)):
        result = jnp.where(at == k, jnp.float32(values[k]), result)
    return result


def first_kernel(total, *refs):
    sources = refs[:9]
    out_ref, weights_ref, rim_weights_ref, rate_ref, forcing_ref = refs[9:14]
    neighbor_ref, tags_ref, codes_ref = refs[14:17]
    state_ref, cos_ref, sin_ref, damping_ref, volume_ref, lifts_ref = refs[17:23]
    blocks, stack, semaphores = refs[23:]
    targets = (
        state_ref, neighbor_ref, tags_ref, codes_ref, lifts_ref, volume_ref, damping_ref,
        cos_ref, sin_ref,
    )
    copies = [
        pltpu.make_async_copy(source, target, semaphores.at[k])
        for k, (source, target) in enumerate(zip(sources, targets))
    ]
    for copy in copies:
        copy.start()
    for copy in copies[:4]:
        copy.wait()
    slices, _, columns = state_ref.shape

    def ahead():
        for copy in copies[4:]:
            copy.wait()
        for face in range(6):
            lift = lifts_ref[face].T
            weights_ref[:, FACE * face : FACE * (face + 1)] = lift
            if face < 2:
                rim_weights_ref[face] = lift
        weights_ref[:, 6 * FACE :] = volume_ref[...]

    image = operator(
        state_ref, blocks, stack, weights_ref, neighbor_ref, tags_ref, codes_ref, ahead
    )
    rate_ref[...] = 1.0 / (1.0 + damping_ref[...])
    angles = [2.0 * math.pi * k / total for k in range(total)]
    for item in range(slices):
        at = lax.axis_index("tm") * slices + item
        forcing = wave(at, [math.cos(x) for x in angles]) * cos_ref[...].astype(jnp.float32)
        forcing += wave(at, [math.sin(x) for x in angles]) * sin_ref[...].astype(jnp.float32)
        forcing_ref[item] = forcing
        out_ref[item] = (
            image[:, item * columns : (item + 1) * columns]
            + forcing
            + damping_ref[...] * state_ref[item]
        )


def carry_kernel(
    pieces, part_ref, near_ref, far_ref, rate_ref, rim_weights_ref, neighbor_ref, tags_ref,
    codes_ref, out_ref, *refs
):
    *piece_refs, carry_ref = refs
    slices, rows, columns = part_ref.shape
    count = columns // LANES
    low, high = rim(
        near_ref, far_ref, slices, rim_weights_ref, neighbor_ref, tags_ref, codes_ref, count
    )
    for block in range(count):
        span = slice(block * LANES, (block + 1) * LANES)
        rate = rate_ref[:, span]
        carry = None
        for item in range(slices):
            value = part_ref[item, :, span]
            piece = slice(item * LANES, (item + 1) * LANES)
            if block == 0:
                value = value + low[:, piece]
            if block == count - 1:
                value = value + high[:, piece]
            out_ref[item, :, span] = value
            carry = rate * value if carry is None else rate * (carry + value)
        carry_ref[:, span] = carry
    if pieces == 1:
        piece_refs[0][...] = carry_ref[...]
    else:
        for step in range(pieces):
            piece_refs[step][...] = carry_ref[row_part(step, pieces, rows), :]


def row_part(step, pieces, rows):
    share = rows // pieces
    return pl.ds(pl.multiple_of((lax.axis_index("tm") ^ step) * share, 8), share)


def periodic(carries, factor):
    count = len(carries)
    total = carries[0]
    for k in range(1, count):
        total = carries[k] + factor * total
    power = factor
    for _ in range(count - 1):
        power = power * factor
    entering = [total / (1.0 - power)]
    for k in range(count - 1):
        entering.append(carries[k] + factor * entering[-1])
    return entering


def around_kernel(slices, pieces, *refs):
    got, rate_ref = refs[:pieces], refs[pieces]
    sent, held = refs[pieces + 1 : 2 * pieces + 1], refs[2 * pieces + 1]
    me = lax.axis_index("tm")
    rate = rate_ref[row_part(0, pieces, rate_ref.shape[0]), :]
    factor = rate
    for _ in range(slices - 1):
        factor = factor * rate
    for step in range(pieces):
        held[me ^ step] = got[step][...]
    entering = periodic([held[k] for k in range(pieces)], factor)
    for k in range(pieces):
        held[k] = entering[k]
    for step in range(pieces):
        sent[step][...] = held[me ^ step]


def solve_kernel(pieces, *refs):
    piece_refs = refs[:pieces]
    right_ref, rate_ref, state_ref, before_ref, near_ref, far_ref = refs[pieces:]
    slices, rows, columns = right_ref.shape
    if pieces == 1:
        before_ref[...] = piece_refs[0][...]
    else:
        for step in range(pieces):
            before_ref[row_part(step, pieces, rows), :] = piece_refs[step][...]
    rate = rate_ref[...]
    value = before_ref[...]
    low = []
    high = []
    for item in range(slices):
        value = rate * (value + right_ref[item])
        state_ref[item] = value
        cube = value.reshape(NF, NP**3, columns)
        low.append(cube[:, 0:16, 0:LANES].reshape(FACE, LANES))
        high.append(cube[:, 48:64, columns - LANES :].reshape(FACE, LANES))
    send(low, high, near_ref, far_ref)


def second_kernel(
    state_ref, before_ref, forcing_ref, weights_ref, neighbor_ref, tags_ref, codes_ref, out_ref,
    result_ref, blocks, stack, semaphore,
):
    slices, _, columns = state_ref.shape
    copy = pltpu.make_async_copy(state_ref, result_ref, semaphore)
    copy.start()
    image = operator(
        state_ref, blocks, stack, weights_ref, neighbor_ref, tags_ref, codes_ref
    )
    for item in range(slices):
        previous = before_ref[...] if item == 0 else state_ref[item - 1]
        out_ref[item] = (
            image[:, item * columns : (item + 1) * columns]
            + forcing_ref[item]
            + (previous - state_ref[item])
        )
    copy.wait()


def finish_kernel(
    part_ref, near_ref, far_ref, rim_weights_ref, neighbor_ref, tags_ref, codes_ref, out_ref,
    held, semaphores,
):
    slices, _, columns = part_ref.shape
    count = columns // LANES
    low, high = rim(
        near_ref, far_ref, slices, rim_weights_ref, neighbor_ref, tags_ref, codes_ref, count
    )
    copies = []
    for block in range(count):
        span = pl.ds(block * LANES, LANES)
        for item in range(slices):
            value = part_ref[item, :, span]
            piece = slice(item * LANES, (item + 1) * LANES)
            if block == 0:
                value = value + low[:, piece]
            if block == count - 1:
                value = value + high[:, piece]
            held[item, :, span] = value.astype(held.dtype)
        copy = pltpu.make_async_copy(
            held.at[:, :, span], out_ref.at[:, :, span], semaphores.at[block]
        )
        copy.start()
        copies.append(copy)
    for copy in copies:
        copy.wait()


VMEM = pl.BlockSpec(memory_space=pltpu.VMEM)
HBM = pl.BlockSpec(memory_space=pltpu.HBM)


def call(kernel, name, outs, args, scratch=(), flops=0, in_specs=None, out_specs=None):
    size = sum(math.prod(a.shape) * a.dtype.itemsize for a in list(args) + list(outs))
    return pl.pallas_call(
        kernel,
        name=name,
        out_shape=outs,
        in_specs=in_specs or [VMEM] * len(args),
        out_specs=out_specs or [VMEM] * len(outs),
        scratch_shapes=list(scratch),
        compiler_params=pltpu.CompilerParams(vmem_limit_bytes=40 * 2**20),
        cost_estimate=pl.CostEstimate(flops=flops, bytes_accessed=size, transcendentals=0),
    )(*args)


def exchange(near, far):
    count = lax.axis_size("space")
    inner = [(i, i + 1) for i in range(0, count - 1, 2)]
    outer = [(i, (i + 1) % count) for i in range(1, count, 2)]
    near = lax.ppermute(near, "space", inner + [(j, i) for i, j in inner])
    far = lax.ppermute(far, "space", outer + [(j, i) for i, j in outer])
    return near, far


def swapped(value, step):
    count = lax.axis_size("tm")
    return lax.ppermute(value, "tm", [(i, i ^ step) for i in range(count)])


def in_hbm(value):
    return pltpu.with_memory_space_constraint(value, pltpu.HBM)


def local(guess, source_cos, source_sin, damping, volume, lifts, neighbor, tags, codes):
    slices, rows, columns = guess.shape
    devices = lax.axis_size("tm")
    f32, bf16 = jnp.float32, jnp.bfloat16
    shape = jax.ShapeDtypeStruct
    whole = shape((slices, rows, columns), f32)
    plane = shape((rows, columns), f32)
    packed = shape(((slices + 1) // 2, FACE, LANES), f32)
    depth = rows + 6 * FACE
    scratch = [
        pltpu.VMEM((slices * columns // LANES, rows, LANES), f32),
        pltpu.VMEM((depth, 2 * slices * columns), bf16),
    ]
    work = 4 * rows * depth * slices * columns
    end = pltpu.VMEM((slices, NF, NP * NP, LANES), f32)
    share = rows // devices
    pairs = devices & (devices - 1) == 0 and devices <= 8 and share % 8 == 0
    pieces = devices if pairs else 1
    piece = shape((rows // pieces, columns), f32)

    near, far = call(
        ends_kernel, "ends", [packed] * 2,
        [in_hbm(guess.reshape(slices, NF, NP**3, columns))],
        [end, end, pltpu.SemaphoreType.DMA((2,))], in_specs=[HBM],
    )
    near, far = exchange(near, far)
    operands = (
        guess, neighbor, tags, codes, jnp.swapaxes(lifts, 1, 2), volume, damping, source_cos,
        source_sin,
    )
    part, weights, rim_weights, rate, forcing, *tables = call(
        functools.partial(first_kernel, slices * devices), "first",
        [whole, shape((rows, depth), bf16), shape((2, rows, FACE), bf16), plane, whole]
        + [shape(neighbor.shape, jnp.int32)] * 3,
        [in_hbm(operand) for operand in operands],
        [
            pltpu.VMEM(whole.shape, f32),
            pltpu.VMEM(plane.shape, bf16),
            pltpu.VMEM(plane.shape, bf16),
            pltpu.VMEM(plane.shape, f32),
            pltpu.VMEM(volume.shape, bf16),
            pltpu.VMEM((6, FACE, rows), bf16),
            *scratch,
            pltpu.SemaphoreType.DMA((len(operands),)),
        ],
        flops=work, in_specs=[HBM] * len(operands),
    )
    known, *parts = call(
        functools.partial(carry_kernel, pieces), "carry", [whole] + [piece] * pieces,
        [part, near, far, rate, rim_weights, *tables], [pltpu.VMEM(plane.shape, f32)],
    )
    if pairs:
        parts = parts[:1] + [swapped(parts[step], step) for step in range(1, pieces)]
        parts = call(
            functools.partial(around_kernel, slices, pieces), "around", [piece] * pieces,
            [*parts, rate], [pltpu.VMEM((pieces, *piece.shape), f32)],
        )
        parts = list(parts[:1]) + [swapped(parts[step], step) for step in range(1, pieces)]
    else:
        me = lax.axis_index("tm")
        factor = lax.dynamic_slice_in_dim(rate, me * share, share, 0) ** slices
        carries = lax.all_to_all(parts[0], "tm", split_axis=0, concat_axis=0, tiled=True)
        carries = carries.reshape(devices, share, columns)
        back = jnp.concatenate(periodic([carries[k] for k in range(devices)], factor), axis=0)
        parts = [lax.all_to_all(back, "tm", split_axis=0, concat_axis=0, tiled=True)]
    state, before, near, far = call(
        functools.partial(solve_kernel, pieces), "solve",
        [whole, plane, packed, packed], [*parts, known, rate],
    )
    near, far = exchange(near, far)
    part, result = call(
        second_kernel, "second", [whole, whole],
        [state, before, forcing, weights, *tables],
        [*scratch, pltpu.SemaphoreType.DMA], flops=work, out_specs=[VMEM, HBM],
    )
    (after,) = call(
        finish_kernel, "finish", [shape(whole.shape, bf16)],
        [part, near, far, rim_weights, *tables],
        [pltpu.VMEM(whole.shape, bf16), pltpu.SemaphoreType.DMA((columns // LANES,))],
        out_specs=[HBM],
    )
    return result, after


def solution(mesh):
    column = P(None, ("groups", "space"))
    state = P("tm", None, ("groups", "space"))
    in_specs = (state, column, column, column, P(), P(), column, column, column)
    return jax.shard_map(
        local, mesh=mesh, in_specs=in_specs, out_specs=(state, state), check_vma=False
    )
```

```python
import functools
import math

import jax
import jax.numpy as jnp
from jax import lax
from jax.experimental import pallas as pl
from jax.experimental.pallas import tpu as pltpu
from jax.sharding import PartitionSpec as P

NF = 5
NP = 4
FACE = NF * NP * NP
LANES = 128
HALF = 64


def split(value):
    high = value.astype(jnp.bfloat16)
    low = (value - high.astype(jnp.float32)).astype(jnp.bfloat16)
    return high, low


def end_trace(cube, face):
    rows = cube[:, 0:16] if face == 0 else cube[:, 48:64]
    return rows.reshape(FACE, LANES)


def side_trace(cube, face):
    tiles = cube.reshape(NF, 2, 2, 16, LANES)
    part = tiles[:, :, :, 0:8] if face == 2 else tiles[:, :, :, 8:16]
    even = part[:, :, 0].reshape(FACE // 8, 8, LANES)
    odd = part[:, :, 1].reshape(FACE // 8, 8, LANES)
    lower = lax.broadcasted_iota(jnp.int32, (FACE // 8, 8, LANES), 1) < 4
    if face == 2:
        odd = pltpu.roll(odd, 4, axis=1)
    else:
        even = pltpu.roll(even, 4, axis=1)
    return jnp.where(lower, even, odd).reshape(FACE, LANES)


def lane_index(row):
    return jnp.broadcast_to(row, (FACE, LANES))


def orientation(code):
    swap = (code & 1) == 1
    turn_i = (code & 2) == 2
    turn_j = (code & 4) == 4
    result = []
    for tile in range(2):
        row = lax.broadcasted_iota(jnp.int32, (8, LANES), 0) + 8 * tile
        i, j = row >> 2, row & 3
        i = jnp.where(turn_i, 3 - i, i)
        j = jnp.where(turn_j, 3 - j, j)
        source = jnp.where(swap, j * 4 + i, i * 4 + j)
        result.append((source >= 8, source & 7))
    return result


def oriented(value, plan):
    pieces = []
    for field in range(NF):
        first = value[field * 16 : field * 16 + 8]
        second = value[field * 16 + 8 : field * 16 + 16]
        for upper, sub in plan:
            pick = functools.partial(jnp.take_along_axis, axis=0, mode="promise_in_bounds")
            pieces.append(jnp.where(upper, pick(second, sub), pick(first, sub)))
    return jnp.concatenate(pieces, axis=0)


def gather_lanes(value, row):
    return jnp.take_along_axis(value, lane_index(row), axis=1, mode="promise_in_bounds")


def operator(
    state, blocks, stack, weights_ref, neighbor_ref, tags_ref, codes_ref, ahead=lambda: None
):
    slices, rows, columns = state.shape
    count = columns // LANES
    wide = slices * columns
    base = 6 * FACE
    lane = lax.broadcasted_iota(jnp.int32, (FACE, LANES), 1)
    for item in range(slices):
        for block in range(count):
            n = item * count + block
            value = state[item, :, block * LANES : (block + 1) * LANES]
            blocks[n] = value
            high, low = split(value)
            stack[base:, n * LANES : (n + 1) * LANES] = high
            stack[base:, wide + n * LANES : wide + (n + 1) * LANES] = low
    for item in range(slices):
        cubes = []
        turned = []
        for block in range(count):
            cube = blocks[item * count + block].reshape(NF, NP**3, LANES)
            cubes.append(cube)
            turned.append(
                [pltpu.roll(end_trace(cube, face), HALF, axis=1) for face in range(2)]
            )
        zero = jnp.zeros((FACE, LANES), jnp.float32)
        for block in range(count):
            n = item * count + block
            cube = cubes[block]
            before = turned[block - 1][1] if block > 0 else zero
            after = turned[block + 1][0] if block + 1 < count else zero
            ends = [end_trace(cube, 0), end_trace(cube, 1)]
            sides = [side_trace(cube, 2), side_trace(cube, 3)]
            tops = [
                blocks[n, pl.ds(0, FACE, stride=4), :],
                blocks[n, pl.ds(3, FACE, stride=4), :],
            ]
            mine = ends + sides + tops
            across = [
                jnp.where(lane < HALF, before, turned[block][1]),
                jnp.where(lane < HALF, turned[block][0], after),
                sides[1],
                sides[0],
                tops[1],
                tops[0],
            ]
            for face in range(6):
                span = slice(block * LANES, (block + 1) * LANES)
                target = neighbor_ref[face : face + 1, span]
                kind = tags_ref[face : face + 1, span]
                code = codes_ref[face : face + 1, span]
                if face < 2:
                    target = target + HALF
                plan = orientation(code)
                taken = oriented(gather_lanes(across[face], target & (LANES - 1)), plan)
                keep = jnp.where((kind == 1) | (kind == 3), 1.0, 0.0)
                flip = jnp.where(kind == 1, -1.0, keep)
                axis = 1 + face // 2
                inner = []
                for field in range(NF):
                    own = mine[face][field * 16 : (field + 1) * 16]
                    inner.append(own * (flip if field == axis else keep))
                seen = jnp.where(kind == 0, taken, jnp.concatenate(inner, axis=0))
                high, low = split(seen)
                place = FACE * face
                stack[place : place + FACE, n * LANES : (n + 1) * LANES] = high
                stack[place : place + FACE, wide + n * LANES : wide + (n + 1) * LANES] = low
    ahead()
    image = jnp.dot(weights_ref[...], stack[:, 0:wide], preferred_element_type=jnp.float32)
    return image + jnp.dot(
        weights_ref[...], stack[:, wide:], preferred_element_type=jnp.float32
    )


def even_place():
    return (lax.axis_index("space") & 1) == 0


def rim(near, far, slices, rim_weights_ref, neighbor_ref, tags_ref, codes_ref, count):
    lane = lax.broadcasted_iota(jnp.int32, (1, LANES), 1)
    even = even_place()
    result = []
    for face in range(2):
        block = 0 if face == 0 else count - 1
        span = slice(block * LANES, (block + 1) * LANES)
        target = neighbor_ref[face : face + 1, span] & (HALF - 1)
        inside = lane < HALF if face == 0 else lane >= HALF
        use = (tags_ref[face : face + 1, span] == 0) & inside
        plan = orientation(codes_ref[face : face + 1, span])
        pieces = []
        for item in range(slices):
            a, b = (far, near) if face == 0 else (near, far)
            halo = jnp.where(even, a[item // 2], b[item // 2])
            taken = gather_lanes(halo, target + HALF * (item % 2))
            pieces.append(split(jnp.where(use, oriented(taken, plan), 0.0)))
        both = jnp.concatenate([p[0] for p in pieces] + [p[1] for p in pieces], axis=1)
        product = jnp.dot(rim_weights_ref[face], both, preferred_element_type=jnp.float32)
        wide = slices * LANES
        result.append(product[:, :wide] + product[:, wide:])
    return result


def send(low, high, near_ref, far_ref):
    slices = len(low)
    lane = lax.broadcasted_iota(jnp.int32, (FACE, LANES), 1)
    even = even_place()
    for item in range(0, slices, 2):
        other = min(item + 1, slices - 1)
        first = jnp.where(lane < HALF, low[item], pltpu.roll(low[other], HALF, axis=1))
        last = jnp.where(lane < HALF, pltpu.roll(high[item], HALF, axis=1), high[other])
        near_ref[item // 2] = jnp.where(even, last, first)
        far_ref[item // 2] = jnp.where(even, first, last)


def ends_kernel(state_ref, near_ref, far_ref, low, high, semaphore):
    slices, _, _, columns = state_ref.shape
    copies = [
        pltpu.make_async_copy(
            state_ref.at[:, :, pl.ds(0, 16), pl.ds(0, LANES)], low, semaphore.at[0]
        ),
        pltpu.make_async_copy(
            state_ref.at[:, :, pl.ds(48, 16), pl.ds(columns - LANES, LANES)], high, semaphore.at[1]
        ),
    ]
    for copy in copies:
        copy.start()
    for copy in copies:
        copy.wait()
    send(
        [low[item].reshape(FACE, LANES) for item in range(slices)],
        [high[item].reshape(FACE, LANES) for item in range(slices)],
        near_ref,
        far_ref,
    )


def wave(at, values):
    result = jnp.float32(values[0])
    for k in range(1, len(values)):
        result = jnp.where(at == k, jnp.float32(values[k]), result)
    return result


def first_kernel(total, *refs):
    sources = refs[:9]
    out_ref, weights_ref, rim_weights_ref, rate_ref, forcing_ref = refs[9:14]
    neighbor_ref, tags_ref, codes_ref = refs[14:17]
    state_ref, cos_ref, sin_ref, damping_ref, volume_ref, lifts_ref = refs[17:23]
    blocks, stack, semaphores = refs[23:]
    targets = (
        state_ref, neighbor_ref, tags_ref, codes_ref, lifts_ref, volume_ref, damping_ref,
        cos_ref, sin_ref,
    )
    copies = [
        pltpu.make_async_copy(source, target, semaphores.at[k])
        for k, (source, target) in enumerate(zip(sources, targets))
    ]
    for copy in copies:
        copy.start()
    for copy in copies[:4]:
        copy.wait()
    slices, _, columns = state_ref.shape

    def ahead():
        for copy in copies[4:]:
            copy.wait()
        for face in range(6):
            lift = lifts_ref[face].T
            weights_ref[:, FACE * face : FACE * (face + 1)] = lift
            if face < 2:
                rim_weights_ref[face] = lift
        weights_ref[:, 6 * FACE :] = volume_ref[...]

    image = operator(
        state_ref, blocks, stack, weights_ref, neighbor_ref, tags_ref, codes_ref, ahead
    )
    rate_ref[...] = 1.0 / (1.0 + damping_ref[...])
    angles = [2.0 * math.pi * k / total for k in range(total)]
    for item in range(slices):
        at = lax.axis_index("tm") * slices + item
        forcing = wave(at, [math.cos(x) for x in angles]) * cos_ref[...].astype(jnp.float32)
        forcing += wave(at, [math.sin(x) for x in angles]) * sin_ref[...].astype(jnp.float32)
        forcing_ref[item] = forcing
        out_ref[item] = (
            image[:, item * columns : (item + 1) * columns]
            + forcing
            + damping_ref[...] * state_ref[item]
        )


def carry_kernel(
    pieces, part_ref, near_ref, far_ref, rate_ref, rim_weights_ref, neighbor_ref, tags_ref,
    codes_ref, out_ref, *refs
):
    *piece_refs, carry_ref = refs
    slices, rows, columns = part_ref.shape
    count = columns // LANES
    low, high = rim(
        near_ref, far_ref, slices, rim_weights_ref, neighbor_ref, tags_ref, codes_ref, count
    )
    for block in range(count):
        span = slice(block * LANES, (block + 1) * LANES)
        rate = rate_ref[:, span]
        carry = None
        for item in range(slices):
            value = part_ref[item, :, span]
            piece = slice(item * LANES, (item + 1) * LANES)
            if block == 0:
                value = value + low[:, piece]
            if block == count - 1:
                value = value + high[:, piece]
            out_ref[item, :, span] = value
            carry = rate * value if carry is None else rate * (carry + value)
        carry_ref[:, span] = carry
    if pieces == 1:
        piece_refs[0][...] = carry_ref[...]
    else:
        for step, piece_ref in zip(steps(pieces), piece_refs):
            piece_ref[...] = carry_ref[row_part(step, pieces, rows), :]


def steps(pieces):
    return list(range(pieces))[:1] + list(range(1, pieces))[-1:] + list(range(1, pieces - 1))


def row_part(step, pieces, rows):
    share = rows // pieces
    return pl.ds(pl.multiple_of((lax.axis_index("tm") ^ step) * share, 8), share)


def periodic(carries, factor):
    count = len(carries)
    total = carries[0]
    for k in range(1, count):
        total = carries[k] + factor * total
    power = factor
    for _ in range(count - 1):
        power = power * factor
    entering = [total / (1.0 - power)]
    for k in range(count - 1):
        entering.append(carries[k] + factor * entering[-1])
    return entering


def around_kernel(slices, pieces, *refs):
    got, rate_ref = refs[:pieces], refs[pieces]
    sent, held = refs[pieces + 1 : 2 * pieces + 1], refs[2 * pieces + 1]
    me = lax.axis_index("tm")
    rate = rate_ref[row_part(0, pieces, rate_ref.shape[0]), :]
    factor = rate
    for _ in range(slices - 1):
        factor = factor * rate
    for step, piece_ref in zip(steps(pieces), got):
        held[me ^ step] = piece_ref[...]
    entering = periodic([held[k] for k in range(pieces)], factor)
    for k in range(pieces):
        held[k] = entering[k]
    for step, piece_ref in zip(steps(pieces), sent):
        piece_ref[...] = held[me ^ step]


def solve_kernel(pieces, *refs):
    piece_refs = refs[:pieces]
    right_ref, rate_ref, state_ref, before_ref, near_ref, far_ref = refs[pieces:]
    slices, rows, columns = right_ref.shape
    if pieces == 1:
        before_ref[...] = piece_refs[0][...]
    else:
        for step, piece_ref in zip(steps(pieces), piece_refs):
            before_ref[row_part(step, pieces, rows), :] = piece_ref[...]
    rate = rate_ref[...]
    value = before_ref[...]
    low = []
    high = []
    for item in range(slices):
        value = rate * (value + right_ref[item])
        state_ref[item] = value
        cube = value.reshape(NF, NP**3, columns)
        low.append(cube[:, 0:16, 0:LANES].reshape(FACE, LANES))
        high.append(cube[:, 48:64, columns - LANES :].reshape(FACE, LANES))
    send(low, high, near_ref, far_ref)


def second_kernel(
    state_ref, before_ref, forcing_ref, weights_ref, neighbor_ref, tags_ref, codes_ref, out_ref,
    result_ref, blocks, stack, semaphore,
):
    slices, _, columns = state_ref.shape
    copy = pltpu.make_async_copy(state_ref, result_ref, semaphore)
    copy.start()
    image = operator(
        state_ref, blocks, stack, weights_ref, neighbor_ref, tags_ref, codes_ref
    )
    for item in range(slices):
        previous = before_ref[...] if item == 0 else state_ref[item - 1]
        out_ref[item] = (
            image[:, item * columns : (item + 1) * columns]
            + forcing_ref[item]
            + (previous - state_ref[item])
        )
    copy.wait()


def finish_kernel(
    part_ref, near_ref, far_ref, rim_weights_ref, neighbor_ref, tags_ref, codes_ref, out_ref,
    held, semaphores,
):
    slices, _, columns = part_ref.shape
    count = columns // LANES
    low, high = rim(
        near_ref, far_ref, slices, rim_weights_ref, neighbor_ref, tags_ref, codes_ref, count
    )
    copies = []
    for block in range(count):
        span = pl.ds(block * LANES, LANES)
        for item in range(slices):
            value = part_ref[item, :, span]
            piece = slice(item * LANES, (item + 1) * LANES)
            if block == 0:
                value = value + low[:, piece]
            if block == count - 1:
                value = value + high[:, piece]
            held[item, :, span] = value.astype(held.dtype)
        copy = pltpu.make_async_copy(
            held.at[:, :, span], out_ref.at[:, :, span], semaphores.at[block]
        )
        copy.start()
        copies.append(copy)
    for copy in copies:
        copy.wait()


VMEM = pl.BlockSpec(memory_space=pltpu.VMEM)
HBM = pl.BlockSpec(memory_space=pltpu.HBM)


def call(kernel, name, outs, args, scratch=(), flops=0, in_specs=None, out_specs=None):
    size = sum(math.prod(a.shape) * a.dtype.itemsize for a in list(args) + list(outs))
    return pl.pallas_call(
        kernel,
        name=name,
        out_shape=outs,
        in_specs=in_specs or [VMEM] * len(args),
        out_specs=out_specs or [VMEM] * len(outs),
        scratch_shapes=list(scratch),
        compiler_params=pltpu.CompilerParams(vmem_limit_bytes=40 * 2**20),
        cost_estimate=pl.CostEstimate(flops=flops, bytes_accessed=size, transcendentals=0),
    )(*args)


def exchange(near, far):
    count = lax.axis_size("space")
    inner = [(i, i + 1) for i in range(0, count - 1, 2)]
    outer = [(i, (i + 1) % count) for i in range(1, count, 2)]
    near = lax.ppermute(near, "space", inner + [(j, i) for i, j in inner])
    far = lax.ppermute(far, "space", outer + [(j, i) for i, j in outer])
    return near, far


def swapped(value, step):
    if step == 0:
        return value
    count = lax.axis_size("tm")
    return lax.ppermute(value, "tm", [(i, i ^ step) for i in range(count)])


def in_hbm(value):
    return pltpu.with_memory_space_constraint(value, pltpu.HBM)


def local(guess, source_cos, source_sin, damping, volume, lifts, neighbor, tags, codes):
    slices, rows, columns = guess.shape
    devices = lax.axis_size("tm")
    f32, bf16 = jnp.float32, jnp.bfloat16
    shape = jax.ShapeDtypeStruct
    whole = shape((slices, rows, columns), f32)
    plane = shape((rows, columns), f32)
    packed = shape(((slices + 1) // 2, FACE, LANES), f32)
    depth = rows + 6 * FACE
    scratch = [
        pltpu.VMEM((slices * columns // LANES, rows, LANES), f32),
        pltpu.VMEM((depth, 2 * slices * columns), bf16),
    ]
    work = 4 * rows * depth * slices * columns
    end = pltpu.VMEM((slices, NF, NP * NP, LANES), f32)
    share = rows // devices
    pairs = devices & (devices - 1) == 0 and devices <= 8 and share % 8 == 0
    pieces = devices if pairs else 1
    piece = shape((rows // pieces, columns), f32)

    near, far = call(
        ends_kernel, "ends", [packed] * 2,
        [in_hbm(guess.reshape(slices, NF, NP**3, columns))],
        [end, end, pltpu.SemaphoreType.DMA((2,))], in_specs=[HBM],
    )
    near, far = exchange(near, far)
    operands = (
        guess, neighbor, tags, codes, jnp.swapaxes(lifts, 1, 2), volume, damping, source_cos,
        source_sin,
    )
    part, weights, rim_weights, rate, forcing, *tables = call(
        functools.partial(first_kernel, slices * devices), "first",
        [whole, shape((rows, depth), bf16), shape((2, rows, FACE), bf16), plane, whole]
        + [shape(neighbor.shape, jnp.int32)] * 3,
        [in_hbm(operand) for operand in operands],
        [
            pltpu.VMEM(whole.shape, f32),
            pltpu.VMEM(plane.shape, bf16),
            pltpu.VMEM(plane.shape, bf16),
            pltpu.VMEM(plane.shape, f32),
            pltpu.VMEM(volume.shape, bf16),
            pltpu.VMEM((6, FACE, rows), bf16),
            *scratch,
            pltpu.SemaphoreType.DMA((len(operands),)),
        ],
        flops=work, in_specs=[HBM] * len(operands),
    )
    known, *parts = call(
        functools.partial(carry_kernel, pieces), "carry", [whole] + [piece] * pieces,
        [part, near, far, rate, rim_weights, *tables], [pltpu.VMEM(plane.shape, f32)],
    )
    if pairs:
        parts = [swapped(part, step) for step, part in zip(steps(pieces), parts)]
        parts = call(
            functools.partial(around_kernel, slices, pieces), "around", [piece] * pieces,
            [*parts, rate], [pltpu.VMEM((pieces, *piece.shape), f32)],
        )
        parts = [swapped(part, step) for step, part in zip(steps(pieces), parts)]
    else:
        me = lax.axis_index("tm")
        factor = lax.dynamic_slice_in_dim(rate, me * share, share, 0) ** slices
        carries = lax.all_to_all(parts[0], "tm", split_axis=0, concat_axis=0, tiled=True)
        carries = carries.reshape(devices, share, columns)
        back = jnp.concatenate(periodic([carries[k] for k in range(devices)], factor), axis=0)
        parts = [lax.all_to_all(back, "tm", split_axis=0, concat_axis=0, tiled=True)]
    state, before, near, far = call(
        functools.partial(solve_kernel, pieces), "solve",
        [whole, plane, packed, packed], [*parts, known, rate],
    )
    near, far = exchange(near, far)
    part, result = call(
        second_kernel, "second", [whole, whole],
        [state, before, forcing, weights, *tables],
        [*scratch, pltpu.SemaphoreType.DMA], flops=work, out_specs=[VMEM, HBM],
    )
    (after,) = call(
        finish_kernel, "finish", [shape(whole.shape, bf16)],
        [part, near, far, rim_weights, *tables],
        [pltpu.VMEM(whole.shape, bf16), pltpu.SemaphoreType.DMA((columns // LANES,))],
        out_specs=[HBM],
    )
    return result, after


def solution(mesh):
    column = P(None, ("groups", "space"))
    state = P("tm", None, ("groups", "space"))
    in_specs = (state, column, column, column, P(), P(), column, column, column)
    return jax.shard_map(
        local, mesh=mesh, in_specs=in_specs, out_specs=(state, state), check_vma=False
    )
```

```python
import functools
import math

import jax
import jax.numpy as jnp
from jax import lax
from jax.experimental import pallas as pl
from jax.experimental.pallas import tpu as pltpu
from jax.sharding import PartitionSpec as P

NF = 5
NP = 4
FACE = NF * NP * NP
LANES = 128
HALF = 64


def split(value):
    high = value.astype(jnp.bfloat16)
    low = (value - high.astype(jnp.float32)).astype(jnp.bfloat16)
    return high, low


def end_trace(cube, face):
    rows = cube[:, 0:16] if face == 0 else cube[:, 48:64]
    return rows.reshape(FACE, LANES)


def side_trace(cube, face):
    tiles = cube.reshape(NF, 2, 2, 16, LANES)
    part = tiles[:, :, :, 0:8] if face == 2 else tiles[:, :, :, 8:16]
    even = part[:, :, 0].reshape(FACE // 8, 8, LANES)
    odd = part[:, :, 1].reshape(FACE // 8, 8, LANES)
    lower = lax.broadcasted_iota(jnp.int32, (FACE // 8, 8, LANES), 1) < 4
    if face == 2:
        odd = pltpu.roll(odd, 4, axis=1)
    else:
        even = pltpu.roll(even, 4, axis=1)
    return jnp.where(lower, even, odd).reshape(FACE, LANES)


def lane_index(row):
    return jnp.broadcast_to(row, (FACE, LANES))


def orientation(code):
    swap = (code & 1) == 1
    turn_i = (code & 2) == 2
    turn_j = (code & 4) == 4
    result = []
    for tile in range(2):
        row = lax.broadcasted_iota(jnp.int32, (8, LANES), 0) + 8 * tile
        i, j = row >> 2, row & 3
        i = jnp.where(turn_i, 3 - i, i)
        j = jnp.where(turn_j, 3 - j, j)
        source = jnp.where(swap, j * 4 + i, i * 4 + j)
        result.append((source >= 8, source & 7))
    return result


def oriented(value, plan):
    pieces = []
    for field in range(NF):
        first = value[field * 16 : field * 16 + 8]
        second = value[field * 16 + 8 : field * 16 + 16]
        for upper, sub in plan:
            pick = functools.partial(jnp.take_along_axis, axis=0, mode="promise_in_bounds")
            pieces.append(jnp.where(upper, pick(second, sub), pick(first, sub)))
    return jnp.concatenate(pieces, axis=0)


def gather_lanes(value, row):
    return jnp.take_along_axis(value, lane_index(row), axis=1, mode="promise_in_bounds")


def operator(
    state, blocks, stack, weights_ref, neighbor_ref, tags_ref, codes_ref,
    ready=lambda: None, ahead=lambda: None,
):
    slices, rows, columns = state.shape
    count = columns // LANES
    wide = slices * columns
    base = 6 * FACE
    lane = lax.broadcasted_iota(jnp.int32, (FACE, LANES), 1)
    for item in range(slices):
        for block in range(count):
            n = item * count + block
            value = state[item, :, block * LANES : (block + 1) * LANES]
            blocks[n] = value
            high, low = split(value)
            stack[base:, n * LANES : (n + 1) * LANES] = high
            stack[base:, wide + n * LANES : wide + (n + 1) * LANES] = low
    ready()
    for item in range(slices):
        cubes = []
        turned = []
        for block in range(count):
            cube = blocks[item * count + block].reshape(NF, NP**3, LANES)
            cubes.append(cube)
            turned.append(
                [pltpu.roll(end_trace(cube, face), HALF, axis=1) for face in range(2)]
            )
        zero = jnp.zeros((FACE, LANES), jnp.float32)
        for block in range(count):
            n = item * count + block
            cube = cubes[block]
            before = turned[block - 1][1] if block > 0 else zero
            after = turned[block + 1][0] if block + 1 < count else zero
            ends = [end_trace(cube, 0), end_trace(cube, 1)]
            sides = [side_trace(cube, 2), side_trace(cube, 3)]
            tops = [
                blocks[n, pl.ds(0, FACE, stride=4), :],
                blocks[n, pl.ds(3, FACE, stride=4), :],
            ]
            mine = ends + sides + tops
            across = [
                jnp.where(lane < HALF, before, turned[block][1]),
                jnp.where(lane < HALF, turned[block][0], after),
                sides[1],
                sides[0],
                tops[1],
                tops[0],
            ]
            for face in range(6):
                span = slice(block * LANES, (block + 1) * LANES)
                target = neighbor_ref[face : face + 1, span]
                kind = tags_ref[face : face + 1, span]
                code = codes_ref[face : face + 1, span]
                if face < 2:
                    target = target + HALF
                plan = orientation(code)
                taken = oriented(gather_lanes(across[face], target & (LANES - 1)), plan)
                keep = jnp.where((kind == 1) | (kind == 3), 1.0, 0.0)
                flip = jnp.where(kind == 1, -1.0, keep)
                axis = 1 + face // 2
                inner = []
                for field in range(NF):
                    own = mine[face][field * 16 : (field + 1) * 16]
                    inner.append(own * (flip if field == axis else keep))
                seen = jnp.where(kind == 0, taken, jnp.concatenate(inner, axis=0))
                high, low = split(seen)
                place = FACE * face
                stack[place : place + FACE, n * LANES : (n + 1) * LANES] = high
                stack[place : place + FACE, wide + n * LANES : wide + (n + 1) * LANES] = low
    ahead()
    image = jnp.dot(weights_ref[...], stack[:, 0:wide], preferred_element_type=jnp.float32)
    return image + jnp.dot(
        weights_ref[...], stack[:, wide:], preferred_element_type=jnp.float32
    )


def even_place():
    return (lax.axis_index("space") & 1) == 0


def rim(far, near, slices, rim_weights_ref, neighbor_ref, tags_ref, codes_ref, count):
    lane = lax.broadcasted_iota(jnp.int32, (1, LANES), 1)
    even = even_place()
    result = []
    for face in range(2):
        block = 0 if face == 0 else count - 1
        span = slice(block * LANES, (block + 1) * LANES)
        target = neighbor_ref[face : face + 1, span] & (HALF - 1)
        inside = lane < HALF if face == 0 else lane >= HALF
        use = (tags_ref[face : face + 1, span] == 0) & inside
        plan = orientation(codes_ref[face : face + 1, span])
        pieces = []
        for item in range(slices):
            a, b = (far, near) if face == 0 else (near, far)
            halo = jnp.where(even, a[item // 2], b[item // 2])
            taken = gather_lanes(halo, target + HALF * (item % 2))
            pieces.append(split(jnp.where(use, oriented(taken, plan), 0.0)))
        both = jnp.concatenate([p[0] for p in pieces] + [p[1] for p in pieces], axis=1)
        product = jnp.dot(rim_weights_ref[face], both, preferred_element_type=jnp.float32)
        wide = slices * LANES
        result.append(product[:, :wide] + product[:, wide:])
    return result


def send(low, high, far_ref, near_ref):
    slices = len(low)
    lane = lax.broadcasted_iota(jnp.int32, (FACE, LANES), 1)
    even = even_place()
    for item in range(0, slices, 2):
        other = min(item + 1, slices - 1)
        first = jnp.where(lane < HALF, low[item], pltpu.roll(low[other], HALF, axis=1))
        last = jnp.where(lane < HALF, pltpu.roll(high[item], HALF, axis=1), high[other])
        near_ref[item // 2] = jnp.where(even, last, first)
        far_ref[item // 2] = jnp.where(even, first, last)


def ends_kernel(state_ref, far_ref, near_ref, held_ref, low, high, semaphore):
    slices, _, _, columns = state_ref.shape
    copies = [
        pltpu.make_async_copy(
            state_ref.at[:, :, pl.ds(0, 16), pl.ds(0, LANES)], low, semaphore.at[0]
        ),
        pltpu.make_async_copy(
            state_ref.at[:, :, pl.ds(48, 16), pl.ds(columns - LANES, LANES)], high, semaphore.at[1]
        ),
        pltpu.make_async_copy(state_ref, held_ref, semaphore.at[2]),
    ]
    for copy in copies:
        copy.start()
    for copy in copies[:2]:
        copy.wait()
    send(
        [low[item].reshape(FACE, LANES) for item in range(slices)],
        [high[item].reshape(FACE, LANES) for item in range(slices)],
        far_ref,
        near_ref,
    )
    copies[2].wait()


def wave(at, values):
    result = jnp.float32(values[0])
    for k in range(1, len(values)):
        result = jnp.where(at == k, jnp.float32(values[k]), result)
    return result


def first_kernel(total, state_ref, *refs):
    sources = refs[:8]
    out_ref, weights_ref, rim_weights_ref, rate_ref, forcing_ref = refs[8:13]
    neighbor_ref, tags_ref, codes_ref = refs[13:16]
    cos_ref, sin_ref, damping_ref, volume_ref, lifts_ref = refs[16:21]
    blocks, stack, semaphores = refs[21:]
    targets = (
        neighbor_ref, tags_ref, codes_ref, lifts_ref, volume_ref, damping_ref, cos_ref, sin_ref,
    )
    copies = [
        pltpu.make_async_copy(source, target, semaphores.at[k])
        for k, (source, target) in enumerate(zip(sources, targets))
    ]
    for copy in copies:
        copy.start()
    slices, _, columns = state_ref.shape

    def ready():
        for copy in copies[:3]:
            copy.wait()

    def ahead():
        for copy in copies[3:]:
            copy.wait()
        for face in range(6):
            lift = lifts_ref[face].T
            weights_ref[:, FACE * face : FACE * (face + 1)] = lift
            if face < 2:
                rim_weights_ref[face] = lift
        weights_ref[:, 6 * FACE :] = volume_ref[...]

    image = operator(
        state_ref, blocks, stack, weights_ref, neighbor_ref, tags_ref, codes_ref, ready, ahead
    )
    rate_ref[...] = 1.0 / (1.0 + damping_ref[...])
    angles = [2.0 * math.pi * k / total for k in range(total)]
    for item in range(slices):
        at = lax.axis_index("tm") * slices + item
        forcing = wave(at, [math.cos(x) for x in angles]) * cos_ref[...].astype(jnp.float32)
        forcing += wave(at, [math.sin(x) for x in angles]) * sin_ref[...].astype(jnp.float32)
        forcing_ref[item] = forcing
        out_ref[item] = (
            image[:, item * columns : (item + 1) * columns]
            + forcing
            + damping_ref[...] * state_ref[item]
        )


def carry_kernel(
    pieces, part_ref, far_ref, near_ref, rate_ref, rim_weights_ref, neighbor_ref, tags_ref,
    codes_ref, out_ref, *refs
):
    *piece_refs, carry_ref = refs
    slices, rows, columns = part_ref.shape
    count = columns // LANES
    low, high = rim(
        far_ref, near_ref, slices, rim_weights_ref, neighbor_ref, tags_ref, codes_ref, count
    )
    for block in range(count):
        span = slice(block * LANES, (block + 1) * LANES)
        rate = rate_ref[:, span]
        carry = None
        for item in range(slices):
            value = part_ref[item, :, span]
            piece = slice(item * LANES, (item + 1) * LANES)
            if block == 0:
                value = value + low[:, piece]
            if block == count - 1:
                value = value + high[:, piece]
            out_ref[item, :, span] = value
            carry = rate * value if carry is None else rate * (carry + value)
        carry_ref[:, span] = carry
    if pieces == 1:
        piece_refs[0][...] = carry_ref[...]
    else:
        for part in range(pieces):
            piece_refs[part][...] = carry_ref[row_part(part, rows // pieces), :]


def row_part(part, share):
    mine = lax.axis_index("tm") & 1
    return pl.ds(pl.multiple_of(((part & 2) + (mine ^ (part & 1))) * share, 8), share)


def periodic(carries, factor):
    count = len(carries)
    total = carries[0]
    for k in range(1, count):
        total = carries[k] + factor * total
    power = factor
    for _ in range(count - 1):
        power = power * factor
    entering = [total / (1.0 - power)]
    for k in range(count - 1):
        entering.append(carries[k] + factor * entering[-1])
    return entering


def power(rate_ref, part, share, slices):
    rate = rate_ref[row_part(part, share), :]
    factor = rate
    for _ in range(slices - 1):
        factor = factor * rate
    return factor


def ordered(own, other):
    first = (lax.axis_index("tm") & 1) == 0
    return jnp.where(first, own, other), jnp.where(first, other, own)


def pair_kernel(slices, part, own_ref, other_ref, rate_ref, out_ref):
    factor = power(rate_ref, part, own_ref.shape[0], slices)
    early, late = ordered(own_ref[...], other_ref[...])
    out_ref[...] = late + factor * early


def enter_kernel(
    slices, part, own_ref, other_ref, here_ref, there_ref, rate_ref, keep_ref, send_ref
):
    factor = power(rate_ref, part, own_ref.shape[0], slices)
    square = factor * factor
    early, _ = ordered(own_ref[...], other_ref[...])
    enter = (there_ref[...] + square * here_ref[...]) / (1.0 - square * square)
    later = early + factor * enter
    own, other = ordered(enter, later)
    keep_ref[...] = own
    send_ref[...] = other


def solve_kernel(pieces, *refs):
    piece_refs = refs[:pieces]
    right_ref, rate_ref, state_ref, before_ref, far_ref, near_ref = refs[pieces:]
    slices, rows, columns = right_ref.shape
    if pieces == 1:
        before_ref[...] = piece_refs[0][...]
    else:
        for part in range(pieces):
            before_ref[row_part(part, rows // pieces), :] = piece_refs[part][...]
    rate = rate_ref[...]
    value = before_ref[...]
    low = []
    high = []
    for item in range(slices):
        value = rate * (value + right_ref[item])
        state_ref[item] = value
        cube = value.reshape(NF, NP**3, columns)
        low.append(cube[:, 0:16, 0:LANES].reshape(FACE, LANES))
        high.append(cube[:, 48:64, columns - LANES :].reshape(FACE, LANES))
    send(low, high, far_ref, near_ref)


def second_kernel(
    state_ref, before_ref, forcing_ref, weights_ref, neighbor_ref, tags_ref, codes_ref, out_ref,
    result_ref, blocks, stack, semaphore,
):
    slices, _, columns = state_ref.shape
    copy = pltpu.make_async_copy(state_ref, result_ref, semaphore)
    copy.start()
    image = operator(
        state_ref, blocks, stack, weights_ref, neighbor_ref, tags_ref, codes_ref
    )
    for item in range(slices):
        previous = before_ref[...] if item == 0 else state_ref[item - 1]
        out_ref[item] = (
            image[:, item * columns : (item + 1) * columns]
            + forcing_ref[item]
            + (previous - state_ref[item])
        )
    copy.wait()


def finish_kernel(
    part_ref, far_ref, near_ref, rim_weights_ref, neighbor_ref, tags_ref, codes_ref, out_ref,
    held, semaphores,
):
    slices, _, columns = part_ref.shape
    count = columns // LANES
    low, high = rim(
        far_ref, near_ref, slices, rim_weights_ref, neighbor_ref, tags_ref, codes_ref, count
    )
    copies = []
    for block in range(count):
        span = pl.ds(block * LANES, LANES)
        for item in range(slices):
            value = part_ref[item, :, span]
            piece = slice(item * LANES, (item + 1) * LANES)
            if block == 0:
                value = value + low[:, piece]
            if block == count - 1:
                value = value + high[:, piece]
            held[item, :, span] = value.astype(held.dtype)
        copy = pltpu.make_async_copy(
            held.at[:, :, span], out_ref.at[:, :, span], semaphores.at[block]
        )
        copy.start()
        copies.append(copy)
    for copy in copies:
        copy.wait()


VMEM = pl.BlockSpec(memory_space=pltpu.VMEM)
HBM = pl.BlockSpec(memory_space=pltpu.HBM)


def call(kernel, name, outs, args, scratch=(), flops=0, in_specs=None, out_specs=None):
    size = sum(math.prod(a.shape) * a.dtype.itemsize for a in list(args) + list(outs))
    return pl.pallas_call(
        kernel,
        name=name,
        out_shape=outs,
        in_specs=in_specs or [VMEM] * len(args),
        out_specs=out_specs or [VMEM] * len(outs),
        scratch_shapes=list(scratch),
        compiler_params=pltpu.CompilerParams(vmem_limit_bytes=40 * 2**20),
        cost_estimate=pl.CostEstimate(flops=flops, bytes_accessed=size, transcendentals=0),
    )(*args)


def exchange(far, near):
    count = lax.axis_size("space")
    inner = [(i, i + 1) for i in range(0, count - 1, 2)]
    outer = [(i, (i + 1) % count) for i in range(1, count, 2)]
    far = lax.ppermute(far, "space", outer + [(j, i) for i, j in outer])
    near = lax.ppermute(near, "space", inner + [(j, i) for i, j in inner])
    return far, near


def swapped(value, step):
    count = lax.axis_size("tm")
    return lax.ppermute(value, "tm", [(i, i ^ step) for i in range(count)])


def in_hbm(value):
    return pltpu.with_memory_space_constraint(value, pltpu.HBM)


def local(guess, source_cos, source_sin, damping, volume, lifts, neighbor, tags, codes):
    slices, rows, columns = guess.shape
    devices = lax.axis_size("tm")
    f32, bf16 = jnp.float32, jnp.bfloat16
    shape = jax.ShapeDtypeStruct
    whole = shape((slices, rows, columns), f32)
    plane = shape((rows, columns), f32)
    packed = shape(((slices + 1) // 2, FACE, LANES), f32)
    depth = rows + 6 * FACE
    scratch = [
        pltpu.VMEM((slices * columns // LANES, rows, LANES), f32),
        pltpu.VMEM((depth, 2 * slices * columns), bf16),
    ]
    work = 4 * rows * depth * slices * columns
    end = pltpu.VMEM((slices, NF, NP * NP, LANES), f32)
    share = rows // devices
    pairs = devices == 4 and share % 8 == 0
    pieces = devices if pairs else 1
    piece = shape((rows // pieces, columns), f32)

    cube = guess.reshape(slices, NF, NP**3, columns)
    far, near, held = call(
        ends_kernel, "ends", [packed, packed, shape(cube.shape, f32)], [in_hbm(cube)],
        [end, end, pltpu.SemaphoreType.DMA((3,))], in_specs=[HBM],
    )
    far, near = exchange(far, near)
    operands = (
        neighbor, tags, codes, jnp.swapaxes(lifts, 1, 2), volume, damping, source_cos,
        source_sin,
    )
    part, weights, rim_weights, rate, forcing, *tables = call(
        functools.partial(first_kernel, slices * devices), "first",
        [whole, shape((rows, depth), bf16), shape((2, rows, FACE), bf16), plane, whole]
        + [shape(neighbor.shape, jnp.int32)] * 3,
        [held.reshape(guess.shape)] + [in_hbm(operand) for operand in operands],
        [
            pltpu.VMEM(plane.shape, bf16),
            pltpu.VMEM(plane.shape, bf16),
            pltpu.VMEM(plane.shape, f32),
            pltpu.VMEM(volume.shape, bf16),
            pltpu.VMEM((6, FACE, rows), bf16),
            *scratch,
            pltpu.SemaphoreType.DMA((len(operands),)),
        ],
        flops=work, in_specs=[VMEM] + [HBM] * len(operands),
    )
    known, *parts = call(
        functools.partial(carry_kernel, pieces), "carry", [whole] + [piece] * pieces,
        [part, far, near, rate, rim_weights, *tables], [pltpu.VMEM(plane.shape, f32)],
    )
    if pairs:
        around = []
        others = [swapped(parts[k + 1], 1) for k in (0, 2)]
        for k in (0, 2):
            (here,) = call(
                functools.partial(pair_kernel, slices, k), "pair", [piece],
                [parts[k], others[k // 2], rate],
            )
            around.append((here, swapped(here, 2)))
        own = parts[::2]
        parts = []
        for k in (0, 2):
            keep, pass_on = call(
                functools.partial(enter_kernel, slices, k), "enter", [piece] * 2,
                [own[k // 2], others[k // 2], *around[k // 2], rate],
            )
            parts += [keep, swapped(pass_on, 1)]
    else:
        me = lax.axis_index("tm")
        factor = lax.dynamic_slice_in_dim(rate, me * share, share, 0) ** slices
        carries = lax.all_to_all(parts[0], "tm", split_axis=0, concat_axis=0, tiled=True)
        carries = carries.reshape(devices, share, columns)
        back = jnp.concatenate(periodic([carries[k] for k in range(devices)], factor), axis=0)
        parts = [lax.all_to_all(back, "tm", split_axis=0, concat_axis=0, tiled=True)]
    state, before, far, near = call(
        functools.partial(solve_kernel, pieces), "solve",
        [whole, plane, packed, packed], [*parts, known, rate],
    )
    far, near = exchange(far, near)
    part, result = call(
        second_kernel, "second", [whole, whole],
        [state, before, forcing, weights, *tables],
        [*scratch, pltpu.SemaphoreType.DMA], flops=work, out_specs=[VMEM, HBM],
    )
    (after,) = call(
        finish_kernel, "finish", [shape(whole.shape, bf16)],
        [part, far, near, rim_weights, *tables],
        [pltpu.VMEM(whole.shape, bf16), pltpu.SemaphoreType.DMA((columns // LANES,))],
        out_specs=[HBM],
    )
    return result, after


def solution(mesh):
    column = P(None, ("groups", "space"))
    state = P("tm", None, ("groups", "space"))
    in_specs = (state, column, column, column, P(), P(), column, column, column)
    return jax.shard_map(
        local, mesh=mesh, in_specs=in_specs, out_specs=(state, state), check_vma=False
    )
```

```python
import functools
import math

import jax
import jax.numpy as jnp
from jax import lax
from jax.experimental import pallas as pl
from jax.experimental.pallas import tpu as pltpu
from jax.sharding import PartitionSpec as P

NF = 5
NP = 4
FACE = NF * NP * NP
LANES = 128
HALF = 64


def split(value):
    high = value.astype(jnp.bfloat16)
    low = (value - high.astype(jnp.float32)).astype(jnp.bfloat16)
    return high, low


def end_trace(cube, face):
    rows = cube[:, 0:16] if face == 0 else cube[:, 48:64]
    return rows.reshape(FACE, LANES)


def side_trace(cube, face):
    tiles = cube.reshape(NF, 2, 2, 16, LANES)
    part = tiles[:, :, :, 0:8] if face == 2 else tiles[:, :, :, 8:16]
    even = part[:, :, 0].reshape(FACE // 8, 8, LANES)
    odd = part[:, :, 1].reshape(FACE // 8, 8, LANES)
    lower = lax.broadcasted_iota(jnp.int32, (FACE // 8, 8, LANES), 1) < 4
    if face == 2:
        odd = pltpu.roll(odd, 4, axis=1)
    else:
        even = pltpu.roll(even, 4, axis=1)
    return jnp.where(lower, even, odd).reshape(FACE, LANES)


def lane_index(row):
    return jnp.broadcast_to(row, (FACE, LANES))


def orientation(code):
    swap = (code & 1) == 1
    turn_i = (code & 2) == 2
    turn_j = (code & 4) == 4
    result = []
    for tile in range(2):
        row = lax.broadcasted_iota(jnp.int32, (8, LANES), 0) + 8 * tile
        i, j = row >> 2, row & 3
        i = jnp.where(turn_i, 3 - i, i)
        j = jnp.where(turn_j, 3 - j, j)
        source = jnp.where(swap, j * 4 + i, i * 4 + j)
        result.append((source >= 8, source & 7))
    return result


def oriented(value, plan):
    pieces = []
    for field in range(NF):
        first = value[field * 16 : field * 16 + 8]
        second = value[field * 16 + 8 : field * 16 + 16]
        for upper, sub in plan:
            pick = functools.partial(jnp.take_along_axis, axis=0, mode="promise_in_bounds")
            pieces.append(jnp.where(upper, pick(second, sub), pick(first, sub)))
    return jnp.concatenate(pieces, axis=0)


def gather_lanes(value, row):
    return jnp.take_along_axis(value, lane_index(row), axis=1, mode="promise_in_bounds")


def operator(
    state, blocks, stack, weights_ref, neighbor_ref, tags_ref, codes_ref,
    ready=lambda: None, ahead=lambda: None,
):
    slices, rows, columns = state.shape
    count = columns // LANES
    wide = slices * columns
    base = 6 * FACE
    lane = lax.broadcasted_iota(jnp.int32, (FACE, LANES), 1)
    for item in range(slices):
        for block in range(count):
            n = item * count + block
            value = state[item, :, block * LANES : (block + 1) * LANES]
            blocks[n] = value
            high, low = split(value)
            stack[base:, n * LANES : (n + 1) * LANES] = high
            stack[base:, wide + n * LANES : wide + (n + 1) * LANES] = low
    ready()
    for item in range(slices):
        cubes = []
        turned = []
        for block in range(count):
            cube = blocks[item * count + block].reshape(NF, NP**3, LANES)
            cubes.append(cube)
            turned.append(
                [pltpu.roll(end_trace(cube, face), HALF, axis=1) for face in range(2)]
            )
        zero = jnp.zeros((FACE, LANES), jnp.float32)
        for block in range(count):
            n = item * count + block
            cube = cubes[block]
            before = turned[block - 1][1] if block > 0 else zero
            after = turned[block + 1][0] if block + 1 < count else zero
            ends = [end_trace(cube, 0), end_trace(cube, 1)]
            sides = [side_trace(cube, 2), side_trace(cube, 3)]
            tops = [
                blocks[n, pl.ds(0, FACE, stride=4), :],
                blocks[n, pl.ds(3, FACE, stride=4), :],
            ]
            mine = ends + sides + tops
            across = [
                jnp.where(lane < HALF, before, turned[block][1]),
                jnp.where(lane < HALF, turned[block][0], after),
                sides[1],
                sides[0],
                tops[1],
                tops[0],
            ]
            for face in range(6):
                span = slice(block * LANES, (block + 1) * LANES)
                target = neighbor_ref[face : face + 1, span]
                kind = tags_ref[face : face + 1, span]
                code = codes_ref[face : face + 1, span]
                if face < 2:
                    target = target + HALF
                plan = orientation(code)
                taken = oriented(gather_lanes(across[face], target & (LANES - 1)), plan)
                keep = jnp.where((kind == 1) | (kind == 3), 1.0, 0.0)
                flip = jnp.where(kind == 1, -1.0, keep)
                axis = 1 + face // 2
                inner = []
                for field in range(NF):
                    own = mine[face][field * 16 : (field + 1) * 16]
                    inner.append(own * (flip if field == axis else keep))
                seen = jnp.where(kind == 0, taken, jnp.concatenate(inner, axis=0))
                high, low = split(seen)
                place = FACE * face
                stack[place : place + FACE, n * LANES : (n + 1) * LANES] = high
                stack[place : place + FACE, wide + n * LANES : wide + (n + 1) * LANES] = low
    ahead()
    image = jnp.dot(weights_ref[...], stack[:, 0:wide], preferred_element_type=jnp.float32)
    return image + jnp.dot(
        weights_ref[...], stack[:, wide:], preferred_element_type=jnp.float32
    )


def even_place():
    return (lax.axis_index("space") & 1) == 0


def rim(far, near, slices, rim_weights_ref, neighbor_ref, tags_ref, codes_ref, count):
    lane = lax.broadcasted_iota(jnp.int32, (1, LANES), 1)
    even = even_place()
    result = []
    for face in range(2):
        block = 0 if face == 0 else count - 1
        span = slice(block * LANES, (block + 1) * LANES)
        target = neighbor_ref[face : face + 1, span] & (HALF - 1)
        inside = lane < HALF if face == 0 else lane >= HALF
        use = (tags_ref[face : face + 1, span] == 0) & inside
        plan = orientation(codes_ref[face : face + 1, span])
        pieces = []
        for item in range(slices):
            a, b = (far, near) if face == 0 else (near, far)
            halo = jnp.where(even, a[item // 2], b[item // 2])
            taken = gather_lanes(halo, target + HALF * (item % 2))
            pieces.append(split(jnp.where(use, oriented(taken, plan), 0.0)))
        both = jnp.concatenate([p[0] for p in pieces] + [p[1] for p in pieces], axis=1)
        product = jnp.dot(rim_weights_ref[face], both, preferred_element_type=jnp.float32)
        wide = slices * LANES
        result.append(product[:, :wide] + product[:, wide:])
    return result


def packed(low, high):
    lane = lax.broadcasted_iota(jnp.int32, (FACE, LANES), 1)
    first = jnp.where(lane < HALF, low[0], pltpu.roll(low[1], HALF, axis=1))
    last = jnp.where(lane < HALF, pltpu.roll(high[0], HALF, axis=1), high[1])
    return first, last


def send(low, high, near_ref, far_ref=None):
    slices = len(low)
    even = even_place()
    for item in range(0, slices, 2):
        other = min(item + 1, slices - 1)
        first, last = packed([low[item], low[other]], [high[item], high[other]])
        near_ref[item // 2] = jnp.where(even, last, first)
        if far_ref is not None:
            far_ref[item // 2] = jnp.where(even, first, last)


def spread_kernel(
    keep0_ref, pass0_ref, keep3_ref, pass3_ref, edges_ref, others_ref, rate_ref, far_ref,
    far_pass_ref,
):
    columns = keep0_ref.shape[1]
    even = even_place()
    rate = jnp.where(
        even,
        rate_ref[:, 0:16, 0:LANES].reshape(FACE, LANES),
        rate_ref[:, 48:64, columns - LANES :].reshape(FACE, LANES),
    )
    lane = lax.broadcasted_iota(jnp.int32, (FACE, LANES), 1)
    for low_ref, high_ref, ends_ref, to_ref in (
        (keep0_ref, keep3_ref, edges_ref, far_ref),
        (pass0_ref, pass3_ref, others_ref, far_pass_ref),
    ):
        ends = jnp.where(even, ends_ref[0], ends_ref[1])
        turned = pltpu.roll(ends, HALF, axis=1)
        enter = jnp.where(even, low_ref[:, 0:LANES], high_ref[:, columns - LANES :])
        early = rate * (enter + jnp.where(even, ends, turned))
        late = rate * (early + jnp.where(even, turned, ends))
        turned = pltpu.roll(jnp.where(even, late, early), HALF, axis=1)
        to_ref[0] = jnp.where(
            lane < HALF, jnp.where(even, early, turned), jnp.where(even, turned, late)
        )


def ends_kernel(state_ref, far_ref, near_ref, held_ref, low, high, semaphore):
    slices, _, _, columns = state_ref.shape
    copies = [
        pltpu.make_async_copy(
            state_ref.at[:, :, pl.ds(0, 16), pl.ds(0, LANES)], low, semaphore.at[0]
        ),
        pltpu.make_async_copy(
            state_ref.at[:, :, pl.ds(48, 16), pl.ds(columns - LANES, LANES)], high, semaphore.at[1]
        ),
        pltpu.make_async_copy(state_ref, held_ref, semaphore.at[2]),
    ]
    for copy in copies:
        copy.start()
    for copy in copies[:2]:
        copy.wait()
    send(
        [low[item].reshape(FACE, LANES) for item in range(slices)],
        [high[item].reshape(FACE, LANES) for item in range(slices)],
        near_ref,
        far_ref,
    )
    copies[2].wait()


def wave(at, values):
    result = jnp.float32(values[0])
    for k in range(1, len(values)):
        result = jnp.where(at == k, jnp.float32(values[k]), result)
    return result


def first_kernel(total, state_ref, *refs):
    sources = refs[:8]
    out_ref, weights_ref, rim_weights_ref, rate_ref, forcing_ref = refs[8:13]
    neighbor_ref, tags_ref, codes_ref = refs[13:16]
    cos_ref, sin_ref, damping_ref, volume_ref, lifts_ref = refs[16:21]
    blocks, stack, semaphores = refs[21:]
    targets = (
        neighbor_ref, tags_ref, codes_ref, lifts_ref, volume_ref, damping_ref, cos_ref, sin_ref,
    )
    copies = [
        pltpu.make_async_copy(source, target, semaphores.at[k])
        for k, (source, target) in enumerate(zip(sources, targets))
    ]
    for copy in copies:
        copy.start()
    slices, _, columns = state_ref.shape

    def ready():
        for copy in copies[:3]:
            copy.wait()

    def ahead():
        for copy in copies[3:]:
            copy.wait()
        for face in range(6):
            lift = lifts_ref[face].T
            weights_ref[:, FACE * face : FACE * (face + 1)] = lift
            if face < 2:
                rim_weights_ref[face] = lift
        weights_ref[:, 6 * FACE :] = volume_ref[...]

    image = operator(
        state_ref, blocks, stack, weights_ref, neighbor_ref, tags_ref, codes_ref, ready, ahead
    )
    rate_ref[...] = 1.0 / (1.0 + damping_ref[...])
    angles = [2.0 * math.pi * k / total for k in range(total)]
    for item in range(slices):
        at = lax.axis_index("tm") * slices + item
        forcing = wave(at, [math.cos(x) for x in angles]) * cos_ref[...].astype(jnp.float32)
        forcing += wave(at, [math.sin(x) for x in angles]) * sin_ref[...].astype(jnp.float32)
        forcing_ref[item] = forcing
        out_ref[item] = (
            image[:, item * columns : (item + 1) * columns]
            + forcing
            + damping_ref[...] * state_ref[item]
        )


def carry_kernel(
    pieces, part_ref, far_ref, near_ref, rate_ref, rim_weights_ref, neighbor_ref, tags_ref,
    codes_ref, out_ref, *refs
):
    *piece_refs, edges_ref, carry_ref = refs
    slices, rows, columns = part_ref.shape
    count = columns // LANES
    low, high = rim(
        far_ref, near_ref, slices, rim_weights_ref, neighbor_ref, tags_ref, codes_ref, count
    )
    for block in range(count):
        span = slice(block * LANES, (block + 1) * LANES)
        rate = rate_ref[:, span]
        carry = None
        for item in range(slices):
            value = part_ref[item, :, span]
            piece = slice(item * LANES, (item + 1) * LANES)
            if block == 0:
                value = value + low[:, piece]
            if block == count - 1:
                value = value + high[:, piece]
            out_ref[item, :, span] = value
            carry = rate * value if carry is None else rate * (carry + value)
        carry_ref[:, :, span] = carry.reshape(NF, NP**3, LANES)
    if pieces == 1:
        piece_refs[0][...] = carry_ref[...].reshape(rows, columns)
        edges_ref[...] = jnp.zeros_like(edges_ref)
        return
    for part in range(pieces):
        piece_refs[part][...] = carry_ref[:, row_part(part), :].reshape(FACE, columns)
    edges = []
    for item in range(slices):
        first = end_trace(out_ref[item, :, 0:LANES].reshape(NF, NP**3, LANES), 0)
        last = end_trace(out_ref[item, :, columns - LANES :].reshape(NF, NP**3, LANES), 1)
        edges.append((first, last))
    edges_ref[0], edges_ref[1] = packed(*zip(*edges))


def row_part(part):
    half = (lax.axis_index("tm") & 1) ^ (part & 1)
    return pl.ds(pl.multiple_of((half if part < 2 else 3 - half) * 16, 16), 16)


def periodic(carries, factor):
    count = len(carries)
    total = carries[0]
    for k in range(1, count):
        total = carries[k] + factor * total
    power = factor
    for _ in range(count - 1):
        power = power * factor
    entering = [total / (1.0 - power)]
    for k in range(count - 1):
        entering.append(carries[k] + factor * entering[-1])
    return entering


def power(rate_ref, part, slices):
    rate = rate_ref[:, row_part(part), :].reshape(FACE, rate_ref.shape[2])
    factor = rate
    for _ in range(slices - 1):
        factor = factor * rate
    return factor


def ordered(own, other):
    first = (lax.axis_index("tm") & 1) == 0
    return jnp.where(first, own, other), jnp.where(first, other, own)


def pair_kernel(slices, part, own_ref, other_ref, rate_ref, out_ref):
    factor = power(rate_ref, part, slices)
    early, late = ordered(own_ref[...], other_ref[...])
    out_ref[...] = late + factor * early


def enter_kernel(
    slices, part, own_ref, other_ref, here_ref, there_ref, rate_ref, keep_ref, send_ref
):
    factor = power(rate_ref, part, slices)
    square = factor * factor
    early, _ = ordered(own_ref[...], other_ref[...])
    enter = (there_ref[...] + square * here_ref[...]) / (1.0 - square * square)
    later = early + factor * enter
    own, other = ordered(enter, later)
    keep_ref[...] = own
    send_ref[...] = other


def solve_kernel(pieces, *refs):
    piece_refs = refs[:pieces]
    right_ref, rate_ref, state_ref, before_ref, near_ref, *far_refs = refs[pieces:]
    slices, rows, columns = right_ref.shape
    if pieces == 1:
        before_ref[...] = piece_refs[0][...].reshape(before_ref.shape)
    else:
        for part in range(pieces):
            before_ref[:, row_part(part), :] = piece_refs[part][...].reshape(NF, 16, columns)
    rate = rate_ref[...]
    value = before_ref[...].reshape(rows, columns)
    low = []
    high = []
    for item in range(slices):
        value = rate * (value + right_ref[item])
        state_ref[item] = value
        cube = value.reshape(NF, NP**3, columns)
        low.append(cube[:, 0:16, 0:LANES].reshape(FACE, LANES))
        high.append(cube[:, 48:64, columns - LANES :].reshape(FACE, LANES))
    send(low, high, near_ref, *far_refs)


def second_kernel(
    state_ref, before_ref, forcing_ref, weights_ref, neighbor_ref, tags_ref, codes_ref, out_ref,
    result_ref, blocks, stack, semaphore,
):
    slices, _, columns = state_ref.shape
    copy = pltpu.make_async_copy(state_ref, result_ref, semaphore)
    copy.start()
    image = operator(
        state_ref, blocks, stack, weights_ref, neighbor_ref, tags_ref, codes_ref
    )
    for item in range(slices):
        previous = before_ref[...].reshape(state_ref.shape[1:]) if item == 0 else state_ref[item - 1]
        out_ref[item] = (
            image[:, item * columns : (item + 1) * columns]
            + forcing_ref[item]
            + (previous - state_ref[item])
        )
    copy.wait()


def finish_kernel(
    part_ref, far_ref, far_pass_ref, near_ref, rim_weights_ref, neighbor_ref, tags_ref, codes_ref, out_ref,
    held, semaphores,
):
    slices, _, columns = part_ref.shape
    count = columns // LANES
    first = (lax.axis_index("tm") & 1) == 0
    far = jnp.where(first, far_ref[...], far_pass_ref[...])
    low, high = rim(
        far, near_ref, slices, rim_weights_ref, neighbor_ref, tags_ref, codes_ref, count
    )
    copies = []
    for block in range(count):
        span = pl.ds(block * LANES, LANES)
        for item in range(slices):
            value = part_ref[item, :, span]
            piece = slice(item * LANES, (item + 1) * LANES)
            if block == 0:
                value = value + low[:, piece]
            if block == count - 1:
                value = value + high[:, piece]
            held[item, :, span] = value.astype(held.dtype)
        copy = pltpu.make_async_copy(
            held.at[:, :, span], out_ref.at[:, :, span], semaphores.at[block]
        )
        copy.start()
        copies.append(copy)
    for copy in copies:
        copy.wait()


VMEM = pl.BlockSpec(memory_space=pltpu.VMEM)
HBM = pl.BlockSpec(memory_space=pltpu.HBM)


def call(kernel, name, outs, args, scratch=(), flops=0, in_specs=None, out_specs=None):
    size = sum(math.prod(a.shape) * a.dtype.itemsize for a in list(args) + list(outs))
    return pl.pallas_call(
        kernel,
        name=name,
        out_shape=outs,
        in_specs=in_specs or [VMEM] * len(args),
        out_specs=out_specs or [VMEM] * len(outs),
        scratch_shapes=list(scratch),
        compiler_params=pltpu.CompilerParams(vmem_limit_bytes=40 * 2**20),
        cost_estimate=pl.CostEstimate(flops=flops, bytes_accessed=size, transcendentals=0),
    )(*args)


def near_exchange(near):
    pairs = [(i, i + 1) for i in range(0, lax.axis_size("space") - 1, 2)]
    return lax.ppermute(near, "space", pairs + [(j, i) for i, j in pairs])


def far_exchange(far, across=False):
    count = lax.axis_size("space")
    pairs = [(i, (i + 1) % count) for i in range(1, count, 2)]
    pairs += [(j, i) for i, j in pairs]
    if not across:
        return lax.ppermute(far, "space", pairs)
    places = range(lax.axis_size("tm"))
    return lax.ppermute(
        far, ("tm", "space"),
        [(k * count + i, (k ^ 1) * count + j) for k in places for i, j in pairs],
    )


def swapped(value, step):
    count = lax.axis_size("tm")
    return lax.ppermute(value, "tm", [(i, i ^ step) for i in range(count)])


def in_hbm(value):
    return pltpu.with_memory_space_constraint(value, pltpu.HBM)


def local(guess, source_cos, source_sin, damping, volume, lifts, neighbor, tags, codes):
    slices, rows, columns = guess.shape
    devices = lax.axis_size("tm")
    f32, bf16 = jnp.float32, jnp.bfloat16
    shape = jax.ShapeDtypeStruct
    whole = shape((slices, rows, columns), f32)
    plane = shape((rows, columns), f32)
    halo = shape(((slices + 1) // 2, FACE, LANES), f32)
    edge = shape((2, FACE, LANES), f32)
    split_rows = shape((NF, NP**3, columns), f32)
    depth = rows + 6 * FACE
    scratch = [
        pltpu.VMEM((slices * columns // LANES, rows, LANES), f32),
        pltpu.VMEM((depth, 2 * slices * columns), bf16),
    ]
    work = 4 * rows * depth * slices * columns
    end = pltpu.VMEM((slices, NF, NP * NP, LANES), f32)
    share = rows // devices
    pairs = devices == 4 and slices == 2
    pieces = devices if pairs else 1
    piece = shape((rows // pieces, columns), f32)

    cube = guess.reshape(slices, NF, NP**3, columns)
    far, near, held = call(
        ends_kernel, "ends", [halo, halo, shape(cube.shape, f32)], [in_hbm(cube)],
        [end, end, pltpu.SemaphoreType.DMA((3,))], in_specs=[HBM],
    )
    far, near = far_exchange(far), near_exchange(near)
    operands = (
        neighbor, tags, codes, jnp.swapaxes(lifts, 1, 2), volume, damping, source_cos,
        source_sin,
    )
    part, weights, rim_weights, rate, forcing, *tables = call(
        functools.partial(first_kernel, slices * devices), "first",
        [whole, shape((rows, depth), bf16), shape((2, rows, FACE), bf16), plane, whole]
        + [shape(neighbor.shape, jnp.int32)] * 3,
        [held.reshape(guess.shape)] + [in_hbm(operand) for operand in operands],
        [
            pltpu.VMEM(plane.shape, bf16),
            pltpu.VMEM(plane.shape, bf16),
            pltpu.VMEM(plane.shape, f32),
            pltpu.VMEM(volume.shape, bf16),
            pltpu.VMEM((6, FACE, rows), bf16),
            *scratch,
            pltpu.SemaphoreType.DMA((len(operands),)),
        ],
        flops=work, in_specs=[VMEM] + [HBM] * len(operands),
    )
    known, *parts, edges = call(
        functools.partial(carry_kernel, pieces), "carry", [whole] + [piece] * pieces + [edge],
        [part, far, near, rate, rim_weights, *tables], [pltpu.VMEM(split_rows.shape, f32)],
    )
    if pairs:
        around = []
        rates = rate.reshape(split_rows.shape)
        others = [swapped(parts[k + 1], 1) for k in (0, 2)]
        for k in (0, 2):
            (here,) = call(
                functools.partial(pair_kernel, slices, k), "pair", [piece],
                [parts[k], others[k // 2], rates],
            )
            around.append((here, swapped(here, 2)))
        passed = swapped(edges, 1)
        own = parts[::2]
        parts = []
        entering = []
        for k in (0, 2):
            keep, pass_on = call(
                functools.partial(enter_kernel, slices, k), "enter", [piece] * 2,
                [own[k // 2], others[k // 2], *around[k // 2], rates],
            )
            entering += [keep, pass_on]
            parts += [keep, swapped(pass_on, 1)]
        far, far_pass = call(
            spread_kernel, "spread", [halo] * 2, [*entering, edges, passed, rates]
        )
        halos = [far_exchange(far), far_exchange(far_pass, True)]
    else:
        me = lax.axis_index("tm")
        factor = lax.dynamic_slice_in_dim(rate, me * share, share, 0) ** slices
        carries = lax.all_to_all(parts[0], "tm", split_axis=0, concat_axis=0, tiled=True)
        carries = carries.reshape(devices, share, columns)
        back = jnp.concatenate(periodic([carries[k] for k in range(devices)], factor), axis=0)
        parts = [lax.all_to_all(back, "tm", split_axis=0, concat_axis=0, tiled=True)]
    state, before, near, *far = call(
        functools.partial(solve_kernel, pieces), "solve",
        [whole, split_rows, halo] + [halo] * (not pairs), [*parts, known, rate],
    )
    if not pairs:
        halos = [far_exchange(far[0])] * 2
    near = near_exchange(near)
    part, result = call(
        second_kernel, "second", [whole, whole],
        [state, before, forcing, weights, *tables],
        [*scratch, pltpu.SemaphoreType.DMA], flops=work, out_specs=[VMEM, HBM],
    )
    (after,) = call(
        finish_kernel, "finish", [shape(whole.shape, bf16)],
        [part, *halos, near, rim_weights, *tables],
        [pltpu.VMEM(whole.shape, bf16), pltpu.SemaphoreType.DMA((columns // LANES,))],
        out_specs=[HBM],
    )
    return result, after


def solution(mesh):
    column = P(None, ("groups", "space"))
    state = P("tm", None, ("groups", "space"))
    in_specs = (state, column, column, column, P(), P(), column, column, column)
    return jax.shard_map(
        local, mesh=mesh, in_specs=in_specs, out_specs=(state, state), check_vma=False
    )
```

```python
import functools
import math

import jax
import jax.numpy as jnp
from jax import lax
from jax.experimental import pallas as pl
from jax.experimental.pallas import tpu as pltpu
from jax.sharding import PartitionSpec as P

NF = 5
NP = 4
FACE = NF * NP * NP
LANES = 128
HALF = 64


def split(value):
    high = value.astype(jnp.bfloat16)
    low = (value - high.astype(jnp.float32)).astype(jnp.bfloat16)
    return high, low


def end_trace(cube, face):
    rows = cube[:, 0:16] if face == 0 else cube[:, 48:64]
    return rows.reshape(FACE, LANES)


def side_trace(cube, face):
    tiles = cube.reshape(NF, 2, 2, 16, LANES)
    part = tiles[:, :, :, 0:8] if face == 2 else tiles[:, :, :, 8:16]
    even = part[:, :, 0].reshape(FACE // 8, 8, LANES)
    odd = part[:, :, 1].reshape(FACE // 8, 8, LANES)
    lower = lax.broadcasted_iota(jnp.int32, (FACE // 8, 8, LANES), 1) < 4
    if face == 2:
        odd = pltpu.roll(odd, 4, axis=1)
    else:
        even = pltpu.roll(even, 4, axis=1)
    return jnp.where(lower, even, odd).reshape(FACE, LANES)


def lane_index(row):
    return jnp.broadcast_to(row, (FACE, LANES))


def orientation(code):
    swap = (code & 1) == 1
    turn_i = (code & 2) == 2
    turn_j = (code & 4) == 4
    result = []
    for tile in range(2):
        row = lax.broadcasted_iota(jnp.int32, (8, LANES), 0) + 8 * tile
        i, j = row >> 2, row & 3
        i = jnp.where(turn_i, 3 - i, i)
        j = jnp.where(turn_j, 3 - j, j)
        source = jnp.where(swap, j * 4 + i, i * 4 + j)
        result.append((source >= 8, source & 7))
    return result


def oriented(value, plan):
    pieces = []
    for field in range(NF):
        first = value[field * 16 : field * 16 + 8]
        second = value[field * 16 + 8 : field * 16 + 16]
        for upper, sub in plan:
            pick = functools.partial(jnp.take_along_axis, axis=0, mode="promise_in_bounds")
            pieces.append(jnp.where(upper, pick(second, sub), pick(first, sub)))
    return jnp.concatenate(pieces, axis=0)


def gather_lanes(value, row):
    return jnp.take_along_axis(value, lane_index(row), axis=1, mode="promise_in_bounds")


def operator(
    state, blocks, stack, weights_ref, neighbor_ref, tags_ref, codes_ref,
    ready=lambda: None, ahead=lambda: None,
):
    slices, rows, columns = state.shape
    count = columns // LANES
    wide = slices * columns
    base = 6 * FACE
    lane = lax.broadcasted_iota(jnp.int32, (FACE, LANES), 1)
    for item in range(slices):
        for block in range(count):
            n = item * count + block
            value = state[item, :, block * LANES : (block + 1) * LANES]
            blocks[n] = value
            high, low = split(value)
            stack[base:, n * LANES : (n + 1) * LANES] = high
            stack[base:, wide + n * LANES : wide + (n + 1) * LANES] = low
    ready()
    for item in range(slices):
        cubes = []
        turned = []
        for block in range(count):
            cube = blocks[item * count + block].reshape(NF, NP**3, LANES)
            cubes.append(cube)
            turned.append(
                [pltpu.roll(end_trace(cube, face), HALF, axis=1) for face in range(2)]
            )
        zero = jnp.zeros((FACE, LANES), jnp.float32)
        for block in range(count):
            n = item * count + block
            cube = cubes[block]
            before = turned[block - 1][1] if block > 0 else zero
            after = turned[block + 1][0] if block + 1 < count else zero
            ends = [end_trace(cube, 0), end_trace(cube, 1)]
            sides = [side_trace(cube, 2), side_trace(cube, 3)]
            tops = [
                blocks[n, pl.ds(0, FACE, stride=4), :],
                blocks[n, pl.ds(3, FACE, stride=4), :],
            ]
            mine = ends + sides + tops
            across = [
                jnp.where(lane < HALF, before, turned[block][1]),
                jnp.where(lane < HALF, turned[block][0], after),
                sides[1],
                sides[0],
                tops[1],
                tops[0],
            ]
            for face in range(6):
                span = slice(block * LANES, (block + 1) * LANES)
                target = neighbor_ref[face : face + 1, span]
                kind = tags_ref[face : face + 1, span]
                code = codes_ref[face : face + 1, span]
                if face < 2:
                    target = target + HALF
                plan = orientation(code)
                taken = oriented(gather_lanes(across[face], target & (LANES - 1)), plan)
                keep = jnp.where((kind == 1) | (kind == 3), 1.0, 0.0)
                flip = jnp.where(kind == 1, -1.0, keep)
                axis = 1 + face // 2
                inner = []
                for field in range(NF):
                    own = mine[face][field * 16 : (field + 1) * 16]
                    inner.append(own * (flip if field == axis else keep))
                seen = jnp.where(kind == 0, taken, jnp.concatenate(inner, axis=0))
                high, low = split(seen)
                place = FACE * face
                stack[place : place + FACE, n * LANES : (n + 1) * LANES] = high
                stack[place : place + FACE, wide + n * LANES : wide + (n + 1) * LANES] = low
    ahead()
    image = jnp.dot(weights_ref[...], stack[:, 0:wide], preferred_element_type=jnp.float32)
    return image + jnp.dot(
        weights_ref[...], stack[:, wide:], preferred_element_type=jnp.float32
    )


def even_place():
    return (lax.axis_index("space") & 1) == 0


def rim(far, near, slices, rim_weights_ref, neighbor_ref, tags_ref, codes_ref, count):
    lane = lax.broadcasted_iota(jnp.int32, (1, LANES), 1)
    even = even_place()
    result = []
    for face in range(2):
        block = 0 if face == 0 else count - 1
        span = slice(block * LANES, (block + 1) * LANES)
        target = neighbor_ref[face : face + 1, span] & (HALF - 1)
        inside = lane < HALF if face == 0 else lane >= HALF
        use = (tags_ref[face : face + 1, span] == 0) & inside
        plan = orientation(codes_ref[face : face + 1, span])
        pieces = []
        for item in range(slices):
            a, b = (far, near) if face == 0 else (near, far)
            halo = jnp.where(even, a[item // 2], b[item // 2])
            taken = gather_lanes(halo, target + HALF * (item % 2))
            pieces.append(split(jnp.where(use, oriented(taken, plan), 0.0)))
        both = jnp.concatenate([p[0] for p in pieces] + [p[1] for p in pieces], axis=1)
        product = jnp.dot(rim_weights_ref[face], both, preferred_element_type=jnp.float32)
        wide = slices * LANES
        result.append(product[:, :wide] + product[:, wide:])
    return result


def packed(low, high):
    lane = lax.broadcasted_iota(jnp.int32, (FACE, LANES), 1)
    first = jnp.where(lane < HALF, low[0], pltpu.roll(low[1], HALF, axis=1))
    last = jnp.where(lane < HALF, pltpu.roll(high[0], HALF, axis=1), high[1])
    return first, last


def send(low, high, near_ref, far_ref=None):
    slices = len(low)
    even = even_place()
    for item in range(0, slices, 2):
        other = min(item + 1, slices - 1)
        first, last = packed([low[item], low[other]], [high[item], high[other]])
        near_ref[item // 2] = jnp.where(even, last, first)
        if far_ref is not None:
            far_ref[item // 2] = jnp.where(even, first, last)


def spread_kernel(
    keep0_ref, pass0_ref, keep3_ref, pass3_ref, edges_ref, others_ref, rate_ref, far_pass_ref,
    far_ref,
):
    columns = keep0_ref.shape[1]
    even = even_place()
    rate = jnp.where(
        even,
        rate_ref[:, 0:16, 0:LANES].reshape(FACE, LANES),
        rate_ref[:, 48:64, columns - LANES :].reshape(FACE, LANES),
    )
    lane = lax.broadcasted_iota(jnp.int32, (FACE, LANES), 1)
    for low_ref, high_ref, ends_ref, to_ref in (
        (keep0_ref, keep3_ref, edges_ref, far_ref),
        (pass0_ref, pass3_ref, others_ref, far_pass_ref),
    ):
        ends = jnp.where(even, ends_ref[0], ends_ref[1])
        turned = pltpu.roll(ends, HALF, axis=1)
        enter = jnp.where(even, low_ref[:, 0:LANES], high_ref[:, columns - LANES :])
        early = rate * (enter + jnp.where(even, ends, turned))
        late = rate * (early + jnp.where(even, turned, ends))
        turned = pltpu.roll(jnp.where(even, late, early), HALF, axis=1)
        to_ref[0] = jnp.where(
            lane < HALF, jnp.where(even, early, turned), jnp.where(even, turned, late)
        )


def ends_kernel(state_ref, far_ref, near_ref, held_ref, low, high, semaphore):
    slices, _, _, columns = state_ref.shape
    copies = [
        pltpu.make_async_copy(
            state_ref.at[:, :, pl.ds(0, 16), pl.ds(0, LANES)], low, semaphore.at[0]
        ),
        pltpu.make_async_copy(
            state_ref.at[:, :, pl.ds(48, 16), pl.ds(columns - LANES, LANES)], high, semaphore.at[1]
        ),
        pltpu.make_async_copy(state_ref, held_ref, semaphore.at[2]),
    ]
    for copy in copies:
        copy.start()
    for copy in copies[:2]:
        copy.wait()
    send(
        [low[item].reshape(FACE, LANES) for item in range(slices)],
        [high[item].reshape(FACE, LANES) for item in range(slices)],
        near_ref,
        far_ref,
    )
    copies[2].wait()


def wave(at, values):
    result = jnp.float32(values[0])
    for k in range(1, len(values)):
        result = jnp.where(at == k, jnp.float32(values[k]), result)
    return result


def first_kernel(total, state_ref, *refs):
    sources = refs[:8]
    out_ref, weights_ref, rim_weights_ref, rate_ref, forcing_ref = refs[8:13]
    neighbor_ref, tags_ref, codes_ref = refs[13:16]
    cos_ref, sin_ref, damping_ref, volume_ref, lifts_ref = refs[16:21]
    blocks, stack, semaphores = refs[21:]
    targets = (
        neighbor_ref, tags_ref, codes_ref, lifts_ref, volume_ref, damping_ref, cos_ref, sin_ref,
    )
    copies = [
        pltpu.make_async_copy(source, target, semaphores.at[k])
        for k, (source, target) in enumerate(zip(sources, targets))
    ]
    for copy in copies:
        copy.start()
    slices, _, columns = state_ref.shape

    def ready():
        for copy in copies[:3]:
            copy.wait()

    def ahead():
        for copy in copies[3:]:
            copy.wait()
        for face in range(6):
            lift = lifts_ref[face].T
            weights_ref[:, FACE * face : FACE * (face + 1)] = lift
            if face < 2:
                rim_weights_ref[face] = lift
        weights_ref[:, 6 * FACE :] = volume_ref[...]

    image = operator(
        state_ref, blocks, stack, weights_ref, neighbor_ref, tags_ref, codes_ref, ready, ahead
    )
    rate_ref[...] = 1.0 / (1.0 + damping_ref[...])
    angles = [2.0 * math.pi * k / total for k in range(total)]
    for item in range(slices):
        at = lax.axis_index("tm") * slices + item
        forcing = wave(at, [math.cos(x) for x in angles]) * cos_ref[...].astype(jnp.float32)
        forcing += wave(at, [math.sin(x) for x in angles]) * sin_ref[...].astype(jnp.float32)
        forcing_ref[item] = forcing
        out_ref[item] = (
            image[:, item * columns : (item + 1) * columns]
            + forcing
            + damping_ref[...] * state_ref[item]
        )


def carry_kernel(
    pieces, part_ref, far_ref, near_ref, rate_ref, rim_weights_ref, neighbor_ref, tags_ref,
    codes_ref, out_ref, *refs
):
    *piece_refs, edges_ref, carry_ref = refs
    slices, rows, columns = part_ref.shape
    count = columns // LANES
    low, high = rim(
        far_ref, near_ref, slices, rim_weights_ref, neighbor_ref, tags_ref, codes_ref, count
    )
    for block in range(count):
        span = slice(block * LANES, (block + 1) * LANES)
        rate = rate_ref[:, span]
        carry = None
        for item in range(slices):
            value = part_ref[item, :, span]
            piece = slice(item * LANES, (item + 1) * LANES)
            if block == 0:
                value = value + low[:, piece]
            if block == count - 1:
                value = value + high[:, piece]
            out_ref[item, :, span] = value
            carry = rate * value if carry is None else rate * (carry + value)
        carry_ref[:, :, span] = carry.reshape(NF, NP**3, LANES)
    if pieces == 1:
        piece_refs[0][...] = carry_ref[...].reshape(rows, columns)
        edges_ref[...] = jnp.zeros_like(edges_ref)
        return
    for part in range(pieces):
        piece_refs[part][...] = carry_ref[:, row_part(part), :].reshape(FACE, columns)
    edges = []
    for item in range(slices):
        first = end_trace(out_ref[item, :, 0:LANES].reshape(NF, NP**3, LANES), 0)
        last = end_trace(out_ref[item, :, columns - LANES :].reshape(NF, NP**3, LANES), 1)
        edges.append((first, last))
    edges_ref[0], edges_ref[1] = packed(*zip(*edges))


def row_part(part):
    half = (lax.axis_index("tm") & 1) ^ (part & 1)
    return pl.ds(pl.multiple_of((half if part < 2 else 3 - half) * 16, 16), 16)


def periodic(carries, factor):
    count = len(carries)
    total = carries[0]
    for k in range(1, count):
        total = carries[k] + factor * total
    power = factor
    for _ in range(count - 1):
        power = power * factor
    entering = [total / (1.0 - power)]
    for k in range(count - 1):
        entering.append(carries[k] + factor * entering[-1])
    return entering


def power(rate_ref, part, slices):
    rate = rate_ref[:, row_part(part), :].reshape(FACE, rate_ref.shape[2])
    factor = rate
    for _ in range(slices - 1):
        factor = factor * rate
    return factor


def ordered(own, other):
    first = (lax.axis_index("tm") & 1) == 0
    return jnp.where(first, own, other), jnp.where(first, other, own)


def pair_kernel(slices, part, own_ref, other_ref, rate_ref, out_ref):
    factor = power(rate_ref, part, slices)
    early, late = ordered(own_ref[...], other_ref[...])
    out_ref[...] = late + factor * early


def enter_kernel(
    slices, part, own_ref, other_ref, here_ref, there_ref, rate_ref, keep_ref, send_ref
):
    factor = power(rate_ref, part, slices)
    square = factor * factor
    early, _ = ordered(own_ref[...], other_ref[...])
    enter = (there_ref[...] + square * here_ref[...]) / (1.0 - square * square)
    later = early + factor * enter
    own, other = ordered(enter, later)
    keep_ref[...] = own
    send_ref[...] = other


def solve_kernel(pieces, *refs):
    piece_refs = refs[:pieces]
    right_ref, rate_ref, state_ref, before_ref, near_ref, *far_refs = refs[pieces:]
    slices, rows, columns = right_ref.shape
    if pieces == 1:
        before_ref[...] = piece_refs[0][...].reshape(before_ref.shape)
    else:
        for part in range(pieces):
            before_ref[:, row_part(part), :] = piece_refs[part][...].reshape(NF, 16, columns)
    rate = rate_ref[...]
    value = before_ref[...].reshape(rows, columns)
    low = []
    high = []
    for item in range(slices):
        value = rate * (value + right_ref[item])
        state_ref[item] = value
        cube = value.reshape(NF, NP**3, columns)
        low.append(cube[:, 0:16, 0:LANES].reshape(FACE, LANES))
        high.append(cube[:, 48:64, columns - LANES :].reshape(FACE, LANES))
    send(low, high, near_ref, *far_refs)


def second_kernel(
    state_ref, before_ref, forcing_ref, weights_ref, neighbor_ref, tags_ref, codes_ref, out_ref,
    result_ref, blocks, stack, semaphore,
):
    slices, _, columns = state_ref.shape
    copy = pltpu.make_async_copy(state_ref, result_ref, semaphore)
    copy.start()
    image = operator(
        state_ref, blocks, stack, weights_ref, neighbor_ref, tags_ref, codes_ref
    )
    for item in range(slices):
        previous = before_ref[...].reshape(state_ref.shape[1:]) if item == 0 else state_ref[item - 1]
        out_ref[item] = (
            image[:, item * columns : (item + 1) * columns]
            + forcing_ref[item]
            + (previous - state_ref[item])
        )
    copy.wait()


def finish_kernel(
    part_ref, far_pass_ref, far_ref, near_ref, rim_weights_ref, neighbor_ref, tags_ref, codes_ref, out_ref,
    held, semaphores,
):
    slices, _, columns = part_ref.shape
    count = columns // LANES
    first = (lax.axis_index("tm") & 1) == 0
    far = jnp.where(first, far_ref[...], far_pass_ref[...])
    low, high = rim(
        far, near_ref, slices, rim_weights_ref, neighbor_ref, tags_ref, codes_ref, count
    )
    copies = []
    for block in range(count):
        span = pl.ds(block * LANES, LANES)
        for item in range(slices):
            value = part_ref[item, :, span]
            piece = slice(item * LANES, (item + 1) * LANES)
            if block == 0:
                value = value + low[:, piece]
            if block == count - 1:
                value = value + high[:, piece]
            held[item, :, span] = value.astype(held.dtype)
        copy = pltpu.make_async_copy(
            held.at[:, :, span], out_ref.at[:, :, span], semaphores.at[block]
        )
        copy.start()
        copies.append(copy)
    for copy in copies:
        copy.wait()


VMEM = pl.BlockSpec(memory_space=pltpu.VMEM)
HBM = pl.BlockSpec(memory_space=pltpu.HBM)


def call(kernel, name, outs, args, scratch=(), flops=0, in_specs=None, out_specs=None):
    size = sum(math.prod(a.shape) * a.dtype.itemsize for a in list(args) + list(outs))
    return pl.pallas_call(
        kernel,
        name=name,
        out_shape=outs,
        in_specs=in_specs or [VMEM] * len(args),
        out_specs=out_specs or [VMEM] * len(outs),
        scratch_shapes=list(scratch),
        compiler_params=pltpu.CompilerParams(vmem_limit_bytes=40 * 2**20),
        cost_estimate=pl.CostEstimate(flops=flops, bytes_accessed=size, transcendentals=0),
    )(*args)


def near_exchange(near):
    pairs = [(i, i + 1) for i in range(0, lax.axis_size("space") - 1, 2)]
    return lax.ppermute(near, "space", pairs + [(j, i) for i, j in pairs])


def far_exchange(far, across=False):
    count = lax.axis_size("space")
    pairs = [(i, (i + 1) % count) for i in range(1, count, 2)]
    pairs += [(j, i) for i, j in pairs]
    if not across:
        return lax.ppermute(far, "space", pairs)
    places = range(lax.axis_size("tm"))
    return lax.ppermute(
        far, ("tm", "space"),
        [(k * count + i, (k ^ 1) * count + j) for k in places for i, j in pairs],
    )


def swapped(value, step):
    count = lax.axis_size("tm")
    return lax.ppermute(value, "tm", [(i, i ^ step) for i in range(count)])


def in_hbm(value):
    return pltpu.with_memory_space_constraint(value, pltpu.HBM)


def local(guess, source_cos, source_sin, damping, volume, lifts, neighbor, tags, codes):
    slices, rows, columns = guess.shape
    devices = lax.axis_size("tm")
    f32, bf16 = jnp.float32, jnp.bfloat16
    shape = jax.ShapeDtypeStruct
    whole = shape((slices, rows, columns), f32)
    plane = shape((rows, columns), f32)
    halo = shape(((slices + 1) // 2, FACE, LANES), f32)
    edge = shape((2, FACE, LANES), f32)
    split_rows = shape((NF, NP**3, columns), f32)
    depth = rows + 6 * FACE
    scratch = [
        pltpu.VMEM((slices * columns // LANES, rows, LANES), f32),
        pltpu.VMEM((depth, 2 * slices * columns), bf16),
    ]
    work = 4 * rows * depth * slices * columns
    end = pltpu.VMEM((slices, NF, NP * NP, LANES), f32)
    share = rows // devices
    pairs = devices == 4 and slices == 2
    pieces = devices if pairs else 1
    piece = shape((rows // pieces, columns), f32)

    cube = guess.reshape(slices, NF, NP**3, columns)
    far, near, held = call(
        ends_kernel, "ends", [halo, halo, shape(cube.shape, f32)], [in_hbm(cube)],
        [end, end, pltpu.SemaphoreType.DMA((3,))], in_specs=[HBM],
    )
    far, near = far_exchange(far), near_exchange(near)
    operands = (
        neighbor, tags, codes, jnp.swapaxes(lifts, 1, 2), volume, damping, source_cos,
        source_sin,
    )
    part, weights, rim_weights, rate, forcing, *tables = call(
        functools.partial(first_kernel, slices * devices), "first",
        [whole, shape((rows, depth), bf16), shape((2, rows, FACE), bf16), plane, whole]
        + [shape(neighbor.shape, jnp.int32)] * 3,
        [held.reshape(guess.shape)] + [in_hbm(operand) for operand in operands],
        [
            pltpu.VMEM(plane.shape, bf16),
            pltpu.VMEM(plane.shape, bf16),
            pltpu.VMEM(plane.shape, f32),
            pltpu.VMEM(volume.shape, bf16),
            pltpu.VMEM((6, FACE, rows), bf16),
            *scratch,
            pltpu.SemaphoreType.DMA((len(operands),)),
        ],
        flops=work, in_specs=[VMEM] + [HBM] * len(operands),
    )
    known, *parts, edges = call(
        functools.partial(carry_kernel, pieces), "carry", [whole] + [piece] * pieces + [edge],
        [part, far, near, rate, rim_weights, *tables], [pltpu.VMEM(split_rows.shape, f32)],
    )
    if pairs:
        around = []
        rates = rate.reshape(split_rows.shape)
        others = [swapped(parts[k + 1], 1) for k in (0, 2)]
        for k in (0, 2):
            (here,) = call(
                functools.partial(pair_kernel, slices, k), "pair", [piece],
                [parts[k], others[k // 2], rates],
            )
            around.append((here, swapped(here, 2)))
        passed = swapped(edges, 1)
        own = parts[::2]
        parts = []
        entering = []
        for k in (0, 2):
            keep, pass_on = call(
                functools.partial(enter_kernel, slices, k), "enter", [piece] * 2,
                [own[k // 2], others[k // 2], *around[k // 2], rates],
            )
            entering += [keep, pass_on]
            parts += [keep, swapped(pass_on, 1)]
        far_pass, far = call(
            spread_kernel, "spread", [halo] * 2, [*entering, edges, passed, rates]
        )
        halos = [far_exchange(far_pass, True), far_exchange(far)]
    else:
        me = lax.axis_index("tm")
        factor = lax.dynamic_slice_in_dim(rate, me * share, share, 0) ** slices
        carries = lax.all_to_all(parts[0], "tm", split_axis=0, concat_axis=0, tiled=True)
        carries = carries.reshape(devices, share, columns)
        back = jnp.concatenate(periodic([carries[k] for k in range(devices)], factor), axis=0)
        parts = [lax.all_to_all(back, "tm", split_axis=0, concat_axis=0, tiled=True)]
    state, before, near, *far = call(
        functools.partial(solve_kernel, pieces), "solve",
        [whole, split_rows, halo] + [halo] * (not pairs), [*parts, known, rate],
    )
    if not pairs:
        halos = [far_exchange(far[0])] * 2
    near = near_exchange(near)
    part, result = call(
        second_kernel, "second", [whole, whole],
        [state, before, forcing, weights, *tables],
        [*scratch, pltpu.SemaphoreType.DMA], flops=work, out_specs=[VMEM, HBM],
    )
    (after,) = call(
        finish_kernel, "finish", [shape(whole.shape, bf16)],
        [part, *halos, near, rim_weights, *tables],
        [pltpu.VMEM(whole.shape, bf16), pltpu.SemaphoreType.DMA((columns // LANES,))],
        out_specs=[HBM],
    )
    return result, after


def solution(mesh):
    column = P(None, ("groups", "space"))
    state = P("tm", None, ("groups", "space"))
    in_specs = (state, column, column, column, P(), P(), column, column, column)
    return jax.shard_map(
        local, mesh=mesh, in_specs=in_specs, out_specs=(state, state), check_vma=False
    )
```

```python
import functools
import math

import jax
import jax.numpy as jnp
from jax import lax
from jax.experimental import pallas as pl
from jax.experimental.pallas import tpu as pltpu
from jax.sharding import PartitionSpec as P

NF = 5
NP = 4
FACE = NF * NP * NP
LANES = 128
HALF = 64


def split(value):
    high = value.astype(jnp.bfloat16)
    low = (value - high.astype(jnp.float32)).astype(jnp.bfloat16)
    return high, low


def end_trace(cube, face):
    rows = cube[:, 0:16] if face == 0 else cube[:, 48:64]
    return rows.reshape(FACE, LANES)


def side_trace(cube, face):
    tiles = cube.reshape(NF, 2, 2, 16, LANES)
    part = tiles[:, :, :, 0:8] if face == 2 else tiles[:, :, :, 8:16]
    even = part[:, :, 0].reshape(FACE // 8, 8, LANES)
    odd = part[:, :, 1].reshape(FACE // 8, 8, LANES)
    lower = lax.broadcasted_iota(jnp.int32, (FACE // 8, 8, LANES), 1) < 4
    if face == 2:
        odd = pltpu.roll(odd, 4, axis=1)
    else:
        even = pltpu.roll(even, 4, axis=1)
    return jnp.where(lower, even, odd).reshape(FACE, LANES)


def lane_index(row):
    return jnp.broadcast_to(row, (FACE, LANES))


def orientation(code):
    swap = (code & 1) == 1
    turn_i = (code & 2) == 2
    turn_j = (code & 4) == 4
    result = []
    for tile in range(2):
        row = lax.broadcasted_iota(jnp.int32, (8, LANES), 0) + 8 * tile
        i, j = row >> 2, row & 3
        i = jnp.where(turn_i, 3 - i, i)
        j = jnp.where(turn_j, 3 - j, j)
        source = jnp.where(swap, j * 4 + i, i * 4 + j)
        result.append((source >= 8, source & 7))
    return result


def oriented(value, plan):
    pieces = []
    for field in range(NF):
        first = value[field * 16 : field * 16 + 8]
        second = value[field * 16 + 8 : field * 16 + 16]
        for upper, sub in plan:
            pick = functools.partial(jnp.take_along_axis, axis=0, mode="promise_in_bounds")
            pieces.append(jnp.where(upper, pick(second, sub), pick(first, sub)))
    return jnp.concatenate(pieces, axis=0)


def gather_lanes(value, row):
    return jnp.take_along_axis(value, lane_index(row), axis=1, mode="promise_in_bounds")


def operator(
    state, blocks, stack, weights_ref, neighbor_ref, tags_ref, codes_ref,
    ready=lambda: None, ahead=lambda: None,
):
    slices, rows, columns = state.shape
    count = columns // LANES
    wide = slices * columns
    base = 6 * FACE
    lane = lax.broadcasted_iota(jnp.int32, (FACE, LANES), 1)
    for item in range(slices):
        for block in range(count):
            n = item * count + block
            value = state[item, :, block * LANES : (block + 1) * LANES]
            blocks[n] = value
            high, low = split(value)
            stack[base:, n * LANES : (n + 1) * LANES] = high
            stack[base:, wide + n * LANES : wide + (n + 1) * LANES] = low
    ready()
    for item in range(slices):
        cubes = []
        turned = []
        for block in range(count):
            cube = blocks[item * count + block].reshape(NF, NP**3, LANES)
            cubes.append(cube)
            turned.append(
                [pltpu.roll(end_trace(cube, face), HALF, axis=1) for face in range(2)]
            )
        zero = jnp.zeros((FACE, LANES), jnp.float32)
        for block in range(count):
            n = item * count + block
            cube = cubes[block]
            before = turned[block - 1][1] if block > 0 else zero
            after = turned[block + 1][0] if block + 1 < count else zero
            ends = [end_trace(cube, 0), end_trace(cube, 1)]
            sides = [side_trace(cube, 2), side_trace(cube, 3)]
            tops = [
                blocks[n, pl.ds(0, FACE, stride=4), :],
                blocks[n, pl.ds(3, FACE, stride=4), :],
            ]
            mine = ends + sides + tops
            across = [
                jnp.where(lane < HALF, before, turned[block][1]),
                jnp.where(lane < HALF, turned[block][0], after),
                sides[1],
                sides[0],
                tops[1],
                tops[0],
            ]
            for face in range(6):
                span = slice(block * LANES, (block + 1) * LANES)
                target = neighbor_ref[face : face + 1, span]
                kind = tags_ref[face : face + 1, span]
                code = codes_ref[face : face + 1, span]
                if face < 2:
                    target = target + HALF
                plan = orientation(code)
                taken = oriented(gather_lanes(across[face], target & (LANES - 1)), plan)
                keep = jnp.where((kind == 1) | (kind == 3), 1.0, 0.0)
                flip = jnp.where(kind == 1, -1.0, keep)
                axis = 1 + face // 2
                inner = []
                for field in range(NF):
                    own = mine[face][field * 16 : (field + 1) * 16]
                    inner.append(own * (flip if field == axis else keep))
                seen = jnp.where(kind == 0, taken, jnp.concatenate(inner, axis=0))
                high, low = split(seen)
                place = FACE * face
                stack[place : place + FACE, n * LANES : (n + 1) * LANES] = high
                stack[place : place + FACE, wide + n * LANES : wide + (n + 1) * LANES] = low
    ahead()
    image = jnp.dot(weights_ref[...], stack[:, 0:wide], preferred_element_type=jnp.float32)
    return image + jnp.dot(
        weights_ref[...], stack[:, wide:], preferred_element_type=jnp.float32
    )


def even_place():
    return (lax.axis_index("space") & 1) == 0


def rim(far, near, slices, rim_weights_ref, neighbor_ref, tags_ref, codes_ref, count):
    lane = lax.broadcasted_iota(jnp.int32, (1, LANES), 1)
    even = even_place()
    result = []
    for face in range(2):
        block = 0 if face == 0 else count - 1
        span = slice(block * LANES, (block + 1) * LANES)
        target = neighbor_ref[face : face + 1, span] & (HALF - 1)
        inside = lane < HALF if face == 0 else lane >= HALF
        use = (tags_ref[face : face + 1, span] == 0) & inside
        plan = orientation(codes_ref[face : face + 1, span])
        pieces = []
        for item in range(slices):
            a, b = (far, near) if face == 0 else (near, far)
            halo = jnp.where(even, a[item // 2], b[item // 2])
            taken = gather_lanes(halo, target + HALF * (item % 2))
            pieces.append(split(jnp.where(use, oriented(taken, plan), 0.0)))
        both = jnp.concatenate([p[0] for p in pieces] + [p[1] for p in pieces], axis=1)
        middle = rim_weights_ref.shape[1] // 2
        product = jnp.concatenate(
            [
                jnp.dot(rim_weights_ref[face, part], both, preferred_element_type=jnp.float32)
                for part in (slice(0, middle), slice(middle, 2 * middle))
            ],
            axis=0,
        )
        wide = slices * LANES
        result.append(product[:, :wide] + product[:, wide:])
    return result


def packed(low, high):
    lane = lax.broadcasted_iota(jnp.int32, (FACE, LANES), 1)
    first = jnp.where(lane < HALF, low[0], pltpu.roll(low[1], HALF, axis=1))
    last = jnp.where(lane < HALF, pltpu.roll(high[0], HALF, axis=1), high[1])
    return first, last


def send(low, high, near_ref, far_ref=None):
    slices = len(low)
    even = even_place()
    for item in range(0, slices, 2):
        other = min(item + 1, slices - 1)
        first, last = packed([low[item], low[other]], [high[item], high[other]])
        near_ref[item // 2] = jnp.where(even, last, first)
        if far_ref is not None:
            far_ref[item // 2] = jnp.where(even, first, last)


def spread_kernel(
    keep0_ref, pass0_ref, keep3_ref, pass3_ref, edges_ref, others_ref, rate_ref, far_pass_ref,
    far_ref,
):
    columns = keep0_ref.shape[1]
    even = even_place()
    rate = jnp.where(
        even,
        rate_ref[:, 0:16, 0:LANES].reshape(FACE, LANES),
        rate_ref[:, 48:64, columns - LANES :].reshape(FACE, LANES),
    )
    lane = lax.broadcasted_iota(jnp.int32, (FACE, LANES), 1)
    for low_ref, high_ref, ends_ref, to_ref in (
        (keep0_ref, keep3_ref, edges_ref, far_ref),
        (pass0_ref, pass3_ref, others_ref, far_pass_ref),
    ):
        ends = jnp.where(even, ends_ref[0], ends_ref[1])
        turned = pltpu.roll(ends, HALF, axis=1)
        enter = jnp.where(even, low_ref[:, 0:LANES], high_ref[:, columns - LANES :])
        early = rate * (enter + jnp.where(even, ends, turned))
        late = rate * (early + jnp.where(even, turned, ends))
        turned = pltpu.roll(jnp.where(even, late, early), HALF, axis=1)
        to_ref[0] = jnp.where(
            lane < HALF, jnp.where(even, early, turned), jnp.where(even, turned, late)
        )


def ends_kernel(state_ref, far_ref, near_ref, held_ref, low, high, semaphore):
    slices, _, _, columns = state_ref.shape
    copies = [
        pltpu.make_async_copy(
            state_ref.at[:, :, pl.ds(0, 16), pl.ds(0, LANES)], low, semaphore.at[0]
        ),
        pltpu.make_async_copy(
            state_ref.at[:, :, pl.ds(48, 16), pl.ds(columns - LANES, LANES)], high, semaphore.at[1]
        ),
        pltpu.make_async_copy(state_ref, held_ref, semaphore.at[2]),
    ]
    for copy in copies:
        copy.start()
    for copy in copies[:2]:
        copy.wait()
    send(
        [low[item].reshape(FACE, LANES) for item in range(slices)],
        [high[item].reshape(FACE, LANES) for item in range(slices)],
        near_ref,
        far_ref,
    )
    copies[2].wait()


def wave(at, values):
    result = jnp.float32(values[0])
    for k in range(1, len(values)):
        result = jnp.where(at == k, jnp.float32(values[k]), result)
    return result


def first_kernel(total, state_ref, *refs):
    sources = refs[:8]
    out_ref, weights_ref, rim_weights_ref, rate_ref, forcing_ref = refs[8:13]
    neighbor_ref, tags_ref, codes_ref = refs[13:16]
    cos_ref, sin_ref, damping_ref, volume_ref, lifts_ref = refs[16:21]
    blocks, stack, semaphores = refs[21:]
    targets = (
        neighbor_ref, tags_ref, codes_ref, lifts_ref, volume_ref, damping_ref, cos_ref, sin_ref,
    )
    copies = [
        pltpu.make_async_copy(source, target, semaphores.at[k])
        for k, (source, target) in enumerate(zip(sources, targets))
    ]
    for copy in copies:
        copy.start()
    slices, _, columns = state_ref.shape

    def ready():
        for copy in copies[:3]:
            copy.wait()

    def ahead():
        for copy in copies[3:]:
            copy.wait()
        for face in range(6):
            lift = lifts_ref[face].T
            weights_ref[:, FACE * face : FACE * (face + 1)] = lift
            if face < 2:
                rim_weights_ref[face] = lift
        weights_ref[:, 6 * FACE :] = volume_ref[...]

    image = operator(
        state_ref, blocks, stack, weights_ref, neighbor_ref, tags_ref, codes_ref, ready, ahead
    )
    rate_ref[...] = 1.0 / (1.0 + damping_ref[...])
    angles = [2.0 * math.pi * k / total for k in range(total)]
    for item in range(slices):
        at = lax.axis_index("tm") * slices + item
        forcing = wave(at, [math.cos(x) for x in angles]) * cos_ref[...].astype(jnp.float32)
        forcing += wave(at, [math.sin(x) for x in angles]) * sin_ref[...].astype(jnp.float32)
        forcing_ref[item] = forcing
        out_ref[item] = (
            image[:, item * columns : (item + 1) * columns]
            + forcing
            + damping_ref[...] * state_ref[item]
        )


def carry_kernel(
    pieces, part_ref, far_ref, near_ref, rate_ref, rim_weights_ref, neighbor_ref, tags_ref,
    codes_ref, out_ref, *refs
):
    *piece_refs, edges_ref, carry_ref = refs
    slices, rows, columns = part_ref.shape
    count = columns // LANES
    low, high = rim(
        far_ref, near_ref, slices, rim_weights_ref, neighbor_ref, tags_ref, codes_ref, count
    )
    for block in range(count):
        span = slice(block * LANES, (block + 1) * LANES)
        rate = rate_ref[:, span]
        carry = None
        for item in range(slices):
            value = part_ref[item, :, span]
            piece = slice(item * LANES, (item + 1) * LANES)
            if block == 0:
                value = value + low[:, piece]
            if block == count - 1:
                value = value + high[:, piece]
            out_ref[item, :, span] = value
            carry = rate * value if carry is None else rate * (carry + value)
        carry_ref[:, :, span] = carry.reshape(NF, NP**3, LANES)
    if pieces == 1:
        piece_refs[0][...] = carry_ref[...].reshape(rows, columns)
        edges_ref[...] = jnp.zeros_like(edges_ref)
        return
    for part in range(pieces):
        piece_refs[part][...] = carry_ref[:, row_part(part), :].reshape(FACE, columns)
    edges = []
    for item in range(slices):
        first = end_trace(out_ref[item, :, 0:LANES].reshape(NF, NP**3, LANES), 0)
        last = end_trace(out_ref[item, :, columns - LANES :].reshape(NF, NP**3, LANES), 1)
        edges.append((first, last))
    edges_ref[0], edges_ref[1] = packed(*zip(*edges))


def row_part(part):
    half = (lax.axis_index("tm") & 1) ^ (part & 1)
    return pl.ds(pl.multiple_of((half if part < 2 else 3 - half) * 16, 16), 16)


def periodic(carries, factor):
    count = len(carries)
    total = carries[0]
    for k in range(1, count):
        total = carries[k] + factor * total
    power = factor
    for _ in range(count - 1):
        power = power * factor
    entering = [total / (1.0 - power)]
    for k in range(count - 1):
        entering.append(carries[k] + factor * entering[-1])
    return entering


def power(rate_ref, part, slices):
    rate = rate_ref[:, row_part(part), :].reshape(FACE, rate_ref.shape[2])
    factor = rate
    for _ in range(slices - 1):
        factor = factor * rate
    return factor


def ordered(own, other):
    first = (lax.axis_index("tm") & 1) == 0
    return jnp.where(first, own, other), jnp.where(first, other, own)


def pair_kernel(slices, part, own_ref, other_ref, rate_ref, out_ref):
    factor = power(rate_ref, part, slices)
    early, late = ordered(own_ref[...], other_ref[...])
    out_ref[...] = late + factor * early


def enter_kernel(
    slices, part, own_ref, other_ref, here_ref, there_ref, rate_ref, keep_ref, send_ref
):
    factor = power(rate_ref, part, slices)
    square = factor * factor
    early, _ = ordered(own_ref[...], other_ref[...])
    enter = (there_ref[...] + square * here_ref[...]) / (1.0 - square * square)
    later = early + factor * enter
    own, other = ordered(enter, later)
    keep_ref[...] = own
    send_ref[...] = other


def solve_kernel(pieces, *refs):
    piece_refs = refs[:pieces]
    right_ref, rate_ref, state_ref, before_ref, near_ref, *far_refs = refs[pieces:]
    slices, rows, columns = right_ref.shape
    if pieces == 1:
        before_ref[...] = piece_refs[0][...].reshape(before_ref.shape)
    else:
        for part in range(pieces):
            before_ref[:, row_part(part), :] = piece_refs[part][...].reshape(NF, 16, columns)
    rate = rate_ref[...]
    value = before_ref[...].reshape(rows, columns)
    low = []
    high = []
    for item in range(slices):
        value = rate * (value + right_ref[item])
        state_ref[item] = value
        cube = value.reshape(NF, NP**3, columns)
        low.append(cube[:, 0:16, 0:LANES].reshape(FACE, LANES))
        high.append(cube[:, 48:64, columns - LANES :].reshape(FACE, LANES))
    send(low, high, near_ref, *far_refs)


def second_kernel(
    state_ref, before_ref, forcing_ref, weights_ref, neighbor_ref, tags_ref, codes_ref, out_ref,
    result_ref, blocks, stack, semaphore,
):
    slices, _, columns = state_ref.shape
    copy = pltpu.make_async_copy(state_ref, result_ref, semaphore)
    copy.start()
    image = operator(
        state_ref, blocks, stack, weights_ref, neighbor_ref, tags_ref, codes_ref
    )
    for item in range(slices):
        previous = before_ref[...].reshape(state_ref.shape[1:]) if item == 0 else state_ref[item - 1]
        out_ref[item] = (
            image[:, item * columns : (item + 1) * columns]
            + forcing_ref[item]
            + (previous - state_ref[item])
        )
    copy.wait()


def finish_kernel(
    part_ref, far_pass_ref, far_ref, near_ref, rim_weights_ref, neighbor_ref, tags_ref, codes_ref, out_ref,
    held, semaphores,
):
    slices, _, columns = part_ref.shape
    count = columns // LANES
    first = (lax.axis_index("tm") & 1) == 0
    far = jnp.where(first, far_ref[...], far_pass_ref[...])
    low, high = rim(
        far, near_ref, slices, rim_weights_ref, neighbor_ref, tags_ref, codes_ref, count
    )
    copies = []
    for block in range(count):
        span = pl.ds(block * LANES, LANES)
        for item in range(slices):
            value = part_ref[item, :, span]
            piece = slice(item * LANES, (item + 1) * LANES)
            if block == 0:
                value = value + low[:, piece]
            if block == count - 1:
                value = value + high[:, piece]
            held[item, :, span] = value.astype(held.dtype)
        copy = pltpu.make_async_copy(
            held.at[:, :, span], out_ref.at[:, :, span], semaphores.at[block]
        )
        copy.start()
        copies.append(copy)
    for copy in copies:
        copy.wait()


VMEM = pl.BlockSpec(memory_space=pltpu.VMEM)
HBM = pl.BlockSpec(memory_space=pltpu.HBM)


def call(kernel, name, outs, args, scratch=(), flops=0, in_specs=None, out_specs=None):
    size = sum(math.prod(a.shape) * a.dtype.itemsize for a in list(args) + list(outs))
    return pl.pallas_call(
        kernel,
        name=name,
        out_shape=outs,
        in_specs=in_specs or [VMEM] * len(args),
        out_specs=out_specs or [VMEM] * len(outs),
        scratch_shapes=list(scratch),
        compiler_params=pltpu.CompilerParams(vmem_limit_bytes=40 * 2**20),
        cost_estimate=pl.CostEstimate(flops=flops, bytes_accessed=size, transcendentals=0),
    )(*args)


def near_exchange(near):
    pairs = [(i, i + 1) for i in range(0, lax.axis_size("space") - 1, 2)]
    return lax.ppermute(near, "space", pairs + [(j, i) for i, j in pairs])


def far_exchange(far, across=False):
    count = lax.axis_size("space")
    pairs = [(i, (i + 1) % count) for i in range(1, count, 2)]
    pairs += [(j, i) for i, j in pairs]
    if not across:
        return lax.ppermute(far, "space", pairs)
    places = range(lax.axis_size("tm"))
    return lax.ppermute(
        far, ("tm", "space"),
        [(k * count + i, (k ^ 1) * count + j) for k in places for i, j in pairs],
    )


def swapped(value, step):
    count = lax.axis_size("tm")
    return lax.ppermute(value, "tm", [(i, i ^ step) for i in range(count)])


def in_hbm(value):
    return pltpu.with_memory_space_constraint(value, pltpu.HBM)


def local(guess, source_cos, source_sin, damping, volume, lifts, neighbor, tags, codes):
    slices, rows, columns = guess.shape
    devices = lax.axis_size("tm")
    f32, bf16 = jnp.float32, jnp.bfloat16
    shape = jax.ShapeDtypeStruct
    whole = shape((slices, rows, columns), f32)
    plane = shape((rows, columns), f32)
    halo = shape(((slices + 1) // 2, FACE, LANES), f32)
    edge = shape((2, FACE, LANES), f32)
    split_rows = shape((NF, NP**3, columns), f32)
    depth = rows + 6 * FACE
    scratch = [
        pltpu.VMEM((slices * columns // LANES, rows, LANES), f32),
        pltpu.VMEM((depth, 2 * slices * columns), bf16),
    ]
    work = 4 * rows * depth * slices * columns
    end = pltpu.VMEM((slices, NF, NP * NP, LANES), f32)
    share = rows // devices
    pairs = devices == 4 and slices == 2
    pieces = devices if pairs else 1
    piece = shape((rows // pieces, columns), f32)

    cube = guess.reshape(slices, NF, NP**3, columns)
    far, near, held = call(
        ends_kernel, "ends", [halo, halo, shape(cube.shape, f32)], [in_hbm(cube)],
        [end, end, pltpu.SemaphoreType.DMA((3,))], in_specs=[HBM],
    )
    far, near = far_exchange(far), near_exchange(near)
    operands = (
        neighbor, tags, codes, jnp.swapaxes(lifts, 1, 2), volume, damping, source_cos,
        source_sin,
    )
    part, weights, rim_weights, rate, forcing, *tables = call(
        functools.partial(first_kernel, slices * devices), "first",
        [whole, shape((rows, depth), bf16), shape((2, rows, FACE), bf16), plane, whole]
        + [shape(neighbor.shape, jnp.int32)] * 3,
        [held.reshape(guess.shape)] + [in_hbm(operand) for operand in operands],
        [
            pltpu.VMEM(plane.shape, bf16),
            pltpu.VMEM(plane.shape, bf16),
            pltpu.VMEM(plane.shape, f32),
            pltpu.VMEM(volume.shape, bf16),
            pltpu.VMEM((6, FACE, rows), bf16),
            *scratch,
            pltpu.SemaphoreType.DMA((len(operands),)),
        ],
        flops=work, in_specs=[VMEM] + [HBM] * len(operands),
    )
    known, *parts, edges = call(
        functools.partial(carry_kernel, pieces), "carry", [whole] + [piece] * pieces + [edge],
        [part, far, near, rate, rim_weights, *tables], [pltpu.VMEM(split_rows.shape, f32)],
    )
    if pairs:
        around = []
        rates = rate.reshape(split_rows.shape)
        others = [swapped(parts[k + 1], 1) for k in (0, 2)]
        for k in (0, 2):
            (here,) = call(
                functools.partial(pair_kernel, slices, k), "pair", [piece],
                [parts[k], others[k // 2], rates],
            )
            around.append((here, swapped(here, 2)))
        passed = swapped(edges, 1)
        own = parts[::2]
        parts = []
        entering = []
        for k in (0, 2):
            keep, pass_on = call(
                functools.partial(enter_kernel, slices, k), "enter", [piece] * 2,
                [own[k // 2], others[k // 2], *around[k // 2], rates],
            )
            entering += [keep, pass_on]
            parts += [keep, swapped(pass_on, 1)]
        far_pass, far = call(
            spread_kernel, "spread", [halo] * 2, [*entering, edges, passed, rates]
        )
        halos = [far_exchange(far_pass, True), far_exchange(far)]
    else:
        me = lax.axis_index("tm")
        factor = lax.dynamic_slice_in_dim(rate, me * share, share, 0) ** slices
        carries = lax.all_to_all(parts[0], "tm", split_axis=0, concat_axis=0, tiled=True)
        carries = carries.reshape(devices, share, columns)
        back = jnp.concatenate(periodic([carries[k] for k in range(devices)], factor), axis=0)
        parts = [lax.all_to_all(back, "tm", split_axis=0, concat_axis=0, tiled=True)]
    state, before, near, *far = call(
        functools.partial(solve_kernel, pieces), "solve",
        [whole, split_rows, halo] + [halo] * (not pairs), [*parts, known, rate],
    )
    if not pairs:
        halos = [far_exchange(far[0])] * 2
    near = near_exchange(near)
    part, result = call(
        second_kernel, "second", [whole, whole],
        [state, before, forcing, weights, *tables],
        [*scratch, pltpu.SemaphoreType.DMA], flops=work, out_specs=[VMEM, HBM],
    )
    (after,) = call(
        finish_kernel, "finish", [shape(whole.shape, bf16)],
        [part, *halos, near, rim_weights, *tables],
        [pltpu.VMEM(whole.shape, bf16), pltpu.SemaphoreType.DMA((columns // LANES,))],
        out_specs=[HBM],
    )
    return result, after


def solution(mesh):
    column = P(None, ("groups", "space"))
    state = P("tm", None, ("groups", "space"))
    in_specs = (state, column, column, column, P(), P(), column, column, column)
    return jax.shard_map(
        local, mesh=mesh, in_specs=in_specs, out_specs=(state, state), check_vma=False
    )
```

```python
import functools
import math

import jax
import jax.numpy as jnp
from jax import lax
from jax.experimental import pallas as pl
from jax.experimental.pallas import tpu as pltpu
from jax.sharding import PartitionSpec as P

NF = 5
NP = 4
FACE = NF * NP * NP
LANES = 128
HALF = 64


def split(value):
    high = value.astype(jnp.bfloat16)
    low = (value - high.astype(jnp.float32)).astype(jnp.bfloat16)
    return high, low


def end_trace(cube, face):
    rows = cube[:, 0:16] if face == 0 else cube[:, 48:64]
    return rows.reshape(FACE, LANES)


def side_trace(cube, face):
    tiles = cube.reshape(NF, 2, 2, 16, LANES)
    part = tiles[:, :, :, 0:8] if face == 2 else tiles[:, :, :, 8:16]
    even = part[:, :, 0].reshape(FACE // 8, 8, LANES)
    odd = part[:, :, 1].reshape(FACE // 8, 8, LANES)
    lower = lax.broadcasted_iota(jnp.int32, (FACE // 8, 8, LANES), 1) < 4
    if face == 2:
        odd = pltpu.roll(odd, 4, axis=1)
    else:
        even = pltpu.roll(even, 4, axis=1)
    return jnp.where(lower, even, odd).reshape(FACE, LANES)


def lane_index(row):
    return jnp.broadcast_to(row, (FACE, LANES))


def orientation(code):
    swap = (code & 1) == 1
    turn_i = (code & 2) == 2
    turn_j = (code & 4) == 4
    result = []
    for tile in range(2):
        row = lax.broadcasted_iota(jnp.int32, (8, LANES), 0) + 8 * tile
        i, j = row >> 2, row & 3
        i = jnp.where(turn_i, 3 - i, i)
        j = jnp.where(turn_j, 3 - j, j)
        source = jnp.where(swap, j * 4 + i, i * 4 + j)
        result.append((source >= 8, source & 7))
    return result


def oriented(value, plan):
    pieces = []
    for field in range(NF):
        first = value[field * 16 : field * 16 + 8]
        second = value[field * 16 + 8 : field * 16 + 16]
        for upper, sub in plan:
            pick = functools.partial(jnp.take_along_axis, axis=0, mode="promise_in_bounds")
            pieces.append(jnp.where(upper, pick(second, sub), pick(first, sub)))
    return jnp.concatenate(pieces, axis=0)


def gather_lanes(value, row):
    return jnp.take_along_axis(value, lane_index(row), axis=1, mode="promise_in_bounds")


def operator(
    state, blocks, stack, weights_ref, neighbor_ref, tags_ref, codes_ref,
    ready=lambda: None, ahead=lambda: None,
):
    slices, rows, columns = state.shape
    count = columns // LANES
    wide = slices * columns
    base = 6 * FACE
    lane = lax.broadcasted_iota(jnp.int32, (FACE, LANES), 1)
    for item in range(slices):
        for block in range(count):
            n = item * count + block
            value = state[item, :, block * LANES : (block + 1) * LANES]
            blocks[n] = value
            high, low = split(value)
            stack[base:, n * LANES : (n + 1) * LANES] = high
            stack[base:, wide + n * LANES : wide + (n + 1) * LANES] = low
    ready()
    for item in range(slices):
        cubes = []
        turned = []
        for block in range(count):
            cube = blocks[item * count + block].reshape(NF, NP**3, LANES)
            cubes.append(cube)
            turned.append(
                [pltpu.roll(end_trace(cube, face), HALF, axis=1) for face in range(2)]
            )
        zero = jnp.zeros((FACE, LANES), jnp.float32)
        for block in range(count):
            n = item * count + block
            cube = cubes[block]
            before = turned[block - 1][1] if block > 0 else zero
            after = turned[block + 1][0] if block + 1 < count else zero
            ends = [end_trace(cube, 0), end_trace(cube, 1)]
            sides = [side_trace(cube, 2), side_trace(cube, 3)]
            tops = [
                blocks[n, pl.ds(0, FACE, stride=4), :],
                blocks[n, pl.ds(3, FACE, stride=4), :],
            ]
            mine = ends + sides + tops
            across = [
                jnp.where(lane < HALF, before, turned[block][1]),
                jnp.where(lane < HALF, turned[block][0], after),
                sides[1],
                sides[0],
                tops[1],
                tops[0],
            ]
            for face in range(6):
                span = slice(block * LANES, (block + 1) * LANES)
                target = neighbor_ref[face : face + 1, span]
                kind = tags_ref[face : face + 1, span]
                code = codes_ref[face : face + 1, span]
                if face < 2:
                    target = target + HALF
                plan = orientation(code)
                taken = oriented(gather_lanes(across[face], target & (LANES - 1)), plan)
                keep = jnp.where((kind == 1) | (kind == 3), 1.0, 0.0)
                flip = jnp.where(kind == 1, -1.0, keep)
                axis = 1 + face // 2
                inner = []
                for field in range(NF):
                    own = mine[face][field * 16 : (field + 1) * 16]
                    inner.append(own * (flip if field == axis else keep))
                seen = jnp.where(kind == 0, taken, jnp.concatenate(inner, axis=0))
                high, low = split(seen)
                place = FACE * face
                stack[place : place + FACE, n * LANES : (n + 1) * LANES] = high
                stack[place : place + FACE, wide + n * LANES : wide + (n + 1) * LANES] = low
    ahead()
    halves = []
    for part in (slice(0, rows // 2), slice(rows // 2, rows)):
        image = jnp.dot(weights_ref[part], stack[:, 0:wide], preferred_element_type=jnp.float32)
        low = jnp.dot(weights_ref[part], stack[:, wide:], preferred_element_type=jnp.float32)
        halves.append(image + low)
    return jnp.concatenate(halves, axis=0)


def even_place():
    return (lax.axis_index("space") & 1) == 0


def rim(far, near, slices, rim_weights_ref, neighbor_ref, tags_ref, codes_ref, count):
    lane = lax.broadcasted_iota(jnp.int32, (1, LANES), 1)
    even = even_place()
    result = []
    for face in range(2):
        block = 0 if face == 0 else count - 1
        span = slice(block * LANES, (block + 1) * LANES)
        target = neighbor_ref[face : face + 1, span] & (HALF - 1)
        inside = lane < HALF if face == 0 else lane >= HALF
        use = (tags_ref[face : face + 1, span] == 0) & inside
        plan = orientation(codes_ref[face : face + 1, span])
        pieces = []
        for item in range(slices):
            a, b = (far, near) if face == 0 else (near, far)
            halo = jnp.where(even, a[item // 2], b[item // 2])
            taken = gather_lanes(halo, target + HALF * (item % 2))
            pieces.append(split(jnp.where(use, oriented(taken, plan), 0.0)))
        both = jnp.concatenate([p[0] for p in pieces] + [p[1] for p in pieces], axis=1)
        middle = rim_weights_ref.shape[1] // 2
        product = jnp.concatenate(
            [
                jnp.dot(rim_weights_ref[face, part], both, preferred_element_type=jnp.float32)
                for part in (slice(0, middle), slice(middle, 2 * middle))
            ],
            axis=0,
        )
        wide = slices * LANES
        result.append(product[:, :wide] + product[:, wide:])
    return result


def packed(low, high):
    lane = lax.broadcasted_iota(jnp.int32, (FACE, LANES), 1)
    first = jnp.where(lane < HALF, low[0], pltpu.roll(low[1], HALF, axis=1))
    last = jnp.where(lane < HALF, pltpu.roll(high[0], HALF, axis=1), high[1])
    return first, last


def send(low, high, near_ref, far_ref=None):
    slices = len(low)
    even = even_place()
    for item in range(0, slices, 2):
        other = min(item + 1, slices - 1)
        first, last = packed([low[item], low[other]], [high[item], high[other]])
        near_ref[item // 2] = jnp.where(even, last, first)
        if far_ref is not None:
            far_ref[item // 2] = jnp.where(even, first, last)


def spread_kernel(
    keep0_ref, pass0_ref, keep3_ref, pass3_ref, edges_ref, others_ref, rate_ref, far_pass_ref,
    far_ref,
):
    columns = keep0_ref.shape[1]
    even = even_place()
    rate = jnp.where(
        even,
        rate_ref[:, 0:16, 0:LANES].reshape(FACE, LANES),
        rate_ref[:, 48:64, columns - LANES :].reshape(FACE, LANES),
    )
    lane = lax.broadcasted_iota(jnp.int32, (FACE, LANES), 1)
    for low_ref, high_ref, ends_ref, to_ref in (
        (keep0_ref, keep3_ref, edges_ref, far_ref),
        (pass0_ref, pass3_ref, others_ref, far_pass_ref),
    ):
        ends = jnp.where(even, ends_ref[0], ends_ref[1])
        turned = pltpu.roll(ends, HALF, axis=1)
        enter = jnp.where(even, low_ref[:, 0:LANES], high_ref[:, columns - LANES :])
        early = rate * (enter + jnp.where(even, ends, turned))
        late = rate * (early + jnp.where(even, turned, ends))
        turned = pltpu.roll(jnp.where(even, late, early), HALF, axis=1)
        to_ref[0] = jnp.where(
            lane < HALF, jnp.where(even, early, turned), jnp.where(even, turned, late)
        )


def ends_kernel(state_ref, far_ref, near_ref, held_ref, low, high, semaphore):
    slices, _, _, columns = state_ref.shape
    copies = [
        pltpu.make_async_copy(
            state_ref.at[:, :, pl.ds(0, 16), pl.ds(0, LANES)], low, semaphore.at[0]
        ),
        pltpu.make_async_copy(
            state_ref.at[:, :, pl.ds(48, 16), pl.ds(columns - LANES, LANES)], high, semaphore.at[1]
        ),
        pltpu.make_async_copy(state_ref, held_ref, semaphore.at[2]),
    ]
    for copy in copies:
        copy.start()
    for copy in copies[:2]:
        copy.wait()
    send(
        [low[item].reshape(FACE, LANES) for item in range(slices)],
        [high[item].reshape(FACE, LANES) for item in range(slices)],
        near_ref,
        far_ref,
    )
    copies[2].wait()


def wave(at, values):
    result = jnp.float32(values[0])
    for k in range(1, len(values)):
        result = jnp.where(at == k, jnp.float32(values[k]), result)
    return result


def first_kernel(total, state_ref, *refs):
    sources = refs[:8]
    out_ref, weights_ref, rim_weights_ref, rate_ref, forcing_ref = refs[8:13]
    neighbor_ref, tags_ref, codes_ref = refs[13:16]
    cos_ref, sin_ref, damping_ref, volume_ref, lifts_ref = refs[16:21]
    blocks, stack, semaphores = refs[21:]
    targets = (
        neighbor_ref, tags_ref, codes_ref, lifts_ref, volume_ref, damping_ref, cos_ref, sin_ref,
    )
    copies = [
        pltpu.make_async_copy(source, target, semaphores.at[k])
        for k, (source, target) in enumerate(zip(sources, targets))
    ]
    for copy in copies:
        copy.start()
    slices, _, columns = state_ref.shape

    def ready():
        for copy in copies[:3]:
            copy.wait()

    def ahead():
        for copy in copies[3:]:
            copy.wait()
        for face in range(6):
            lift = lifts_ref[face].T
            weights_ref[:, FACE * face : FACE * (face + 1)] = lift
            if face < 2:
                rim_weights_ref[face] = lift
        weights_ref[:, 6 * FACE :] = volume_ref[...]

    image = operator(
        state_ref, blocks, stack, weights_ref, neighbor_ref, tags_ref, codes_ref, ready, ahead
    )
    rate_ref[...] = 1.0 / (1.0 + damping_ref[...])
    angles = [2.0 * math.pi * k / total for k in range(total)]
    for item in range(slices):
        at = lax.axis_index("tm") * slices + item
        forcing = wave(at, [math.cos(x) for x in angles]) * cos_ref[...].astype(jnp.float32)
        forcing += wave(at, [math.sin(x) for x in angles]) * sin_ref[...].astype(jnp.float32)
        forcing_ref[item] = forcing
        out_ref[item] = (
            image[:, item * columns : (item + 1) * columns]
            + forcing
            + damping_ref[...] * state_ref[item]
        )


def carry_kernel(
    pieces, part_ref, far_ref, near_ref, rate_ref, rim_weights_ref, neighbor_ref, tags_ref,
    codes_ref, out_ref, *refs
):
    *piece_refs, edges_ref, carry_ref = refs
    slices, rows, columns = part_ref.shape
    count = columns // LANES
    low, high = rim(
        far_ref, near_ref, slices, rim_weights_ref, neighbor_ref, tags_ref, codes_ref, count
    )
    for block in range(count):
        span = slice(block * LANES, (block + 1) * LANES)
        rate = rate_ref[:, span]
        carry = None
        for item in range(slices):
            value = part_ref[item, :, span]
            piece = slice(item * LANES, (item + 1) * LANES)
            if block == 0:
                value = value + low[:, piece]
            if block == count - 1:
                value = value + high[:, piece]
            out_ref[item, :, span] = value
            carry = rate * value if carry is None else rate * (carry + value)
        carry_ref[:, :, span] = carry.reshape(NF, NP**3, LANES)
    if pieces == 1:
        piece_refs[0][...] = carry_ref[...].reshape(rows, columns)
        edges_ref[...] = jnp.zeros_like(edges_ref)
        return
    for part in range(pieces):
        piece_refs[part][...] = carry_ref[:, row_part(part), :].reshape(FACE, columns)
    edges = []
    for item in range(slices):
        first = end_trace(out_ref[item, :, 0:LANES].reshape(NF, NP**3, LANES), 0)
        last = end_trace(out_ref[item, :, columns - LANES :].reshape(NF, NP**3, LANES), 1)
        edges.append((first, last))
    edges_ref[0], edges_ref[1] = packed(*zip(*edges))


def row_part(part):
    half = (lax.axis_index("tm") & 1) ^ (part & 1)
    return pl.ds(pl.multiple_of((half if part < 2 else 3 - half) * 16, 16), 16)


def periodic(carries, factor):
    count = len(carries)
    total = carries[0]
    for k in range(1, count):
        total = carries[k] + factor * total
    power = factor
    for _ in range(count - 1):
        power = power * factor
    entering = [total / (1.0 - power)]
    for k in range(count - 1):
        entering.append(carries[k] + factor * entering[-1])
    return entering


def power(rate_ref, part, slices):
    rate = rate_ref[:, row_part(part), :].reshape(FACE, rate_ref.shape[2])
    factor = rate
    for _ in range(slices - 1):
        factor = factor * rate
    return factor


def ordered(own, other):
    first = (lax.axis_index("tm") & 1) == 0
    return jnp.where(first, own, other), jnp.where(first, other, own)


def pair_kernel(slices, part, own_ref, other_ref, rate_ref, out_ref):
    factor = power(rate_ref, part, slices)
    early, late = ordered(own_ref[...], other_ref[...])
    out_ref[...] = late + factor * early


def enter_kernel(
    slices, part, own_ref, other_ref, here_ref, there_ref, rate_ref, keep_ref, send_ref
):
    factor = power(rate_ref, part, slices)
    square = factor * factor
    early, _ = ordered(own_ref[...], other_ref[...])
    enter = (there_ref[...] + square * here_ref[...]) / (1.0 - square * square)
    later = early + factor * enter
    own, other = ordered(enter, later)
    keep_ref[...] = own
    send_ref[...] = other


def solve_kernel(pieces, *refs):
    piece_refs = refs[:pieces]
    right_ref, rate_ref, state_ref, before_ref, near_ref, *far_refs = refs[pieces:]
    slices, rows, columns = right_ref.shape
    if pieces == 1:
        before_ref[...] = piece_refs[0][...].reshape(before_ref.shape)
    else:
        for part in range(pieces):
            before_ref[:, row_part(part), :] = piece_refs[part][...].reshape(NF, 16, columns)
    rate = rate_ref[...]
    value = before_ref[...].reshape(rows, columns)
    low = []
    high = []
    for item in range(slices):
        value = rate * (value + right_ref[item])
        state_ref[item] = value
        cube = value.reshape(NF, NP**3, columns)
        low.append(cube[:, 0:16, 0:LANES].reshape(FACE, LANES))
        high.append(cube[:, 48:64, columns - LANES :].reshape(FACE, LANES))
    send(low, high, near_ref, *far_refs)


def second_kernel(
    state_ref, before_ref, forcing_ref, weights_ref, neighbor_ref, tags_ref, codes_ref, out_ref,
    result_ref, blocks, stack, semaphore,
):
    slices, _, columns = state_ref.shape
    copy = pltpu.make_async_copy(state_ref, result_ref, semaphore)
    copy.start()
    image = operator(
        state_ref, blocks, stack, weights_ref, neighbor_ref, tags_ref, codes_ref
    )
    for item in range(slices):
        previous = before_ref[...].reshape(state_ref.shape[1:]) if item == 0 else state_ref[item - 1]
        out_ref[item] = (
            image[:, item * columns : (item + 1) * columns]
            + forcing_ref[item]
            + (previous - state_ref[item])
        )
    copy.wait()


def finish_kernel(
    part_ref, far_pass_ref, far_ref, near_ref, rim_weights_ref, neighbor_ref, tags_ref, codes_ref, out_ref,
    held, semaphores,
):
    slices, _, columns = part_ref.shape
    count = columns // LANES
    first = (lax.axis_index("tm") & 1) == 0
    far = jnp.where(first, far_ref[...], far_pass_ref[...])
    low, high = rim(
        far, near_ref, slices, rim_weights_ref, neighbor_ref, tags_ref, codes_ref, count
    )
    copies = []
    for block in range(count):
        span = pl.ds(block * LANES, LANES)
        for item in range(slices):
            value = part_ref[item, :, span]
            piece = slice(item * LANES, (item + 1) * LANES)
            if block == 0:
                value = value + low[:, piece]
            if block == count - 1:
                value = value + high[:, piece]
            held[item, :, span] = value.astype(held.dtype)
        copy = pltpu.make_async_copy(
            held.at[:, :, span], out_ref.at[:, :, span], semaphores.at[block]
        )
        copy.start()
        copies.append(copy)
    for copy in copies:
        copy.wait()


VMEM = pl.BlockSpec(memory_space=pltpu.VMEM)
HBM = pl.BlockSpec(memory_space=pltpu.HBM)


def call(kernel, name, outs, args, scratch=(), flops=0, in_specs=None, out_specs=None):
    size = sum(math.prod(a.shape) * a.dtype.itemsize for a in list(args) + list(outs))
    return pl.pallas_call(
        kernel,
        name=name,
        out_shape=outs,
        in_specs=in_specs or [VMEM] * len(args),
        out_specs=out_specs or [VMEM] * len(outs),
        scratch_shapes=list(scratch),
        compiler_params=pltpu.CompilerParams(vmem_limit_bytes=40 * 2**20),
        cost_estimate=pl.CostEstimate(flops=flops, bytes_accessed=size, transcendentals=0),
    )(*args)


def near_exchange(near):
    pairs = [(i, i + 1) for i in range(0, lax.axis_size("space") - 1, 2)]
    return lax.ppermute(near, "space", pairs + [(j, i) for i, j in pairs])


def far_exchange(far, across=False):
    count = lax.axis_size("space")
    pairs = [(i, (i + 1) % count) for i in range(1, count, 2)]
    pairs += [(j, i) for i, j in pairs]
    if not across:
        return lax.ppermute(far, "space", pairs)
    places = range(lax.axis_size("tm"))
    return lax.ppermute(
        far, ("tm", "space"),
        [(k * count + i, (k ^ 1) * count + j) for k in places for i, j in pairs],
    )


def swapped(value, step):
    count = lax.axis_size("tm")
    return lax.ppermute(value, "tm", [(i, i ^ step) for i in range(count)])


def in_hbm(value):
    return pltpu.with_memory_space_constraint(value, pltpu.HBM)


def local(guess, source_cos, source_sin, damping, volume, lifts, neighbor, tags, codes):
    slices, rows, columns = guess.shape
    devices = lax.axis_size("tm")
    f32, bf16 = jnp.float32, jnp.bfloat16
    shape = jax.ShapeDtypeStruct
    whole = shape((slices, rows, columns), f32)
    plane = shape((rows, columns), f32)
    halo = shape(((slices + 1) // 2, FACE, LANES), f32)
    edge = shape((2, FACE, LANES), f32)
    split_rows = shape((NF, NP**3, columns), f32)
    depth = rows + 6 * FACE
    scratch = [
        pltpu.VMEM((slices * columns // LANES, rows, LANES), f32),
        pltpu.VMEM((depth, 2 * slices * columns), bf16),
    ]
    work = 4 * rows * depth * slices * columns
    end = pltpu.VMEM((slices, NF, NP * NP, LANES), f32)
    share = rows // devices
    pairs = devices == 4 and slices == 2
    pieces = devices if pairs else 1
    piece = shape((rows // pieces, columns), f32)

    cube = guess.reshape(slices, NF, NP**3, columns)
    far, near, held = call(
        ends_kernel, "ends", [halo, halo, shape(cube.shape, f32)], [in_hbm(cube)],
        [end, end, pltpu.SemaphoreType.DMA((3,))], in_specs=[HBM],
    )
    far, near = far_exchange(far), near_exchange(near)
    operands = (
        neighbor, tags, codes, jnp.swapaxes(lifts, 1, 2), volume, damping, source_cos,
        source_sin,
    )
    part, weights, rim_weights, rate, forcing, *tables = call(
        functools.partial(first_kernel, slices * devices), "first",
        [whole, shape((rows, depth), bf16), shape((2, rows, FACE), bf16), plane, whole]
        + [shape(neighbor.shape, jnp.int32)] * 3,
        [held.reshape(guess.shape)] + [in_hbm(operand) for operand in operands],
        [
            pltpu.VMEM(plane.shape, bf16),
            pltpu.VMEM(plane.shape, bf16),
            pltpu.VMEM(plane.shape, f32),
            pltpu.VMEM(volume.shape, bf16),
            pltpu.VMEM((6, FACE, rows), bf16),
            *scratch,
            pltpu.SemaphoreType.DMA((len(operands),)),
        ],
        flops=work, in_specs=[VMEM] + [HBM] * len(operands),
    )
    known, *parts, edges = call(
        functools.partial(carry_kernel, pieces), "carry", [whole] + [piece] * pieces + [edge],
        [part, far, near, rate, rim_weights, *tables], [pltpu.VMEM(split_rows.shape, f32)],
    )
    if pairs:
        around = []
        rates = rate.reshape(split_rows.shape)
        others = [swapped(parts[k + 1], 1) for k in (0, 2)]
        for k in (0, 2):
            (here,) = call(
                functools.partial(pair_kernel, slices, k), "pair", [piece],
                [parts[k], others[k // 2], rates],
            )
            around.append((here, swapped(here, 2)))
        passed = swapped(edges, 1)
        own = parts[::2]
        parts = []
        entering = []
        for k in (0, 2):
            keep, pass_on = call(
                functools.partial(enter_kernel, slices, k), "enter", [piece] * 2,
                [own[k // 2], others[k // 2], *around[k // 2], rates],
            )
            entering += [keep, pass_on]
            parts += [keep, swapped(pass_on, 1)]
        far_pass, far = call(
            spread_kernel, "spread", [halo] * 2, [*entering, edges, passed, rates]
        )
        halos = [far_exchange(far_pass, True), far_exchange(far)]
    else:
        me = lax.axis_index("tm")
        factor = lax.dynamic_slice_in_dim(rate, me * share, share, 0) ** slices
        carries = lax.all_to_all(parts[0], "tm", split_axis=0, concat_axis=0, tiled=True)
        carries = carries.reshape(devices, share, columns)
        back = jnp.concatenate(periodic([carries[k] for k in range(devices)], factor), axis=0)
        parts = [lax.all_to_all(back, "tm", split_axis=0, concat_axis=0, tiled=True)]
    state, before, near, *far = call(
        functools.partial(solve_kernel, pieces), "solve",
        [whole, split_rows, halo] + [halo] * (not pairs), [*parts, known, rate],
    )
    if not pairs:
        halos = [far_exchange(far[0])] * 2
    near = near_exchange(near)
    part, result = call(
        second_kernel, "second", [whole, whole],
        [state, before, forcing, weights, *tables],
        [*scratch, pltpu.SemaphoreType.DMA], flops=work, out_specs=[VMEM, HBM],
    )
    (after,) = call(
        finish_kernel, "finish", [shape(whole.shape, bf16)],
        [part, *halos, near, rim_weights, *tables],
        [pltpu.VMEM(whole.shape, bf16), pltpu.SemaphoreType.DMA((columns // LANES,))],
        out_specs=[HBM],
    )
    return result, after


def solution(mesh):
    column = P(None, ("groups", "space"))
    state = P("tm", None, ("groups", "space"))
    in_specs = (state, column, column, column, P(), P(), column, column, column)
    return jax.shard_map(
        local, mesh=mesh, in_specs=in_specs, out_specs=(state, state), check_vma=False
    )
```
